32 devices in a mesh: wide: 8 (over z, x), narrow: 4 (over y, core).
Axes of the slice: x: 2, y: 2, z: 4, core: 2. Of those that a mesh axis runs over, the one named last changes fastest.
Arguments:
- recording: bfloat16 [32768, 512], P(('wide', 'narrow')), may hold values from -6 to 6
- conv_weight: bfloat16 [3, 3, 512, 512], replicated, may hold values from -0.15625 to 0.15625
- conv_bias: float32 [3, 512], replicated, may hold values from -3 to 3
- projection: bfloat16 [512, 64], replicated, may hold values from -0.25 to 0.25
Outputs:
- path_points: bfloat16 [32768, 64], P(('wide', 'narrow'))
- level_one: float32 [8, 64], P('wide')
- level_two: float32 [8, 4096], P('wide')
- level_three: float32 [8, 64, 4096], P('wide', 'narrow')
The draws below stay inside these ranges and needn't reach their ends.
All inputs are finite; a program needn't handle non-finite values.
Results may differ from the reference program's by a relative error of at most 0.0075.
Values may be sent and summed in bfloat16 or wider, within the bound.
No kernel may reach another device: no remote copies, remote signals or barrier semaphores. Data moves between devices by JAX's collectives and lax.ppermute only.
A program may use at most 64 MiB of HBM per device.

```python
import jax
import jax.numpy as jnp
from jax import lax

C = 512
PATH = 64
LAYERS = 3
TAPS = 3
TD = 1024
TOTAL = 32768
N_WIDE = 8
N_NARROW = 4


def levels(own_key, shape, shards, smallest, largest):
    level = 1.0
    for position, shards_of in shards:
        heights = jax.random.uniform(jax.random.fold_in(jax.random.fold_in(own_key, 6), position), (shards_of,), jnp.float32, smallest / len(shards), largest / len(shards))
        level = level * jnp.repeat(jnp.exp(heights), shape[position] // shards_of).reshape((-1,) + (1,) * (len(shape) - 1 - position))
    return level


def noise(stream_key, shape, scale, most, cuts=(), held_as=jnp.bfloat16):
    entries = scale * jax.random.normal(stream_key, shape, jnp.float32)
    if cuts:
        entries = entries * levels(stream_key, shape, cuts, -0.22, 0.18)
    return jnp.clip(entries, -most, most).astype(held_as)


def setup_inputs(seed: int = 0) -> dict:
    key_of = jax.random.split(jax.random.key(seed), 5)
    return {
        "recording": noise(key_of[0], (TOTAL, C), 1.0, 6.0, ((0, 32),)),
        "conv_weight": noise(key_of[1], (LAYERS, TAPS, C, C), (TAPS * C) ** -0.5, 0.15625),
        "conv_bias": noise(key_of[2], (LAYERS, C), 0.5, 3.0, (), jnp.float32),
        "projection": noise(key_of[3], (C, PATH), C ** -0.5, 0.25),
    }


PRECISE = lax.Precision.HIGHEST


def conv_layer(hidden, weights, layer_bias, dilation):
    padded = jnp.pad(hidden, ((dilation, dilation), (0, 0)))
    length = hidden.shape[0]
    totals = layer_bias.astype(jnp.float32)[None, :]
    for tap_idx in range(3):
        window = padded[tap_idx * dilation: tap_idx * dilation + length]
        totals = totals + jnp.dot(window, weights[tap_idx], preferred_element_type=jnp.float32)
    return (hidden.astype(jnp.float32) + jax.nn.silu(totals)).astype(jnp.bfloat16)


def sig_update(signature, increments, row_start, row_count):
    first_level, second_level, third_level = signature
    path_width = increments.shape[1]
    step_count = increments.shape[0]
    running = jnp.cumsum(increments, axis=0)
    totals = running[-1]
    before = first_level[None, :] + running - increments
    remaining = totals[None, :] - running
    before_rows = lax.dynamic_slice_in_dim(before, row_start, row_count, 1)
    step_rows = lax.dynamic_slice_in_dim(increments, row_start, row_count, 1)
    second_terms = ((before_rows + 0.5 * step_rows)[:, :, None] * increments[:, None, :]).reshape(step_count, row_count * path_width)
    third_terms = ((0.5 * before_rows + step_rows / 6.0)[:, :, None] * increments[:, None, :]).reshape(step_count, row_count * path_width)
    gained = jnp.einsum('nm,nk->mk', second_terms, remaining, precision=PRECISE)
    gained = gained + jnp.einsum('nm,nk->mk', third_terms, increments, precision=PRECISE)
    second_rows = lax.dynamic_slice_in_dim(second_level, row_start, row_count, 0)
    carried = (second_rows[:, :, None] * totals[None, None, :]).reshape(row_count, path_width * path_width)
    third_level = third_level + carried + gained.reshape(row_count, path_width * path_width)
    second_level = second_level + jnp.einsum('ni,nj->ij', before, increments, precision=PRECISE)
    second_level = second_level + 0.5 * jnp.einsum('ni,nj->ij', increments, increments, precision=PRECISE)
    first_level = first_level + totals
    return first_level, second_level, third_level


def reference(recording, conv_weight, conv_bias, projection):
    hidden = recording
    for layer_idx in range(LAYERS):
        hidden = conv_layer(hidden, conv_weight[layer_idx], conv_bias[layer_idx], 2 ** layer_idx)
    path_points = jnp.dot(hidden, projection, preferred_element_type=jnp.float32).astype(jnp.bfloat16)
    points = path_points.astype(jnp.float32)
    earlier = jnp.concatenate([jnp.zeros((1, PATH), jnp.float32), points[:-1]], axis=0)
    increments = (points - earlier) * (TOTAL ** -0.2)
    blocks = increments.reshape(N_WIDE, N_NARROW, TD, PATH)
    empty_state = (jnp.zeros((PATH,), jnp.float32), jnp.zeros((PATH, PATH), jnp.float32),
                   jnp.zeros((PATH, PATH * PATH), jnp.float32))

    def inner(signature, piece):
        return sig_update(signature, piece, 0, PATH), None

    def outer(signature, wide_block):
        signature, unused = lax.scan(inner, signature, wide_block)
        return signature, signature

    unused_final, stacked = lax.scan(outer, empty_state, blocks)
    return (path_points, stacked[0], stacked[1].reshape(N_WIDE, PATH * PATH),
            stacked[2].reshape(N_WIDE, PATH, PATH * PATH))
```

```python
import functools

import jax
import jax.numpy as jnp
from jax import lax
from jax.experimental import pallas as pl
from jax.experimental.pallas import tpu as pltpu
from jax.sharding import PartitionSpec as P

HALO = 16
LANES = 128
F32 = jnp.float32
BF16 = jnp.bfloat16
NT = (((1,), (1,)), ((), ()))
WHOLE = ("wide", "narrow")


def shifted(array, axis, by):
    size = lax.axis_size(axis)
    pairs = [(i, i + by) for i in range(size) if 0 <= i + by < size]
    return lax.ppermute(array, axis, pairs)


def exchanged(array, axis, distance):
    size = lax.axis_size(axis)
    return lax.ppermute(array, axis, [(i, i ^ distance) for i in range(size)])


def conv_kernel(chunk, rec, left, right, weights, bias, proj, points, piece, even, odd):
    layers = weights.shape[0]
    length = rec.shape[0]
    rows = length + 2 * HALO
    place = lax.axis_index("wide") * lax.axis_size("narrow") + lax.axis_index("narrow")
    last = lax.axis_size("wide") * lax.axis_size("narrow") - 1
    lower = jnp.where(place == 0, HALO, 0)
    upper = jnp.where(place == last, HALO + length, rows)
    even[8 : 8 + HALO, :] = left[...].astype(F32)
    even[8 + HALO : 8 + HALO + length, :] = rec[...].astype(F32)
    even[8 + HALO + length : 8 + rows, :] = right[...].astype(F32)
    source, target = even, odd
    for layer in range(layers):
        reach = 2**layer
        for start in range(0, rows, chunk):
            windows = [
                source[8 + start + k * reach : 8 + start + k * reach + chunk, :] for k in (-1, 0, 1)
            ]
            stacked = jnp.concatenate([window.astype(BF16) for window in windows], axis=1)
            conv = jnp.dot(stacked, weights[layer], preferred_element_type=F32)
            half = 0.5 * (conv + bias[layer : layer + 1, :])
            hidden = windows[1] + (half + half * jnp.tanh(half))
            hidden = hidden.astype(BF16).astype(F32)
            step = start + lax.broadcasted_iota(jnp.int32, (chunk, 1), 0)
            inside = jnp.logical_and(step >= lower, step < upper)
            target[8 + start : 8 + start + chunk, :] = jnp.where(inside, hidden, 0.0)
        source, target = target, source
    final = source[8 : 8 + rows, :].astype(BF16)
    path = lax.dot_general(proj[...], final, NT, preferred_element_type=F32)
    path = path.astype(BF16).astype(F32)
    width = piece.shape[1]
    path = jnp.concatenate([path, jnp.zeros((path.shape[0], width - rows), F32)], axis=1)
    points[...] = pltpu.roll(path, width - HALO, 1)[:, :length].astype(BF16)
    piece[...] = pltpu.roll(path, width - HALO + 1, 1).astype(BF16)


def sig_kernel(masks, row_count, *refs):
    pieces, (third, second, sent, ends), (diff, lead, rest, lhs) = (
        refs[: len(masks)],
        refs[len(masks) : len(masks) + 4],
        refs[len(masks) + 4 :],
    )
    width, padded = pieces[0].shape
    length = padded - LANES
    me = lax.axis_index("narrow")
    first_row = pl.multiple_of(me * row_count, row_count)
    group = max(1, 16 // row_count)
    half_rows = width // 2 * row_count
    sums = [jnp.zeros((half_rows, width), F32) for _ in range(2)]
    crossed = jnp.zeros((width, width), F32)
    lane = lax.broadcasted_iota(jnp.int32, (width, LANES), 1)
    end_points = jnp.zeros((width, LANES), F32)
    for mask, piece in zip(masks, pieces):
        wide_x = piece[...].astype(F32)
        after = pltpu.roll(wide_x, padded - 1, 1)[:, :length]
        before = pltpu.roll(wide_x, 1, 1)[:, :length]
        here = wide_x[:, :length]
        middle = 0.5 * (after + before)
        diff[...] = after - before
        lead[...] = 2.0 * here + middle
        rest[...] = middle - here
        here = piece[:, :length]
        crossed += lax.dot_general(after.astype(BF16), here, NT, preferred_element_type=F32)
        own_lead = lead[pl.ds(first_row, row_count), :]
        own_diff = diff[pl.ds(first_row, row_count), :]
        for h in range(2):
            for at in range(0, width // 2, group):
                terms = []
                for g in range(group):
                    j = 2 * (at + g) + h
                    terms.append(diff[j : j + 1, :] * own_lead + rest[j : j + 1, :] * own_diff)
                term = terms[0] if group == 1 else jnp.concatenate(terms, axis=0)
                lhs[h, at * row_count : (at + group) * row_count, :] = term.astype(BF16)
            sums[h] += lax.dot_general(lhs[h], here, NT, preferred_element_type=F32)
        is_last = jnp.bitwise_xor(me, mask) == lax.axis_size("narrow") - 1
        final = jnp.broadcast_to(wide_x[:, length : length + 1], (width, LANES))
        previous = jnp.broadcast_to(wide_x[:, length - 1 : length], (width, LANES))
        end_points = jnp.where(is_last, jnp.where(lane == 0, final, previous), end_points)
    total = jnp.concatenate(sums, axis=1)
    doubled = jnp.concatenate([crossed, crossed], axis=1)
    third[...] = total
    second[...] = doubled
    ends[...] = end_points
    pack(sent, total, doubled)


def pack(sent, total, doubled):
    count = total.shape[0]
    high = doubled.astype(BF16).astype(F32)
    lane = lax.broadcasted_iota(jnp.int32, doubled.shape, 1)
    sent[:count, :] = total.astype(BF16)
    sent[count:, :] = jnp.where(lane < LANES // 2, high, doubled - high).astype(BF16)


def unpack(received, count):
    coded = received[count:, :].astype(F32)
    return received[:count, :].astype(F32), coded + pltpu.roll(coded, LANES // 2, 1)


def add_kernel(third, second, received, new_third, new_second, sent):
    more_third, more_second = unpack(received, third.shape[0])
    total = third[...] + more_third
    doubled = second[...] + more_second
    new_third[...] = total
    new_second[...] = doubled
    pack(sent, total, doubled)


def final_kernel(scale, row_count, third, second, received, ends, level_one, level_two, level_three, held):
    width = second.shape[0]
    more_third, more_second = unpack(received, third.shape[0])
    crossed = (second[...] + more_second)[:, :width]
    end_cols = ends[...]
    end_rows = end_cols.T
    x_col, a_col = end_cols[:, 0:1], end_cols[:, 1:2]
    x_row, a_row = end_rows[0:1, :], end_rows[1:2, :]
    xx = x_col * x_row
    pairs = 0.5 * xx + 0.5 * (crossed.T - crossed)
    edge = a_col * x_row - a_col * a_row - 2.0 * x_col * a_row
    factor = pairs - edge / 6.0 - xx / 3.0
    level_one[...] = scale * x_row
    held[:, :width] = scale**2 * pairs
    level_two[:, :width] = held[pl.ds(0, width // 2, stride=2), :width]
    level_two[:, width:] = held[pl.ds(1, width // 2, stride=2), :width]
    held[:, :width] = scale**3 * factor
    first_row = pl.multiple_of(lax.axis_index("narrow") * row_count, row_count)
    own = held[pl.ds(first_row, row_count), :width]
    lane = lax.broadcasted_iota(jnp.int32, (row_count, LANES), 1)
    x_twice = jnp.concatenate([x_row, x_row], axis=1)
    total = (third[...] + more_third) * (scale**3 / 6.0)
    for at in range(width // 2):
        low = jnp.broadcast_to(own[:, 2 * at : 2 * at + 1], (row_count, LANES))
        high = jnp.broadcast_to(own[:, 2 * at + 1 : 2 * at + 2], (row_count, LANES))
        level_three[:, at * LANES : (at + 1) * LANES] = (
            jnp.where(lane < width, low, high) * x_twice
            - total[at * row_count : (at + 1) * row_count, :]
        )


def vmem(count):
    return [pl.BlockSpec(memory_space=pltpu.VMEM)] * count


def params():
    return pltpu.CompilerParams(vmem_limit_bytes=48 * 2**20)


def per_device(recording, conv_weight, conv_bias, projection):
    length, channels = recording.shape
    layers, taps = conv_weight.shape[:2]
    width = projection.shape[1]
    wide_size, narrow_size = lax.axis_size("wide"), lax.axis_size("narrow")
    scale = float(length * wide_size * narrow_size) ** -0.2
    row_count = width // narrow_size
    third_rows = width // 2 * row_count
    shape = jax.ShapeDtypeStruct

    left = shifted(recording[length - HALO :], WHOLE, 1)
    right = shifted(recording[:HALO], WHOLE, -1)
    rows = length + 2 * HALO
    points, piece = pl.pallas_call(
        functools.partial(conv_kernel, rows // 3),
        out_shape=(shape((width, length), BF16), shape((width, length + LANES), BF16)),
        in_specs=vmem(6),
        out_specs=tuple(vmem(2)),
        scratch_shapes=[pltpu.VMEM((rows + 16, channels), F32)] * 2,
        compiler_params=params(),
        name="conv",
    )(
        recording,
        left,
        right,
        conv_weight.reshape(layers, taps * channels, channels),
        conv_bias,
        projection.T,
    )

    masks, pieces = [0], [piece]
    distance = narrow_size // 2
    while distance:
        pieces = pieces + [exchanged(held, "narrow", distance) for held in pieces]
        masks = masks + [mask ^ distance for mask in masks]
        distance //= 2
    sums_shape = (
        shape((third_rows, LANES), F32),
        shape((width, LANES), F32),
        shape((third_rows + width, LANES), BF16),
    )
    third, second, sent, ends = pl.pallas_call(
        functools.partial(sig_kernel, masks, row_count),
        out_shape=sums_shape + (shape((width, LANES), F32),),
        in_specs=vmem(len(pieces)),
        out_specs=tuple(vmem(4)),
        scratch_shapes=[pltpu.VMEM((width, length), F32)] * 3 + [pltpu.VMEM((2, third_rows, length), BF16)],
        compiler_params=params(),
        name="block_sums",
    )(*pieces)

    distance = 1
    received = shifted(sent, "wide", distance)
    while 2 * distance < wide_size:
        distance *= 2
        third, second, sent = pl.pallas_call(
            add_kernel,
            out_shape=sums_shape,
            in_specs=vmem(3),
            out_specs=tuple(vmem(3)),
            compiler_params=params(),
            name="add",
        )(third, second, received)
        received = shifted(sent, "wide", distance)

    level_one, level_two, level_three = pl.pallas_call(
        functools.partial(final_kernel, scale, row_count),
        out_shape=(
            shape((1, width), F32),
            shape((width // 2, LANES), F32),
            shape((row_count, width * width), F32),
        ),
        in_specs=vmem(4),
        out_specs=tuple(vmem(3)),
        scratch_shapes=[pltpu.VMEM((width, LANES), F32)],
        compiler_params=params(),
        name="finish",
    )(third, second, received, ends)
    return points.T, level_one, level_two.reshape(1, width * width), level_three[None]


def solution(mesh):
    return jax.shard_map(
        per_device,
        mesh=mesh,
        in_specs=(P(WHOLE, None), P(), P(), P()),
        out_specs=(P(WHOLE, None), P("wide", None), P("wide", None), P("wide", "narrow", None)),
        check_vma=False,
    )
```

```python
import functools

import jax
import jax.numpy as jnp
from jax import lax
from jax.experimental import pallas as pl
from jax.experimental.pallas import tpu as pltpu
from jax.sharding import PartitionSpec as P

HALO = 16
LANES = 128
F32 = jnp.float32
BF16 = jnp.bfloat16
NT = (((1,), (1,)), ((), ()))
WHOLE = ("wide", "narrow")


def exchanged(array, axis, distance):
    size = lax.axis_size(axis)
    return lax.ppermute(array, axis, [(i, i ^ distance) for i in range(size)])


def edges_exchanged(recording):
    length = recording.shape[0]
    is_odd = lax.axis_index("narrow") % 2
    outer = lax.dynamic_slice_in_dim(recording, is_odd * (length - HALO), HALO, 0)
    inner = lax.dynamic_slice_in_dim(recording, (1 - is_odd) * (length - HALO), HALO, 0)
    size = lax.axis_size("wide") * lax.axis_size("narrow")
    across = [(i, min(max(i - 1 + 2 * (i % 2), 0), size - 1)) for i in range(size)]
    outer = lax.ppermute(outer, WHOLE, across)
    inner = exchanged(inner, "narrow", 1)
    return outer, inner


def conv_kernel(chunk, rec_hbm, outer, inner, weights_hbm, bias, proj, points, piece, even, odd, rec, weights, sems):
    layers = weights.shape[0]
    length = rec.shape[0]
    rows = length + 2 * HALO
    copies = [pltpu.make_async_copy(rec_hbm, rec, sems.at[layers])]
    copies += [pltpu.make_async_copy(weights_hbm.at[i], weights.at[i], sems.at[i]) for i in range(layers)]
    for copy in copies:
        copy.start()
    narrow = lax.axis_index("narrow")
    place = lax.axis_index("wide") * lax.axis_size("narrow") + narrow
    last = lax.axis_size("wide") * lax.axis_size("narrow") - 1
    is_odd = lax.rem(narrow, 2)
    lower = jnp.where(place == 0, HALO, 0)
    upper = jnp.where(place == last, HALO + length, rows)
    far = HALO + length
    at_end = jnp.logical_or(place == 0, place == last)
    even[pl.ds(pl.multiple_of(8 + is_odd * far, 8), HALO), :] = jnp.where(at_end, 0.0, outer[...].astype(F32))
    even[pl.ds(pl.multiple_of(8 + (1 - is_odd) * far, 8), HALO), :] = inner[...].astype(F32)
    copies[0].wait()
    even[8 + HALO : 8 + HALO + length, :] = rec[...].astype(F32)
    source, target = even, odd
    for layer in range(layers):
        copies[1 + layer].wait()
        reach = 2**layer
        for start in range(0, rows, chunk):
            windows = [
                source[8 + start + k * reach : 8 + start + k * reach + chunk, :] for k in (-1, 0, 1)
            ]
            stacked = jnp.concatenate([window.astype(BF16) for window in windows], axis=1)
            conv = jnp.dot(stacked, weights[layer], preferred_element_type=F32)
            half = 0.5 * (conv + bias[layer : layer + 1, :])
            hidden = windows[1] + (half + half * jnp.tanh(half))
            hidden = hidden.astype(BF16).astype(F32)
            step = start + lax.broadcasted_iota(jnp.int32, (chunk, 1), 0)
            inside = jnp.logical_and(step >= lower, step < upper)
            target[8 + start : 8 + start + chunk, :] = jnp.where(inside, hidden, 0.0)
        source, target = target, source
    final = source[8 : 8 + rows, :].astype(BF16)
    path = lax.dot_general(proj[...], final, NT, preferred_element_type=F32)
    path = path.astype(BF16).astype(F32)
    width = piece.shape[1]
    path = jnp.concatenate([path, jnp.zeros((path.shape[0], width - rows), F32)], axis=1)
    points[...] = pltpu.roll(path, width - HALO, 1)[:, :length].astype(BF16)
    piece[...] = pltpu.roll(path, width - HALO + 1, 1).astype(BF16)


def coefficients(piece, diff, lead, rest):
    padded = piece.shape[1]
    length = padded - LANES
    points = piece[...].astype(F32)
    after = pltpu.roll(points, padded - 1, 1)[:, :length]
    before = pltpu.roll(points, 1, 1)[:, :length]
    here = points[:, :length]
    middle = 0.5 * (after + before)
    diff[...] = after - before
    lead[...] = 2.0 * here + middle
    rest[...] = middle - here
    return points, after


def half_sum(half, piece, diff, lead, rest, lhs):
    width, padded = piece.shape
    length = padded - LANES
    row_count = 4 * lhs.shape[1] // width
    first_row = pl.multiple_of(lax.axis_index("narrow") * row_count, row_count)
    group = max(1, 16 // row_count)
    own_lead = lead[pl.ds(first_row, row_count), :]
    own_diff = diff[pl.ds(first_row, row_count), :]
    sums = []
    for h in range(2):
        for at in range(0, width // 4, group):
            terms = []
            for g in range(group):
                row = pl.ds(half * (width // 2) + 2 * (at + g) + h, 1)
                terms.append(diff[row, :] * own_lead + rest[row, :] * own_diff)
            term = terms[0] if group == 1 else jnp.concatenate(terms, axis=0)
            lhs[h, at * row_count : (at + group) * row_count, :] = term.astype(BF16)
        sums.append(lax.dot_general(lhs[h], piece[:, :length], NT, preferred_element_type=F32))
    return jnp.concatenate(sums, axis=1)


def parity():
    return lax.rem(lax.axis_index("wide"), 2)


def sums_kernel(masks, started, *refs):
    before, refs = refs[: 4 * started], refs[4 * started :]
    pieces, (kept, given, second, ends, diff, lead, rest, lhs) = refs[: len(masks)], refs[len(masks) :]
    values = [ref[...] for ref in before]
    for mask, piece in zip(masks, pieces):
        width, padded = piece.shape
        length = padded - LANES
        points, after = coefficients(piece, diff, lead, rest)
        crossed = lax.dot_general(after.astype(BF16), piece[:, :length], NT, preferred_element_type=F32)
        crossed = jnp.concatenate([crossed, crossed], axis=1)
        is_last = jnp.bitwise_xor(lax.axis_index("narrow"), mask) == lax.axis_size("narrow") - 1
        final = jnp.broadcast_to(points[:, length : length + 1], (width, LANES))
        previous = jnp.broadcast_to(points[:, length - 1 : length], (width, LANES))
        lane = lax.broadcasted_iota(jnp.int32, (width, LANES), 1)
        end_points = jnp.where(is_last, jnp.where(lane == 0, final, previous), 0.0)
        given_sum = half_sum(1 - parity(), piece, diff, lead, rest, lhs)
        kept_sum = half_sum(parity(), piece, diff, lead, rest, lhs)
        more = [kept_sum, given_sum, crossed, end_points]
        values = [value + extra for value, extra in zip(values, more)] if values else more
    for target, value in zip((kept, given, second, ends), values):
        target[...] = value


def pack(sent, total, doubled):
    count = total.shape[0]
    high = doubled.astype(BF16).astype(F32)
    lane = lax.broadcasted_iota(jnp.int32, doubled.shape, 1)
    sent[:count, :] = total.astype(BF16)
    sent[count:, :] = jnp.where(lane < LANES // 2, high, doubled - high).astype(BF16)


def unpack(received, count):
    coded = received[count:, :].astype(F32)
    return received[:count, :].astype(F32), coded + pltpu.roll(coded, LANES // 2, 1)


def give_kernel(given, second, sent):
    pack(sent, given[...], second[...])


def pair_kernel(kept, second, received, pair_third, pair_second, sent):
    more_third, more_second = unpack(received, kept.shape[0])
    total = kept[...] + more_third
    doubled = second[...] + more_second
    pair_third[...] = total
    pair_second[...] = doubled
    pack(sent, total, doubled)


def is_later(distance):
    return jnp.bitwise_and(lax.axis_index("wide"), distance) != 0


def scan_kernel(distance, started, *refs):
    before, (group_third, group_second, received, third, second, new_third, new_second, sent) = (
        refs[: 2 * started],
        refs[2 * started :],
    )
    more_third, more_second = unpack(received, group_third.shape[0])
    earlier_third = jnp.where(is_later(distance), more_third, 0.0)
    earlier_second = jnp.where(is_later(distance), more_second, 0.0)
    if started:
        earlier_third, earlier_second = earlier_third + before[0][...], earlier_second + before[1][...]
    third[...] = earlier_third
    second[...] = earlier_second
    total, doubled = group_third[...] + more_third, group_second[...] + more_second
    new_third[...] = total
    new_second[...] = doubled
    pack(sent, total, doubled)


def return_kernel(distance, third, received, kept, earlier, sent):
    count = third.shape[0]
    total = third[...] + jnp.where(is_later(distance), received[:count, :].astype(F32), 0.0)
    earlier[...] = total
    sent[...] = jnp.where(parity() == 0, total + kept[...], total).astype(BF16)


def products(result, half, factor, x_twice, total):
    row_count, width = factor.shape
    lane = lax.broadcasted_iota(jnp.int32, (row_count, LANES), 1)
    factor = jnp.where(half == 0, factor[:, : width // 2], factor[:, width // 2 :])
    for at in range(width // 4):
        low = jnp.broadcast_to(factor[:, 2 * at : 2 * at + 1], (row_count, LANES))
        high = jnp.broadcast_to(factor[:, 2 * at + 1 : 2 * at + 2], (row_count, LANES))
        result[:, at * LANES : (at + 1) * LANES] = (
            jnp.where(lane < width, low, high) * x_twice - total[at * row_count : (at + 1) * row_count, :]
        )


def levels_kernel(
    scale, row_count, distance, second, received, own_second, pair_second, ends, earlier, kept, pair_third,
    level_one, level_two, own_factor, x_twice, own_half, held,
):
    width = second.shape[0]
    count = received.shape[0] - width
    is_first = parity() == 0
    coded = jnp.where(is_later(distance), received[count:, :].astype(F32), 0.0)
    crossed = second[...] + coded + pltpu.roll(coded, LANES // 2, 1)
    crossed = (crossed + jnp.where(is_first, own_second[...], pair_second[...]))[:, :width]
    end_cols = ends[...]
    end_rows = end_cols.T
    x_col, a_col = end_cols[:, 0:1], end_cols[:, 1:2]
    x_row, a_row = end_rows[0:1, :], end_rows[1:2, :]
    xx = x_col * x_row
    pairs = 0.5 * xx + 0.5 * (crossed.T - crossed)
    edge = a_col * x_row - a_col * a_row - 2.0 * x_col * a_row
    factor = pairs - edge / 6.0 - xx / 3.0
    level_one[...] = scale * x_row
    held[:, :width] = scale**2 * pairs
    level_two[:, :width] = held[pl.ds(0, width // 2, stride=2), :width]
    level_two[:, width:] = held[pl.ds(1, width // 2, stride=2), :width]
    held[:, :width] = scale**3 * factor
    first_row = pl.multiple_of(lax.axis_index("narrow") * row_count, row_count)
    own = held[pl.ds(first_row, row_count), :]
    own_factor[...] = own
    twice = jnp.concatenate([x_row, x_row], axis=1)
    x_twice[...] = twice
    total = (earlier[...] + jnp.where(is_first, kept[...], pair_third[...])) * (scale**3 / 6.0)
    products(own_half, parity(), own[:, :width], twice, total)


def finish_kernel(scale, received, given, own_factor, x_twice, own_half, level_three, other_half):
    width = own_factor.shape[1] // 2
    total = (received[...].astype(F32) + given[...]) * (scale**3 / 6.0)
    products(other_half, 1 - parity(), own_factor[:, :width], x_twice[...], total)
    size = own_half.shape[1]
    at = pl.multiple_of(parity() * size, size)
    level_three[:, pl.ds(at, size)] = own_half[...]
    level_three[:, pl.ds(size - at, size)] = other_half[...]


def call(kernel, name, out_shape, scratch=(), in_specs=None, flops=0, moved=0, limit=32 * 2**20):
    shapes = [jax.ShapeDtypeStruct(dims, dtype) for dims, dtype in out_shape]
    vmem = pl.BlockSpec(memory_space=pltpu.VMEM)

    def run(*operands):
        return pl.pallas_call(
            kernel,
            out_shape=tuple(shapes),
            in_specs=in_specs or [vmem] * len(operands),
            out_specs=(vmem,) * len(shapes),
            scratch_shapes=list(scratch),
            compiler_params=pltpu.CompilerParams(vmem_limit_bytes=limit),
            cost_estimate=pl.CostEstimate(flops=flops, bytes_accessed=moved, transcendentals=0),
            name=name,
        )(*operands)

    return run


def path_of(recording, conv_weight, conv_bias, projection):
    length, channels = recording.shape
    layers, taps = conv_weight.shape[:2]
    width = projection.shape[1]
    rows = length + 2 * HALO
    outer, inner = edges_exchanged(recording)
    vmem, hbm = pl.BlockSpec(memory_space=pltpu.VMEM), pl.BlockSpec(memory_space=pltpu.HBM)
    weights = conv_weight.reshape(layers, taps * channels, channels)
    return call(
        functools.partial(conv_kernel, rows // 3),
        "conv",
        [((width, length), BF16), ((width, length + LANES), BF16)],
        scratch=[pltpu.VMEM((rows + 16, channels), F32)] * 2
        + [pltpu.VMEM(recording.shape, BF16), pltpu.VMEM(weights.shape, BF16), pltpu.SemaphoreType.DMA((layers + 1,))],
        in_specs=[hbm, vmem, vmem, hbm, vmem, vmem],
        flops=2 * layers * taps * length * channels**2,
        moved=2 * weights.size,
        limit=60 * 2**20,
    )(recording, outer, inner, weights, conv_bias, projection.T)


def per_device(recording, conv_weight, conv_bias, projection):
    length = recording.shape[0]
    width = projection.shape[1]
    wide_size, narrow_size = lax.axis_size("wide"), lax.axis_size("narrow")
    scale = float(length * wide_size * narrow_size) ** -0.2
    row_count = width // narrow_size
    count = width // 4 * row_count
    points, piece = path_of(recording, conv_weight, conv_bias, projection)

    half, square = ((count, LANES), F32), ((width, LANES), F32)
    message = ((count + width, LANES), BF16)

    order = [0]
    distance = narrow_size // 2
    held = {0: piece}
    while distance:
        for mask in list(order):
            held[mask ^ distance] = exchanged(held[mask], "narrow", distance)
            order.append(mask ^ distance)
        distance //= 2
    sums = ()
    order = sorted(order)
    for masks in (order[:2], order[2:]):
        sums = call(
            functools.partial(sums_kernel, masks, len(sums) > 0),
            "block_sums",
            [half, half, square, square],
            scratch=[pltpu.VMEM((width, length), F32)] * 3 + [pltpu.VMEM((2, count, length), BF16)],
            flops=2 * 10**9,
        )(*sums, *[held[mask] for mask in masks])
    kept, given, second, ends = sums
    (sent,) = call(give_kernel, "give", [message])(given, second)
    received = exchanged(sent, "wide", 1)
    pair_third, pair_second, sent = call(pair_kernel, "pair", [half, square, message])(kept, second, received)
    distance = 2
    received = exchanged(sent, "wide", distance)
    earlier, group_third, group_second = (), pair_third, pair_second
    while 2 * distance < wide_size:
        *earlier, group_third, group_second, sent = call(
            functools.partial(scan_kernel, distance, len(earlier) > 0),
            "scan",
            [half, square, half, square, message],
        )(*earlier, group_third, group_second, received)
        distance *= 2
        received = exchanged(sent, "wide", distance)
    if not earlier:
        earlier = [jnp.zeros(dims, dtype) for dims, dtype in (half, square)]
    total, sent = call(functools.partial(return_kernel, distance), "back", [half, ((count, LANES), BF16)])(
        earlier[0], received, kept
    )
    returned = exchanged(sent, "wide", 1)
    own_size = width * width // 2
    level_one, level_two, own_factor, x_twice, own_half = call(
        functools.partial(levels_kernel, scale, row_count, distance),
        "levels",
        [
            ((1, width), F32),
            ((width // 2, LANES), F32),
            ((row_count, LANES), F32),
            ((1, LANES), F32),
            ((row_count, own_size), F32),
        ],
        scratch=[pltpu.VMEM((width, LANES), F32)],
        flops=10**9,
    )(earlier[1], received, second, pair_second, ends, total, kept, pair_third)
    (level_three,) = call(
        functools.partial(finish_kernel, scale),
        "finish",
        [((row_count, 2 * own_size), F32)],
        scratch=[pltpu.VMEM((row_count, own_size), F32)],
    )(returned, given, own_factor, x_twice, own_half)
    return points.T, level_one, level_two.reshape(1, width * width), level_three[None]


def solution(mesh):
    return jax.shard_map(
        per_device,
        mesh=mesh,
        in_specs=(P(WHOLE, None), P(), P(), P()),
        out_specs=(P(WHOLE, None), P("wide", None), P("wide", None), P("wide", "narrow", None)),
        check_vma=False,
    )
```

```python
import functools

import jax
import jax.numpy as jnp
from jax import lax
from jax.experimental import pallas as pl
from jax.experimental.pallas import tpu as pltpu
from jax.sharding import PartitionSpec as P

HALO = 16
LANES = 128
F32 = jnp.float32
BF16 = jnp.bfloat16
NT = (((1,), (1,)), ((), ()))
WHOLE = ("wide", "narrow")


def exchanged(array, axis, distance):
    size = lax.axis_size(axis)
    return lax.ppermute(array, axis, [(i, i ^ distance) for i in range(size)])


def edges_exchanged(recording):
    length = recording.shape[0]
    is_odd = lax.axis_index("narrow") % 2
    outer = lax.dynamic_slice_in_dim(recording, is_odd * (length - HALO), HALO, 0)
    inner = lax.dynamic_slice_in_dim(recording, (1 - is_odd) * (length - HALO), HALO, 0)
    size = lax.axis_size("wide") * lax.axis_size("narrow")
    across = [(i, min(max(i - 1 + 2 * (i % 2), 0), size - 1)) for i in range(size)]
    outer = lax.ppermute(outer, WHOLE, across)
    inner = exchanged(inner, "narrow", 1)
    return outer, inner


def load_kernel(rec_hbm, weights_hbm, bias_hbm, proj_hbm, rec, first, bias, proj, sems):
    pairs = ((rec_hbm, rec), (weights_hbm.at[0], first), (bias_hbm, bias), (proj_hbm, proj))
    copies = [pltpu.make_async_copy(*pair, sems.at[i]) for i, pair in enumerate(pairs)]
    for copy in copies:
        copy.start()
    for copy in copies:
        copy.wait()


def conv_kernel(chunk, rec, outer, inner, first, weights_hbm, bias, proj, points, piece, even, odd, rest, path, sems):
    layers = 1 + rest.shape[0]
    length = rec.shape[0]
    rows = length + 2 * HALO
    far = HALO + length
    copies = [pltpu.make_async_copy(weights_hbm.at[i + 1], rest.at[i], sems.at[i]) for i in range(layers - 1)]
    copies[0].start()
    narrow = lax.axis_index("narrow")
    place = lax.axis_index("wide") * lax.axis_size("narrow") + narrow
    is_first = place == 0
    is_last = place == lax.axis_size("wide") * lax.axis_size("narrow") - 1
    is_odd = lax.rem(narrow, 2)
    at_end = jnp.logical_or(is_first, is_last)
    even[pl.ds(pl.multiple_of(8 + is_odd * far, 8), HALO), :] = jnp.where(at_end, 0.0, outer[...].astype(F32))
    even[pl.ds(pl.multiple_of(8 + (1 - is_odd) * far, 8), HALO), :] = inner[...].astype(F32)
    even[8 + HALO : 8 + far, :] = rec[...].astype(F32)
    width, padded = path.shape
    path[:, padded - LANES :] = jnp.zeros((width, LANES), F32)
    source, target = even, odd
    for layer in range(layers):
        if layer:
            copies[layer - 1].wait()
            if layer < layers - 1:
                copies[layer].start()
        weights = rest[layer - 1] if layer else first[...]
        reach = 2**layer
        for start in range(0, rows, chunk):
            size = min(chunk, rows - start)
            windows = [
                source[8 + start + k * reach : 8 + start + k * reach + size, :] for k in (-1, 0, 1)
            ]
            stacked = jnp.concatenate([window.astype(BF16) for window in windows], axis=1)
            conv = jnp.dot(stacked, weights, preferred_element_type=F32)
            half = 0.5 * (conv + bias[layer : layer + 1, :])
            hidden = (windows[1] + (half + half * jnp.tanh(half))).astype(BF16)
            if layer < layers - 1:
                target[8 + start : 8 + start + size, :] = hidden.astype(F32)
            else:
                part = lax.dot_general(hidden, proj[...], NT, preferred_element_type=F32)
                path[:, start : start + size] = part.astype(BF16).astype(F32).T
        if layer < layers - 1:
            target[8 : 8 + HALO, :] = jnp.where(is_first, 0.0, target[8 : 8 + HALO, :])
            target[8 + far : 8 + rows, :] = jnp.where(is_last, 0.0, target[8 + far : 8 + rows, :])
        source, target = target, source
    lane = lax.broadcasted_iota(jnp.int32, (width, LANES), 1)
    path[:, :LANES] = jnp.where(jnp.logical_and(is_first, lane < HALO), 0.0, path[:, :LANES])
    points[...] = pltpu.roll(path[...], padded - HALO, 1)[:, :length].astype(BF16)
    piece[...] = pltpu.roll(path[...], padded - HALO + 1, 1).astype(BF16)


def coefficients(piece, diff, lead, rest):
    padded = piece.shape[1]
    length = padded - LANES
    points = piece[...].astype(F32)
    after = pltpu.roll(points, padded - 1, 1)[:, :length]
    before = pltpu.roll(points, 1, 1)[:, :length]
    here = points[:, :length]
    middle = 0.5 * (after + before)
    diff[...] = after - before
    lead[...] = 2.0 * here + middle
    rest[...] = middle - here
    return points, after


def half_sum(half, piece, diff, lead, rest, lhs):
    width, padded = piece.shape
    length = padded - LANES
    row_count = 4 * lhs.shape[1] // width
    first_row = pl.multiple_of(lax.axis_index("narrow") * row_count, row_count)
    group = max(1, 16 // row_count)
    span = 2 * LANES
    sums = []
    for h in range(2):
        for lanes in [slice(at, at + span) for at in range(0, length, span)]:
            own_lead = lead[pl.ds(first_row, row_count), lanes]
            own_diff = diff[pl.ds(first_row, row_count), lanes]
            for at in range(0, width // 4, group):
                terms = []
                for g in range(group):
                    row = pl.ds(half * (width // 2) + 2 * (at + g) + h, 1)
                    terms.append(diff[row, lanes] * own_lead + rest[row, lanes] * own_diff)
                term = terms[0] if group == 1 else jnp.concatenate(terms, axis=0)
                lhs[h, at * row_count : (at + group) * row_count, lanes] = term.astype(BF16)
        sums.append(lax.dot_general(lhs[h], piece[:, :length], NT, preferred_element_type=F32))
    return jnp.concatenate(sums, axis=1)


def parity():
    return lax.rem(lax.axis_index("wide"), 2)


def given_kernel(masks, started, *refs):
    before, refs = refs[: 3 * started], refs[3 * started :]
    pieces, (given, second, ends, sent, diff, lead, rest, lhs) = refs[: len(masks)], refs[len(masks) :]
    values = [ref[...] for ref in before]
    for mask, piece in zip(masks, pieces):
        width, padded = piece.shape
        length = padded - LANES
        points, after = coefficients(piece, diff, lead, rest)
        crossed = lax.dot_general(after.astype(BF16), piece[:, :length], NT, preferred_element_type=F32)
        crossed = jnp.concatenate([crossed, crossed], axis=1)
        is_last = jnp.bitwise_xor(lax.axis_index("narrow"), mask) == lax.axis_size("narrow") - 1
        final = jnp.broadcast_to(points[:, length : length + 1], (width, LANES))
        previous = jnp.broadcast_to(points[:, length - 1 : length], (width, LANES))
        lane = lax.broadcasted_iota(jnp.int32, (width, LANES), 1)
        end_points = jnp.where(is_last, jnp.where(lane == 0, final, previous), 0.0)
        more = [half_sum(1 - parity(), piece, diff, lead, rest, lhs), crossed, end_points]
        values = [value + extra for value, extra in zip(values, more)] if values else more
    for target, value in zip((given, second, ends), values):
        target[...] = value
    pack(sent, values[0], values[1])


def kept_kernel(*refs):
    pieces, (kept, diff, lead, rest, lhs) = refs[:-5], refs[-5:]
    total = None
    for piece in pieces:
        coefficients(piece, diff, lead, rest)
        more = half_sum(parity(), piece, diff, lead, rest, lhs)
        total = more if total is None else total + more
    kept[...] = total


def pack(sent, total, doubled):
    count = total.shape[0]
    high = doubled.astype(BF16).astype(F32)
    lane = lax.broadcasted_iota(jnp.int32, doubled.shape, 1)
    sent[:count, :] = total.astype(BF16)
    sent[count:, :] = jnp.where(lane < LANES // 2, high, doubled - high).astype(BF16)


def unpack(received, count):
    coded = received[count:, :].astype(F32)
    return received[:count, :].astype(F32), coded + pltpu.roll(coded, LANES // 2, 1)


def pair_kernel(kept, second, received, pair_third, pair_second, sent):
    more_third, more_second = unpack(received, kept.shape[0])
    total = kept[...] + more_third
    doubled = second[...] + more_second
    pair_third[...] = total
    pair_second[...] = doubled
    pack(sent, total, doubled)


def is_later(distance):
    return jnp.bitwise_and(lax.axis_index("wide"), distance) != 0


def scan_kernel(distance, started, *refs):
    before, (group_third, group_second, received, third, second, new_third, new_second, sent) = (
        refs[: 2 * started],
        refs[2 * started :],
    )
    more_third, more_second = unpack(received, group_third.shape[0])
    earlier_third = jnp.where(is_later(distance), more_third, 0.0)
    earlier_second = jnp.where(is_later(distance), more_second, 0.0)
    if started:
        earlier_third, earlier_second = earlier_third + before[0][...], earlier_second + before[1][...]
    third[...] = earlier_third
    second[...] = earlier_second
    total, doubled = group_third[...] + more_third, group_second[...] + more_second
    new_third[...] = total
    new_second[...] = doubled
    pack(sent, total, doubled)


def return_kernel(distance, third, received, kept, earlier, sent):
    count = third.shape[0]
    total = third[...] + jnp.where(is_later(distance), received[:count, :].astype(F32), 0.0)
    earlier[...] = total
    sent[...] = jnp.where(parity() == 0, total + kept[...], total).astype(BF16)


def products(result, half, factor, x_twice, total):
    row_count, width = factor.shape
    lane = lax.broadcasted_iota(jnp.int32, (row_count, LANES), 1)
    factor = jnp.where(half == 0, factor[:, : width // 2], factor[:, width // 2 :])
    for at in range(width // 4):
        low = jnp.broadcast_to(factor[:, 2 * at : 2 * at + 1], (row_count, LANES))
        high = jnp.broadcast_to(factor[:, 2 * at + 1 : 2 * at + 2], (row_count, LANES))
        result[:, at * LANES : (at + 1) * LANES] = (
            jnp.where(lane < width, low, high) * x_twice - total[at * row_count : (at + 1) * row_count, :]
        )


def levels_kernel(
    scale, row_count, distance, second, received, own_second, pair_second, ends, earlier, kept, pair_third,
    level_one, level_two, own_factor, x_twice, own_half, held,
):
    width = second.shape[0]
    count = received.shape[0] - width
    is_first = parity() == 0
    coded = jnp.where(is_later(distance), received[count:, :].astype(F32), 0.0)
    crossed = second[...] + coded + pltpu.roll(coded, LANES // 2, 1)
    crossed = (crossed + jnp.where(is_first, own_second[...], pair_second[...]))[:, :width]
    end_cols = ends[...]
    end_rows = end_cols.T
    x_col, a_col = end_cols[:, 0:1], end_cols[:, 1:2]
    x_row, a_row = end_rows[0:1, :], end_rows[1:2, :]
    xx = x_col * x_row
    pairs = 0.5 * xx + 0.5 * (crossed.T - crossed)
    edge = a_col * x_row - a_col * a_row - 2.0 * x_col * a_row
    factor = pairs - edge / 6.0 - xx / 3.0
    level_one[...] = scale * x_row
    held[:, :width] = scale**2 * pairs
    level_two[:, :width] = held[pl.ds(0, width // 2, stride=2), :width]
    level_two[:, width:] = held[pl.ds(1, width // 2, stride=2), :width]
    held[:, :width] = scale**3 * factor
    first_row = pl.multiple_of(lax.axis_index("narrow") * row_count, row_count)
    own = held[pl.ds(first_row, row_count), :]
    own_factor[...] = own
    twice = jnp.concatenate([x_row, x_row], axis=1)
    x_twice[...] = twice
    total = (earlier[...] + jnp.where(is_first, kept[...], pair_third[...])) * (scale**3 / 6.0)
    products(own_half, parity(), own[:, :width], twice, total)


def finish_kernel(scale, received, given, own_factor, x_twice, own_half, level_three, other_half):
    width = own_factor.shape[1] // 2
    total = (received[...].astype(F32) + given[...]) * (scale**3 / 6.0)
    products(other_half, 1 - parity(), own_factor[:, :width], x_twice[...], total)
    size = own_half.shape[1]
    at = pl.multiple_of(parity() * size, size)
    level_three[:, pl.ds(at, size)] = own_half[...]
    level_three[:, pl.ds(size - at, size)] = other_half[...]


def call(kernel, name, out_shape, scratch=(), in_specs=None, flops=0, moved=0, limit=32 * 2**20):
    shapes = [jax.ShapeDtypeStruct(dims, dtype) for dims, dtype in out_shape]
    vmem = pl.BlockSpec(memory_space=pltpu.VMEM)

    def run(*operands):
        return pl.pallas_call(
            kernel,
            out_shape=tuple(shapes),
            in_specs=in_specs or [vmem] * len(operands),
            out_specs=(vmem,) * len(shapes),
            scratch_shapes=list(scratch),
            compiler_params=pltpu.CompilerParams(vmem_limit_bytes=limit),
            cost_estimate=pl.CostEstimate(flops=flops, bytes_accessed=moved, transcendentals=0),
            name=name,
        )(*operands)

    return run


def path_of(recording, conv_weight, conv_bias, projection):
    length, channels = recording.shape
    layers, taps = conv_weight.shape[:2]
    width = projection.shape[1]
    rows = length + 2 * HALO
    outer, inner = edges_exchanged(recording)
    vmem, hbm = pl.BlockSpec(memory_space=pltpu.VMEM), pl.BlockSpec(memory_space=pltpu.HBM)
    weights = conv_weight.reshape(layers, taps * channels, channels)
    far = [pltpu.with_memory_space_constraint(held, pltpu.HBM) for held in (recording, weights, conv_bias, projection.T)]
    near = call(
        load_kernel,
        "load",
        [(recording.shape, BF16), (weights.shape[1:], BF16), (conv_bias.shape, F32), ((width, channels), BF16)],
        scratch=[pltpu.SemaphoreType.DMA((4,))],
        in_specs=[hbm] * 4,
        flops=10**9,
        moved=2 * (recording.size + weights.size // layers),
    )(*far)
    return call(
        functools.partial(conv_kernel, 3 * LANES),
        "conv",
        [((width, length), BF16), ((width, length + LANES), BF16)],
        scratch=[pltpu.VMEM((rows + 16, channels), F32)] * 2
        + [
            pltpu.VMEM((layers - 1,) + weights.shape[1:], BF16),
            pltpu.VMEM((width, length + LANES), F32),
            pltpu.SemaphoreType.DMA((layers - 1,)),
        ],
        in_specs=[vmem] * 4 + [hbm] + [vmem] * 2,
        flops=2 * layers * taps * length * channels**2,
        moved=2 * weights.size,
    )(near[0], outer, inner, near[1], far[1], near[2], near[3])


def per_device(recording, conv_weight, conv_bias, projection):
    length = recording.shape[0]
    width = projection.shape[1]
    wide_size, narrow_size = lax.axis_size("wide"), lax.axis_size("narrow")
    scale = float(length * wide_size * narrow_size) ** -0.2
    row_count = width // narrow_size
    count = width // 4 * row_count
    points, piece = path_of(recording, conv_weight, conv_bias, projection)

    half, square = ((count, LANES), F32), ((width, LANES), F32)
    message = ((count + width, LANES), BF16)

    scratch = [pltpu.VMEM((width, length), F32)] * 3 + [pltpu.VMEM((2, count, length), BF16)]
    share = 10**9 // 2
    pieces = {0: piece, 1: exchanged(piece, "narrow", 1)}
    distance = narrow_size // 2
    arrived = {}
    while distance > 1:
        for mask, held in [(0, piece)] + sorted(arrived.items()):
            arrived[mask ^ distance] = exchanged(held, "narrow", distance)
        distance //= 2
    sums = call(
        functools.partial(given_kernel, (0, 1), False),
        "given",
        [half, square, square, message],
        scratch=scratch,
        flops=2 * share,
    )(piece, pieces[1])[:3]
    sums, arrived = lax.optimization_barrier((sums, arrived))
    masks = []
    for mask, held in sorted(arrived.items()):
        pieces[mask], pieces[mask ^ 1] = held, exchanged(held, "narrow", 1)
        masks += [mask, mask ^ 1]
    given, second, ends, sent = call(
        functools.partial(given_kernel, masks, True),
        "given",
        [half, square, square, message],
        scratch=scratch,
        flops=share * len(masks),
    )(*sums, *[pieces[mask] for mask in masks])
    received = exchanged(sent, "wide", 1)
    (kept,) = call(kept_kernel, "kept", [half], scratch=scratch, flops=share * len(pieces))(
        *[pieces[mask] for mask in sorted(pieces)]
    )
    pair_third, pair_second, sent = call(pair_kernel, "pair", [half, square, message])(kept, second, received)
    distance = 2
    received = exchanged(sent, "wide", distance)
    earlier, group_third, group_second = (), pair_third, pair_second
    while 2 * distance < wide_size:
        *earlier, group_third, group_second, sent = call(
            functools.partial(scan_kernel, distance, len(earlier) > 0),
            "scan",
            [half, square, half, square, message],
        )(*earlier, group_third, group_second, received)
        distance *= 2
        received = exchanged(sent, "wide", distance)
    if not earlier:
        earlier = [jnp.zeros(dims, dtype) for dims, dtype in (half, square)]
    total, sent = call(functools.partial(return_kernel, distance), "back", [half, ((count, LANES), BF16)])(
        earlier[0], received, kept
    )
    returned = exchanged(sent, "wide", 1)
    own_size = width * width // 2
    level_one, level_two, own_factor, x_twice, own_half = call(
        functools.partial(levels_kernel, scale, row_count, distance),
        "levels",
        [
            ((1, width), F32),
            ((width // 2, LANES), F32),
            ((row_count, LANES), F32),
            ((1, LANES), F32),
            ((row_count, own_size), F32),
        ],
        scratch=[pltpu.VMEM((width, LANES), F32)],
        flops=10**9,
    )(earlier[1], received, second, pair_second, ends, total, kept, pair_third)
    (level_three,) = call(
        functools.partial(finish_kernel, scale),
        "finish",
        [((row_count, 2 * own_size), F32)],
        scratch=[pltpu.VMEM((row_count, own_size), F32)],
    )(returned, given, own_factor, x_twice, own_half)
    return points.T, level_one, level_two.reshape(1, width * width), level_three[None]


def solution(mesh):
    return jax.shard_map(
        per_device,
        mesh=mesh,
        in_specs=(P(WHOLE, None), P(), P(), P()),
        out_specs=(P(WHOLE, None), P("wide", None), P("wide", None), P("wide", "narrow", None)),
        check_vma=False,
    )
```

```python
import functools

import jax
import jax.numpy as jnp
from jax import lax
from jax.experimental import pallas as pl
from jax.experimental.pallas import tpu as pltpu
from jax.sharding import PartitionSpec as P

HALO = 16
LANES = 128
F32 = jnp.float32
BF16 = jnp.bfloat16
NT = (((1,), (1,)), ((), ()))
WHOLE = ("wide", "narrow")


def exchanged(array, axis, distance):
    size = lax.axis_size(axis)
    return lax.ppermute(array, axis, [(i, i ^ distance) for i in range(size)])


def edges_exchanged(recording):
    length = recording.shape[0]
    is_odd = lax.axis_index("narrow") % 2
    outer = lax.dynamic_slice_in_dim(recording, is_odd * (length - HALO), HALO, 0)
    inner = lax.dynamic_slice_in_dim(recording, (1 - is_odd) * (length - HALO), HALO, 0)
    wide_size, narrow_size = lax.axis_size("wide"), lax.axis_size("narrow")
    size = wide_size * narrow_size
    inside = {i: (i - 1 + 2 * (i % 2)) % narrow_size for i in range(narrow_size)}
    over = {i: (i - 1 + 2 * (i % 2)) % size for i in range(size)}
    if narrow_size > 2:
        end = size - 1
        over.update({0: 1, 1: 2, 2: 0, end: end - 1, end - 1: end - 2, end - 2: end})
    inner = exchanged(inner, "narrow", 1)
    inside = lax.ppermute(outer, "narrow", list(inside.items()))
    over = lax.ppermute(outer, WHOLE, list(over.items()))
    return over, inside, inner


def load_kernel(rec_hbm, weights_hbm, bias_hbm, proj_hbm, padded, weights, bias, proj, rec, sems):
    early = weights.shape[0]
    pairs = ((rec_hbm, rec), (weights_hbm.at[:early], weights), (bias_hbm, bias), (proj_hbm, proj))
    copies = [pltpu.make_async_copy(*pair, sems.at[i]) for i, pair in enumerate(pairs)]
    for copy in copies:
        copy.start()
    copies[0].wait()
    padded[: 8 + HALO, :] = jnp.zeros((8 + HALO, rec.shape[1]), F32)
    padded[8 + HALO : 8 + HALO + rec.shape[0], :] = rec[...].astype(F32)
    padded[8 + HALO + rec.shape[0] :, :] = jnp.zeros((8 + HALO, rec.shape[1]), F32)
    for copy in copies[1:]:
        copy.wait()


def conv_kernel(chunk, _, over, inside, inner, weights, weights_hbm, bias, proj, piece, padded, even, last_weights, path, sem):
    layers = 1 + weights.shape[0]
    rows = padded.shape[0] - 16
    length = rows - 2 * HALO
    far = HALO + length
    copy = pltpu.make_async_copy(weights_hbm.at[layers - 1], last_weights, sem)
    copy.start()
    narrow = lax.axis_index("narrow")
    place = lax.axis_index("wide") * lax.axis_size("narrow") + narrow
    is_first = place == 0
    is_last = place == lax.axis_size("wide") * lax.axis_size("narrow") - 1
    is_odd = lax.rem(narrow, 2) == 1
    width, full = path.shape
    path[:, full - LANES :] = jnp.zeros((width, LANES), F32)
    at_end = jnp.logical_or(is_first, is_last)
    at_edge = jnp.logical_or(narrow == 0, narrow == lax.axis_size("narrow") - 1)
    beyond = jnp.where(at_edge, over[...].astype(F32), inside[...].astype(F32))
    beyond = jnp.where(at_end, 0.0, beyond)
    within = inner[...].astype(F32)
    padded[8 : 8 + HALO, :] = jnp.where(is_odd, within, beyond)
    padded[8 + far : 8 + rows, :] = jnp.where(is_odd, beyond, within)
    source, target = padded, even
    for layer in range(layers):
        if layer == layers - 1:
            copy.wait()
        reach = 2**layer
        for start in range(0, rows, chunk):
            size = min(chunk, rows - start)
            windows = [
                source[8 + start + k * reach : 8 + start + k * reach + size, :] for k in (-1, 0, 1)
            ]
            conv = bias[layer : layer + 1, :]
            for tap, window in enumerate(windows):
                tap_weights = last_weights[tap] if layer == layers - 1 else weights[layer, tap]
                conv = conv + jnp.dot(window.astype(BF16), tap_weights, preferred_element_type=F32)
            half = 0.5 * conv
            hidden = (windows[1] + (half + half * jnp.tanh(half))).astype(BF16)
            if layer < layers - 1:
                target[8 + start : 8 + start + size, :] = hidden.astype(F32)
            else:
                part = lax.dot_general(hidden, proj[...], NT, preferred_element_type=F32)
                path[:, start : start + size] = part.astype(BF16).astype(F32).T
        if layer < layers - 1:
            target[8 : 8 + HALO, :] = jnp.where(is_first, 0.0, target[8 : 8 + HALO, :])
            target[8 + far : 8 + rows, :] = jnp.where(is_last, 0.0, target[8 + far : 8 + rows, :])
        source, target = target, source
    lane = lax.broadcasted_iota(jnp.int32, (width, LANES), 1)
    path[:, :LANES] = jnp.where(jnp.logical_and(is_first, lane < HALO), 0.0, path[:, :LANES])
    piece[...] = pltpu.roll(path[...], full - HALO + 1, 1).astype(BF16)


def coefficients(piece, diff, lead, rest):
    padded = piece.shape[1]
    length = padded - LANES
    points = piece[...].astype(F32)
    after = pltpu.roll(points, padded - 1, 1)[:, :length]
    before = pltpu.roll(points, 1, 1)[:, :length]
    here = points[:, :length]
    middle = 0.5 * (after + before)
    diff[...] = after - before
    lead[...] = 2.0 * here + middle
    rest[...] = middle - here
    return points, after


def half_sum(half, piece, diff, lead, rest, lhs):
    width, padded = piece.shape
    length = padded - LANES
    row_count = 4 * lhs.shape[1] // width
    first_row = pl.multiple_of(lax.axis_index("narrow") * row_count, row_count)
    group = max(1, 16 // row_count)
    span = 2 * LANES
    sums = []
    for h in range(2):
        for lanes in [slice(at, at + span) for at in range(0, length, span)]:
            own_lead = lead[pl.ds(first_row, row_count), lanes]
            own_diff = diff[pl.ds(first_row, row_count), lanes]
            for at in range(0, width // 4, group):
                terms = []
                for g in range(group):
                    row = pl.ds(half * (width // 2) + 2 * (at + g) + h, 1)
                    terms.append(diff[row, lanes] * own_lead + rest[row, lanes] * own_diff)
                term = terms[0] if group == 1 else jnp.concatenate(terms, axis=0)
                lhs[h, at * row_count : (at + group) * row_count, lanes] = term.astype(BF16)
        sums.append(lax.dot_general(lhs[h], piece[:, :length], NT, preferred_element_type=F32))
    return jnp.concatenate(sums, axis=1)


def parity():
    return lax.rem(lax.axis_index("wide"), 2)


def given_kernel(masks, started, ended, *refs):
    before, refs = refs[: 3 * started], refs[3 * started :]
    pieces, refs = refs[: len(masks)], refs[len(masks) :]
    (given, second, ends, extra), (diff, lead, rest, lhs) = refs[:4], refs[-4:]
    kept_total = None
    values = [ref[...] for ref in before]
    for mask, piece in zip(masks, pieces):
        width, padded = piece.shape
        length = padded - LANES
        points, after = coefficients(piece, diff, lead, rest)
        if mask == 0:
            extra[...] = after.astype(BF16)
        crossed = lax.dot_general(after.astype(BF16), piece[:, :length], NT, preferred_element_type=F32)
        is_last = jnp.bitwise_xor(lax.axis_index("narrow"), mask) == lax.axis_size("narrow") - 1
        final = jnp.broadcast_to(points[:, length : length + 1], (width, LANES))
        previous = jnp.broadcast_to(points[:, length - 1 : length], (width, LANES))
        lane = lax.broadcasted_iota(jnp.int32, (width, LANES), 1)
        end_points = jnp.where(is_last, jnp.where(lane == 0, final, previous), 0.0)
        more = [half_sum(1 - parity(), piece, diff, lead, rest, lhs), folded(crossed), end_points]
        values = [value + other for value, other in zip(values, more)] if values else more
        if not started:
            kept = half_sum(parity(), piece, diff, lead, rest, lhs)
            kept_total = kept if kept_total is None else kept_total + kept
    if not started:
        refs[4][...] = kept_total
    for target, value in zip((given, second, ends), values):
        target[...] = value
    if ended:
        pack(extra, values[0], values[1])


def folded(crossed):
    width = crossed.shape[0]
    turned = crossed.T - crossed
    row = lax.broadcasted_iota(jnp.int32, (width // 2, width), 0)
    lane = lax.broadcasted_iota(jnp.int32, (width // 2, width), 1)
    corner = jnp.concatenate([turned[width // 2 :, width // 2 :], turned[width // 2 :, : width // 2]], axis=1)
    upper = jnp.where(lane > row, turned[: width // 2, :], jnp.where(lane < row, corner, 0.0))
    return jnp.concatenate([upper, upper], axis=1)


def unfolded(upper):
    size = upper.shape[0]
    row = lax.broadcasted_iota(jnp.int32, (size, size), 0)
    lane = lax.broadcasted_iota(jnp.int32, (size, size), 1)
    near, far = upper[:, :size], upper[:, size : 2 * size]
    above = jnp.where(lane > row, near, 0.0)
    below = jnp.where(lane < row, near, 0.0)
    return jnp.concatenate(
        [
            jnp.concatenate([above - above.T, far], axis=1),
            jnp.concatenate([-far.T, below - below.T], axis=1),
        ],
        axis=0,
    )


def kept_kernel(before, *refs):
    pieces, (kept, diff, lead, rest, lhs) = refs[:-5], refs[-5:]
    total = before[...]
    for piece in pieces:
        coefficients(piece, diff, lead, rest)
        total = total + half_sum(parity(), piece, diff, lead, rest, lhs)
    kept[...] = total


def pack(sent, total, doubled):
    count = total.shape[0]
    high = doubled.astype(BF16).astype(F32)
    lane = lax.broadcasted_iota(jnp.int32, doubled.shape, 1)
    sent[:count, :] = total.astype(BF16)
    sent[count:, :] = jnp.where(lane < LANES // 2, high, doubled - high).astype(BF16)


def unpack(received, count):
    coded = received[count:, :].astype(F32)
    return received[:count, :].astype(F32), coded + pltpu.roll(coded, LANES // 2, 1)


def pair_kernel(kept, second, received, pair_third, pair_second, sent):
    more_third, more_second = unpack(received, kept.shape[0])
    total = kept[...] + more_third
    doubled = second[...] + more_second
    pair_third[...] = total
    pair_second[...] = doubled
    pack(sent, total, doubled)


def is_later(distance):
    return jnp.bitwise_and(lax.axis_index("wide"), distance) != 0


def scan_kernel(distance, started, ended, *refs):
    before, refs = refs[: 2 * started], refs[2 * started :]
    group_third, group_second, received, third, second, sent = refs[:6]
    more_third, more_second = unpack(received, group_third.shape[0])
    total, doubled = group_third[...] + more_third, group_second[...] + more_second
    pack(sent, total, doubled)
    earlier_third = jnp.where(is_later(distance), more_third, 0.0)
    earlier_second = jnp.where(is_later(distance), more_second, 0.0)
    if started:
        earlier_third, earlier_second = earlier_third + before[0][...], earlier_second + before[1][...]
    third[...] = earlier_third
    second[...] = earlier_second
    if not ended:
        refs[6][...] = total
        refs[7][...] = doubled


def return_kernel(distance, third, received, kept, earlier, sent):
    count = third.shape[0]
    total = third[...] + jnp.where(is_later(distance), received[:count, :].astype(F32), 0.0)
    earlier[...] = total
    sent[...] = jnp.where(parity() == 0, total + kept[...], total).astype(BF16)


def products(result, half, factor, x_twice, total):
    row_count, width = factor.shape
    lane = lax.broadcasted_iota(jnp.int32, (row_count, LANES), 1)
    factor = jnp.where(half == 0, factor[:, : width // 2], factor[:, width // 2 :])
    for at in range(width // 4):
        low = jnp.broadcast_to(factor[:, 2 * at : 2 * at + 1], (row_count, LANES))
        high = jnp.broadcast_to(factor[:, 2 * at + 1 : 2 * at + 2], (row_count, LANES))
        result[:, at * LANES : (at + 1) * LANES] = (
            jnp.where(lane < width, low, high) * x_twice - total[at * row_count : (at + 1) * row_count, :]
        )


def levels_kernel(
    scale, row_count, distance, second, received, own_second, pair_second, ends, earlier, kept, pair_third, given,
    level_one, level_two, partly, rest, held, own_half, sem,
):
    width = ends.shape[0]
    count = received.shape[0] - second.shape[0]
    is_first = parity() == 0
    end_cols = ends[...]
    end_rows = end_cols.T
    x_col, a_col = end_cols[:, 0:1], end_cols[:, 1:2]
    x_row, a_row = end_rows[0:1, :], end_rows[1:2, :]
    xx = x_col * x_row
    edge = a_col * x_row - a_col * a_row - 2.0 * x_col * a_row
    coded = jnp.where(is_later(distance), received[count:, :].astype(F32), 0.0)
    upper = second[...] + coded + pltpu.roll(coded, LANES // 2, 1)
    upper = upper + jnp.where(is_first, own_second[...], pair_second[...])
    pairs = 0.5 * xx + 0.5 * unfolded(upper)
    factor = pairs - edge / 6.0 - xx / 3.0
    level_one[...] = scale * x_row
    held[:, :width] = scale**3 * factor
    first_row = pl.multiple_of(lax.axis_index("narrow") * row_count, row_count)
    own = held[pl.ds(first_row, row_count), :width]
    twice = jnp.concatenate([x_row, x_row], axis=1)
    total = (earlier[...] + jnp.where(is_first, kept[...], pair_third[...])) * (scale**3 / 6.0)
    products(own_half, parity(), own, twice, total)
    size = own_half.shape[1]
    at = pl.multiple_of(parity() * size, size)
    copy = pltpu.make_async_copy(own_half, partly.at[:, pl.ds(at, size)], sem)
    copy.start()
    products(rest, 1 - parity(), own, twice, given[...] * (scale**3 / 6.0))
    held[:, :width] = scale**2 * pairs
    level_two[:, :width] = held[pl.ds(0, width // 2, stride=2), :width]
    level_two[:, width:] = held[pl.ds(1, width // 2, stride=2), :width]
    copy.wait()


def finish_kernel(scale, row_count, received, rest, partly, level_three, other_half, sem):
    size = rest.shape[1]
    for at in range(size // LANES):
        lanes = slice(at * LANES, (at + 1) * LANES)
        come = received[at * row_count : (at + 1) * row_count, :].astype(F32)
        other_half[:, lanes] = rest[:, lanes] - come * (scale**3 / 6.0)
    at = pl.multiple_of((1 - parity()) * size, size)
    copy = pltpu.make_async_copy(other_half, level_three.at[:, pl.ds(at, size)], sem)
    copy.start()
    copy.wait()


VMEM = pl.BlockSpec(memory_space=pltpu.VMEM)
HBM = pl.BlockSpec(memory_space=pltpu.HBM)


def call(kernel, name, out_shape, scratch=(), in_specs=None, out_specs=None, aliases=None, flops=0, moved=0):
    shapes = [jax.ShapeDtypeStruct(dims, dtype) for dims, dtype in out_shape]

    def run(*operands):
        return pl.pallas_call(
            kernel,
            out_shape=tuple(shapes),
            in_specs=in_specs or [VMEM] * len(operands),
            out_specs=out_specs or (VMEM,) * len(shapes),
            input_output_aliases=aliases or {},
            scratch_shapes=list(scratch),
            compiler_params=pltpu.CompilerParams(vmem_limit_bytes=32 * 2**20),
            cost_estimate=pl.CostEstimate(flops=flops, bytes_accessed=moved, transcendentals=0),
            name=name,
        )(*operands)

    return run


def path_of(recording, conv_weight, conv_bias, projection):
    length, channels = recording.shape
    layers, taps = conv_weight.shape[:2]
    width = projection.shape[1]
    rows = length + 2 * HALO
    edges = edges_exchanged(recording)
    buffer = ((rows + 16, channels), F32)
    far = (recording, conv_weight, conv_bias, projection.T)
    far = [pltpu.with_memory_space_constraint(held, pltpu.HBM) for held in far]
    padded, *near = call(
        load_kernel,
        "load",
        [buffer, ((layers - 1,) + conv_weight.shape[1:], BF16), (conv_bias.shape, F32), ((width, channels), BF16)],
        scratch=[pltpu.VMEM(recording.shape, BF16), pltpu.SemaphoreType.DMA((4,))],
        in_specs=[HBM] * len(far),
        flops=10**9,
        moved=2 * sum(held.size for held in far),
    )(*far)
    piece, _ = call(
        functools.partial(conv_kernel, 3 * LANES),
        "conv",
        [((width, length + LANES), BF16), buffer],
        scratch=[
            pltpu.VMEM(buffer[0], F32),
            pltpu.VMEM(conv_weight.shape[1:], BF16),
            pltpu.VMEM((width, length + LANES), F32),
            pltpu.SemaphoreType.DMA,
        ],
        in_specs=[VMEM] * 5 + [HBM] + [VMEM] * 2,
        aliases={0: 1},
        flops=2 * layers * taps * length * channels**2,
        moved=2 * conv_weight.size,
    )(padded, *edges, near[0], far[1], near[1], near[2])
    return piece


def per_device(recording, conv_weight, conv_bias, projection):
    length = recording.shape[0]
    width = projection.shape[1]
    wide_size, narrow_size = lax.axis_size("wide"), lax.axis_size("narrow")
    scale = float(length * wide_size * narrow_size) ** -0.2
    row_count = width // narrow_size
    count = width // 4 * row_count
    piece = path_of(recording, conv_weight, conv_bias, projection)

    half, square, folds = ((count, LANES), F32), ((width, LANES), F32), ((width // 2, LANES), F32)
    message = ((count + width // 2, LANES), BF16)

    scratch = [pltpu.VMEM((width, length), F32)] * 3 + [pltpu.VMEM((2, count, length), BF16)]
    share = 10**9 // 2
    pieces = {0: piece, 1: exchanged(piece, "narrow", 1)}
    distance = narrow_size // 2
    arrived = {}
    while distance > 1:
        for mask, held in [(0, piece)] + sorted(arrived.items()):
            arrived[mask ^ distance] = exchanged(held, "narrow", distance)
        distance //= 2
    *sums, points, kept = call(
        functools.partial(given_kernel, (0, 1), False, False),
        "given",
        [half, folds, square, ((width, length), BF16), half],
        scratch=scratch,
        flops=4 * share,
    )(piece, pieces[1])
    sums, arrived = lax.optimization_barrier((sums, arrived))
    for mask, held in sorted(arrived.items()):
        pieces[mask], pieces[mask ^ 1] = held, exchanged(held, "narrow", 1)
    masks = sorted(arrived) + [mask ^ 1 for mask in sorted(arrived)]
    for mask in masks:
        *sums, sent = call(
            functools.partial(given_kernel, (mask,), True, mask == masks[-1]),
            "given",
            [half, folds, square, message],
            scratch=scratch,
            flops=share,
        )(*sums, pieces[mask])
    given, second, ends = sums
    received = exchanged(sent, "wide", 1)
    (kept,) = call(kept_kernel, "kept", [half], scratch=scratch, flops=share * len(masks))(
        kept, *[pieces[mask] for mask in masks]
    )
    pair_third, pair_second, sent = call(pair_kernel, "pair", [half, folds, message])(kept, second, received)
    distance = 2
    received = exchanged(sent, "wide", distance)
    earlier, group_third, group_second = (), pair_third, pair_second
    while 2 * distance < wide_size:
        ended = 4 * distance >= wide_size
        *earlier, sent = call(
            functools.partial(scan_kernel, distance, len(earlier) > 0, ended),
            "scan",
            [half, folds, message] + ([] if ended else [half, folds]),
        )(*earlier, group_third, group_second, received)
        if not ended:
            sent, group_third, group_second = earlier[2], earlier[3], sent
            earlier = earlier[:2]
        distance *= 2
        received = exchanged(sent, "wide", distance)
    if not earlier:
        earlier = [jnp.zeros(dims, dtype) for dims, dtype in (half, folds)]
    total, sent = call(functools.partial(return_kernel, distance), "back", [half, ((count, LANES), BF16)])(
        earlier[0], received, kept
    )
    returned = exchanged(sent, "wide", 1)
    own_size = width * width // 2
    third_shape = ((row_count, 2 * own_size), F32)
    half_buffer = ((row_count, own_size), F32)
    level_one, level_two, partly, rest = call(
        functools.partial(levels_kernel, scale, row_count, distance),
        "levels",
        [((1, width), F32), folds, third_shape, half_buffer],
        scratch=[pltpu.VMEM((width, LANES), F32), pltpu.VMEM(half_buffer[0], F32), pltpu.SemaphoreType.DMA],
        out_specs=(VMEM, VMEM, HBM, VMEM),
        flops=10**9,
    )(earlier[1], received, second, pair_second, ends, total, kept, pair_third, given)
    (level_three,) = call(
        functools.partial(finish_kernel, scale, row_count),
        "finish",
        [third_shape],
        scratch=[pltpu.VMEM(half_buffer[0], F32), pltpu.SemaphoreType.DMA],
        in_specs=[VMEM, VMEM, HBM],
        out_specs=(HBM,),
        aliases={2: 0},
    )(returned, rest, partly)
    return points.T, level_one, level_two.reshape(1, width * width), level_three[None]


def solution(mesh):
    return jax.shard_map(
        per_device,
        mesh=mesh,
        in_specs=(P(WHOLE, None), P(), P(), P()),
        out_specs=(P(WHOLE, None), P("wide", None), P("wide", None), P("wide", "narrow", None)),
        check_vma=False,
    )
```

```python
import functools

import jax
import jax.numpy as jnp
from jax import lax
from jax.experimental import pallas as pl
from jax.experimental.pallas import tpu as pltpu
from jax.sharding import PartitionSpec as P

HALO = 16
ENDS = 16
LANES = 128
F32 = jnp.float32
BF16 = jnp.bfloat16
NT = (((1,), (1,)), ((), ()))
WHOLE = ("wide", "narrow")


def exchanged(array, axis, distance):
    size = lax.axis_size(axis)
    return lax.ppermute(array, axis, [(i, i ^ distance) for i in range(size)])


def edges_exchanged(recording):
    length = recording.shape[0]
    is_odd = lax.axis_index("narrow") % 2
    outer = lax.dynamic_slice_in_dim(recording, is_odd * (length - HALO), HALO, 0)
    inner = lax.dynamic_slice_in_dim(recording, (1 - is_odd) * (length - HALO), HALO, 0)
    wide_size, narrow_size = lax.axis_size("wide"), lax.axis_size("narrow")
    size = wide_size * narrow_size
    inside = {i: (i - 1 + 2 * (i % 2)) % narrow_size for i in range(narrow_size)}
    over = {i: (i - 1 + 2 * (i % 2)) % size for i in range(size)}
    if narrow_size > 2:
        end = size - 1
        over.update({0: 1, 1: 2, 2: 0, end: end - 1, end - 1: end - 2, end - 2: end})
    inner = exchanged(inner, "narrow", 1)
    inside = lax.ppermute(outer, "narrow", list(inside.items()))
    over = lax.ppermute(outer, WHOLE, list(over.items()))
    return over, inside, inner


def load_kernel(rec_hbm, weights_hbm, bias_hbm, proj_hbm, padded, weights, bias, proj, rec, sems):
    early = weights.shape[0]
    pairs = ((rec_hbm, rec), (weights_hbm.at[:early], weights), (bias_hbm, bias), (proj_hbm, proj))
    copies = [pltpu.make_async_copy(*pair, sems.at[i]) for i, pair in enumerate(pairs)]
    for copy in copies:
        copy.start()
    copies[0].wait()
    padded[: 8 + HALO, :] = jnp.zeros((8 + HALO, rec.shape[1]), F32)
    padded[8 + HALO : 8 + HALO + rec.shape[0], :] = rec[...].astype(F32)
    padded[8 + HALO + rec.shape[0] :, :] = jnp.zeros((8 + HALO, rec.shape[1]), F32)
    for copy in copies[1:]:
        copy.wait()


def conv_kernel(chunk, _, over, inside, inner, weights, weights_hbm, bias, proj, piece, padded, even, last_weights, path, sem):
    layers = 1 + weights.shape[0]
    rows = padded.shape[0] - 16
    length = rows - 2 * HALO
    far = HALO + length
    copy = pltpu.make_async_copy(weights_hbm.at[layers - 1], last_weights, sem)
    copy.start()
    narrow = lax.axis_index("narrow")
    place = lax.axis_index("wide") * lax.axis_size("narrow") + narrow
    is_first = place == 0
    is_last = place == lax.axis_size("wide") * lax.axis_size("narrow") - 1
    is_odd = lax.rem(narrow, 2) == 1
    width, full = path.shape
    path[:, full - LANES :] = jnp.zeros((width, LANES), F32)
    at_end = jnp.logical_or(is_first, is_last)
    at_edge = jnp.logical_or(narrow == 0, narrow == lax.axis_size("narrow") - 1)
    beyond = jnp.where(at_edge, over[...].astype(F32), inside[...].astype(F32))
    beyond = jnp.where(at_end, 0.0, beyond)
    within = inner[...].astype(F32)
    padded[8 : 8 + HALO, :] = jnp.where(is_odd, within, beyond)
    padded[8 + far : 8 + rows, :] = jnp.where(is_odd, beyond, within)
    source, target = padded, even
    for layer in range(layers):
        if layer == layers - 1:
            copy.wait()
        reach = 2**layer
        for start in range(0, rows, chunk):
            size = min(chunk, rows - start)
            windows = [
                source[8 + start + k * reach : 8 + start + k * reach + size, :] for k in (-1, 0, 1)
            ]
            conv = bias[layer : layer + 1, :]
            for tap, window in enumerate(windows):
                tap_weights = last_weights[tap] if layer == layers - 1 else weights[layer, tap]
                conv = conv + jnp.dot(window.astype(BF16), tap_weights, preferred_element_type=F32)
            half = 0.5 * conv
            hidden = (windows[1] + (half + half * jnp.tanh(half))).astype(BF16)
            if layer < layers - 1:
                target[8 + start : 8 + start + size, :] = hidden.astype(F32)
            else:
                part = lax.dot_general(hidden, proj[...], NT, preferred_element_type=F32)
                path[:, start : start + size] = part.astype(BF16).astype(F32).T
        if layer < layers - 1:
            target[8 : 8 + HALO, :] = jnp.where(is_first, 0.0, target[8 : 8 + HALO, :])
            target[8 + far : 8 + rows, :] = jnp.where(is_last, 0.0, target[8 + far : 8 + rows, :])
        source, target = target, source
    lane = lax.broadcasted_iota(jnp.int32, (width, LANES), 1)
    path[:, :LANES] = jnp.where(jnp.logical_and(is_first, lane < HALO), 0.0, path[:, :LANES])
    piece[...] = pltpu.roll(path[...], full - HALO + 1, 1).astype(BF16)


def coefficients(piece, diff, lead, rest):
    padded = piece.shape[1]
    length = padded - LANES
    points = piece[...].astype(F32)
    after = pltpu.roll(points, padded - 1, 1)[:, :length]
    before = pltpu.roll(points, 1, 1)[:, :length]
    here = points[:, :length]
    middle = 0.5 * (after + before)
    diff[...] = after - before
    lead[...] = 2.0 * here + middle
    rest[...] = middle - here
    return points, after


def half_sum(owner, half, piece, diff, lead, rest, lhs):
    width, padded = piece.shape
    length = padded - LANES
    row_count = 4 * lhs.shape[1] // width
    first_row = pl.multiple_of(owner * row_count, row_count)
    group = max(1, 16 // row_count)
    span = 2 * LANES
    sums = []
    for h in range(2):
        for lanes in [slice(at, at + span) for at in range(0, length, span)]:
            own_lead = lead[pl.ds(first_row, row_count), lanes]
            own_diff = diff[pl.ds(first_row, row_count), lanes]
            for at in range(0, width // 4, group):
                terms = []
                for g in range(group):
                    row = pl.ds(half * (width // 2) + 2 * (at + g) + h, 1)
                    terms.append(diff[row, lanes] * own_lead + rest[row, lanes] * own_diff)
                term = terms[0] if group == 1 else jnp.concatenate(terms, axis=0)
                lhs[h, at * row_count : (at + group) * row_count, lanes] = term.astype(BF16)
        sums.append(lax.dot_general(lhs[h], piece[:, :length], NT, preferred_element_type=F32))
    return jnp.concatenate(sums, axis=1)


def parity():
    return lax.rem(lax.axis_index("wide"), 2)


def target_sum(target, *refs):
    across, mask = target
    owner = jnp.bitwise_xor(lax.axis_index("narrow"), mask)
    return half_sum(owner, 1 - parity() if across else parity(), *refs)


def besides(mask, piece, points, after):
    width, padded = piece.shape
    length = padded - LANES
    crossed = lax.dot_general(after.astype(BF16), piece[:, :length], NT, preferred_element_type=F32)
    lane = lax.broadcasted_iota(jnp.int32, (width, LANES), 1)
    final = jnp.broadcast_to(points[:, length : length + 1], (width, LANES))
    previous = jnp.broadcast_to(points[:, length - 1 : length], (width, LANES))
    rows = jnp.where(lane == 0, final, previous).T
    row = jnp.concatenate([rows[0:1, :], rows[1:2, :]], axis=1)
    is_last = jnp.bitwise_xor(lax.axis_index("narrow"), mask) == lax.axis_size("narrow") - 1
    first = lax.broadcasted_iota(jnp.int32, (ENDS, LANES), 0) == 0
    return folded(crossed), jnp.where(jnp.logical_and(is_last, first), row, 0.0)


def own_kernel(targets, piece, path, second, ends, *refs):
    sums, (diff, lead, rest, lhs) = refs[: len(targets)], refs[len(targets) :]
    points, after = coefficients(piece, diff, lead, rest)
    path[...] = after.astype(BF16)
    second[...], ends[...] = besides(0, piece, points, after)
    for target, total in zip(targets, sums):
        total[...] = target_sum(target, piece, diff, lead, rest, lhs)


def mate_kernel(targets, piece, second, ends, *refs):
    count = len(targets)
    sums, (chip_second, chip_ends), messages, scratch = refs[:count], refs[count : count + 2], refs[count + 2 : -4], refs[-4:]
    diff, lead, rest, lhs = scratch
    points, after = coefficients(piece, diff, lead, rest)
    more_second, more_ends = besides(1, piece, points, after)
    both_second, both_ends = second[...] + more_second, ends[...] + more_ends
    chip_second[...] = both_second
    chip_ends[...] = both_ends
    for target, before, message in zip(targets, sums, messages):
        pack(message, before[...] + target_sum(target, piece, diff, lead, rest, lhs), both_second, both_ends)


def kept_kernel(piece, before, total, diff, lead, rest, lhs):
    coefficients(piece, diff, lead, rest)
    total[...] = before[...] + target_sum((0, 0), piece, diff, lead, rest, lhs)


def folded(crossed):
    width = crossed.shape[0]
    turned = crossed.T - crossed
    row = lax.broadcasted_iota(jnp.int32, (width // 2, width), 0)
    lane = lax.broadcasted_iota(jnp.int32, (width // 2, width), 1)
    corner = jnp.concatenate([turned[width // 2 :, width // 2 :], turned[width // 2 :, : width // 2]], axis=1)
    upper = jnp.where(lane > row, turned[: width // 2, :], jnp.where(lane < row, corner, 0.0))
    return jnp.concatenate([upper, upper], axis=1)


def unfolded(upper):
    size = upper.shape[0]
    row = lax.broadcasted_iota(jnp.int32, (size, size), 0)
    lane = lax.broadcasted_iota(jnp.int32, (size, size), 1)
    near, far = upper[:, :size], upper[:, size : 2 * size]
    above = jnp.where(lane > row, near, 0.0)
    below = jnp.where(lane < row, near, 0.0)
    return jnp.concatenate(
        [
            jnp.concatenate([above - above.T, far], axis=1),
            jnp.concatenate([-far.T, below - below.T], axis=1),
        ],
        axis=0,
    )


def pack(sent, total, doubled, ends=None):
    count, rows = total.shape[0], doubled.shape[0]
    high = doubled.astype(BF16).astype(F32)
    lane = lax.broadcasted_iota(jnp.int32, doubled.shape, 1)
    sent[:count, :] = total.astype(BF16)
    sent[count : count + rows, :] = jnp.where(lane < LANES // 2, high, doubled - high).astype(BF16)
    if ends is not None:
        sent[count + rows :, :] = ends.astype(BF16)


def unpack(received, count, rows):
    coded = received[count : count + rows, :].astype(F32)
    return received[:count, :].astype(F32), coded + pltpu.roll(coded, LANES // 2, 1)


def reduce_kernel(targets, kept, chip_second, chip_ends, *refs):
    parts, refs = refs[: len(targets)], refs[len(targets) :]
    own, other, own_second, other_second, pair, pair_second, ends, sent = refs
    count, rows = kept.shape[0], chip_second.shape[0]
    sums = [[kept[...], chip_second[...]], None]
    last = chip_ends[...]
    for (across, _), part in zip(targets, parts):
        more = unpack(part, count, rows)
        sums[across] = [a + b for a, b in zip(sums[across], more)] if sums[across] else more
        if not across:
            last = last + part[count + rows :, :].astype(F32)
    own[...], own_second[...] = sums[0]
    other[...], other_second[...] = sums[1]
    total, doubled = sums[0][0] + sums[1][0], sums[0][1] + sums[1][1]
    pair[...] = total
    pair_second[...] = doubled
    ends[...] = last
    pack(sent, total, doubled)


def ends_kernel(scale, ends, level_one, x_twice, pairs, factor):
    width = pairs.shape[0]
    x_row, a_row = ends[0:1, :width], ends[0:1, width:]
    x_across = jnp.broadcast_to(x_row, (width, width))
    a_across = jnp.broadcast_to(a_row, (width, width))
    x_down, a_down = x_across.T, a_across.T
    xx = x_down * x_across
    edge = a_down * x_across - a_down * a_across - 2.0 * x_down * a_across
    level_one[...] = scale * x_row
    x_twice[...] = jnp.concatenate([x_row, x_row], axis=1)
    pairs[:, :width] = 0.5 * xx
    factor[:, :width] = 0.5 * xx - edge / 6.0 - xx / 3.0


def is_later(distance):
    return jnp.bitwise_and(lax.axis_index("wide"), distance) != 0


def scan_kernel(distance, started, ended, *refs):
    before, refs = refs[: 2 * started], refs[2 * started :]
    group_third, group_second, received, third, second, sent = refs[:6]
    more_third, more_second = unpack(received, group_third.shape[0], group_second.shape[0])
    total, doubled = group_third[...] + more_third, group_second[...] + more_second
    pack(sent, total, doubled)
    earlier_third = jnp.where(is_later(distance), more_third, 0.0)
    earlier_second = jnp.where(is_later(distance), more_second, 0.0)
    if started:
        earlier_third, earlier_second = earlier_third + before[0][...], earlier_second + before[1][...]
    third[...] = earlier_third
    second[...] = earlier_second
    if not ended:
        refs[6][...] = total
        refs[7][...] = doubled


def return_kernel(distance, third, received, own, other, earlier, sent):
    count = third.shape[0]
    total = third[...] + jnp.where(is_later(distance), received[:count, :].astype(F32), 0.0)
    earlier[...] = total
    sent[...] = (total + other[...] + jnp.where(parity() == 0, own[...], 0.0)).astype(BF16)


def products(result, half, factor, x_twice, total=None):
    row_count, width = factor.shape
    lane = lax.broadcasted_iota(jnp.int32, (row_count, LANES), 1)
    factor = jnp.where(half == 0, factor[:, : width // 2], factor[:, width // 2 :])
    for at in range(width // 4):
        low = jnp.broadcast_to(factor[:, 2 * at : 2 * at + 1], (row_count, LANES))
        high = jnp.broadcast_to(factor[:, 2 * at + 1 : 2 * at + 2], (row_count, LANES))
        value = jnp.where(lane < width, low, high) * x_twice
        if total is not None:
            value = value - total[at * row_count : (at + 1) * row_count, :]
        result[:, at * LANES : (at + 1) * LANES] = value


def levels_kernel(
    scale, row_count, distance, second, received, own_second, other_second, earlier, own, other, x_twice, pairs, factor,
    level_two, partly, rest, held, own_half, sem,
):
    width = pairs.shape[0]
    count, rows = own.shape[0], second.shape[0]
    is_first = parity() == 0
    coded = jnp.where(is_later(distance), received[count : count + rows, :].astype(F32), 0.0)
    upper = second[...] + coded + pltpu.roll(coded, LANES // 2, 1)
    upper = upper + own_second[...] + jnp.where(is_first, 0.0, other_second[...])
    turned = 0.5 * unfolded(upper)
    held[:, :width] = scale**3 * (factor[:, :width] + turned)
    first_row = pl.multiple_of(lax.axis_index("narrow") * row_count, row_count)
    own_factor = held[pl.ds(first_row, row_count), :width]
    total = earlier[...] + own[...] + jnp.where(is_first, 0.0, other[...])
    products(own_half, parity(), own_factor, x_twice[...], total * (scale**3 / 6.0))
    size = own_half.shape[1]
    at = pl.multiple_of(parity() * size, size)
    copy = pltpu.make_async_copy(own_half, partly.at[:, pl.ds(at, size)], sem)
    copy.start()
    products(rest, 1 - parity(), own_factor, x_twice[...])
    held[:, :width] = scale**2 * (pairs[:, :width] + turned)
    level_two[:, :width] = held[pl.ds(0, width // 2, stride=2), :width]
    level_two[:, width:] = held[pl.ds(1, width // 2, stride=2), :width]
    copy.wait()


def finish_kernel(scale, row_count, received, rest, partly, level_three, other_half, sem):
    size = rest.shape[1]
    for at in range(size // LANES):
        lanes = slice(at * LANES, (at + 1) * LANES)
        come = received[at * row_count : (at + 1) * row_count, :].astype(F32)
        other_half[:, lanes] = rest[:, lanes] - come * (scale**3 / 6.0)
    at = pl.multiple_of((1 - parity()) * size, size)
    copy = pltpu.make_async_copy(other_half, level_three.at[:, pl.ds(at, size)], sem)
    copy.start()
    copy.wait()


VMEM = pl.BlockSpec(memory_space=pltpu.VMEM)
HBM = pl.BlockSpec(memory_space=pltpu.HBM)


def call(kernel, name, out_shape, scratch=(), in_specs=None, out_specs=None, aliases=None, flops=0, moved=0):
    shapes = [jax.ShapeDtypeStruct(dims, dtype) for dims, dtype in out_shape]

    def run(*operands):
        return pl.pallas_call(
            kernel,
            out_shape=tuple(shapes),
            in_specs=in_specs or [VMEM] * len(operands),
            out_specs=out_specs or (VMEM,) * len(shapes),
            input_output_aliases=aliases or {},
            scratch_shapes=list(scratch),
            compiler_params=pltpu.CompilerParams(vmem_limit_bytes=32 * 2**20),
            cost_estimate=pl.CostEstimate(flops=flops, bytes_accessed=moved, transcendentals=0),
            name=name,
        )(*operands)

    return run


def path_of(recording, conv_weight, conv_bias, projection):
    length, channels = recording.shape
    layers, taps = conv_weight.shape[:2]
    width = projection.shape[1]
    rows = length + 2 * HALO
    edges = edges_exchanged(recording)
    buffer = ((rows + 16, channels), F32)
    far = (recording, conv_weight, conv_bias, projection.T)
    far = [pltpu.with_memory_space_constraint(held, pltpu.HBM) for held in far]
    padded, *near = call(
        load_kernel,
        "load",
        [buffer, ((layers - 1,) + conv_weight.shape[1:], BF16), (conv_bias.shape, F32), ((width, channels), BF16)],
        scratch=[pltpu.VMEM(recording.shape, BF16), pltpu.SemaphoreType.DMA((4,))],
        in_specs=[HBM] * len(far),
        flops=10**9,
        moved=2 * sum(held.size for held in far),
    )(*far)
    piece, _ = call(
        functools.partial(conv_kernel, 3 * LANES),
        "conv",
        [((width, length + LANES), BF16), buffer],
        scratch=[
            pltpu.VMEM(buffer[0], F32),
            pltpu.VMEM(conv_weight.shape[1:], BF16),
            pltpu.VMEM((width, length + LANES), F32),
            pltpu.SemaphoreType.DMA,
        ],
        in_specs=[VMEM] * 5 + [HBM] + [VMEM] * 2,
        aliases={0: 1},
        flops=2 * layers * taps * length * channels**2,
        moved=2 * conv_weight.size,
    )(padded, *edges, near[0], far[1], near[1], near[2])
    return piece


def per_device(recording, conv_weight, conv_bias, projection):
    length = recording.shape[0]
    width = projection.shape[1]
    wide_size, narrow_size = lax.axis_size("wide"), lax.axis_size("narrow")
    scale = float(length * wide_size * narrow_size) ** -0.2
    row_count = width // narrow_size
    count = width // 4 * row_count
    piece = path_of(recording, conv_weight, conv_bias, projection)

    half, square, folds = ((count, LANES), F32), ((width, LANES), F32), ((width // 2, LANES), F32)
    last = ((ENDS, LANES), F32)
    message = ((count + width // 2, LANES), BF16)
    scratch = [pltpu.VMEM((width, length), F32)] * 3 + [pltpu.VMEM((2, count, length), BF16)]
    share = 10**9 // 2

    mate = exchanged(piece, "narrow", 1)
    targets = [(across, mask) for across in (1, 0) for mask in range(narrow_size - 2, -1, -2)][:-1]
    points, chip_second, chip_ends, own, *sums = call(
        functools.partial(own_kernel, [(0, 0)] + targets),
        "own",
        [((width, length), BF16), folds, last] + [half] * (1 + len(targets)),
        scratch=scratch,
        flops=share * (1 + len(targets)),
    )(piece)
    chip_second, chip_ends, *messages = call(
        functools.partial(mate_kernel, targets),
        "mate",
        [folds, last] + [((count + width // 2 + ENDS, LANES), BF16)] * len(targets),
        scratch=scratch,
        flops=share * len(targets),
    )(mate, chip_second, chip_ends, *sums)
    size = wide_size * narrow_size
    parts = []
    for (across, mask), sent in zip(targets, messages):
        flip = across * narrow_size + mask
        parts.append(lax.ppermute(sent, WHOLE, [(i, i ^ flip) for i in range(size)]))
    (kept,) = call(kept_kernel, "kept", [half], scratch=scratch, flops=share)(mate, own)
    own, other, own_second, other_second, group_third, group_second, ends, sent = call(
        functools.partial(reduce_kernel, targets),
        "reduce",
        [half, half, folds, folds, half, folds, last, message],
    )(kept, chip_second, chip_ends, *parts)
    level_one, x_twice, pairs, factor = call(
        functools.partial(ends_kernel, scale),
        "ends",
        [((1, width), F32), ((1, LANES), F32), square, square],
        flops=share,
    )(ends)

    earlier = ()
    distance = 2
    received = exchanged(sent, "wide", distance)
    while 2 * distance < wide_size:
        ended = 4 * distance >= wide_size
        *earlier, sent = call(
            functools.partial(scan_kernel, distance, len(earlier) > 0, ended),
            "scan",
            [half, folds, message] + ([] if ended else [half, folds]),
        )(*earlier, group_third, group_second, received)
        if not ended:
            sent, group_third, group_second = earlier[2], earlier[3], sent
            earlier = earlier[:2]
        distance *= 2
        received = exchanged(sent, "wide", distance)
    if not earlier:
        earlier = [jnp.zeros(dims, dtype) for dims, dtype in (half, folds)]
    total, sent = call(functools.partial(return_kernel, distance), "back", [half, ((count, LANES), BF16)])(
        earlier[0], received, own, other
    )
    returned = exchanged(sent, "wide", 1)
    own_size = width * width // 2
    third_shape = ((row_count, 2 * own_size), F32)
    half_buffer = ((row_count, own_size), F32)
    level_two, partly, rest = call(
        functools.partial(levels_kernel, scale, row_count, distance),
        "levels",
        [folds, third_shape, half_buffer],
        scratch=[pltpu.VMEM((width, LANES), F32), pltpu.VMEM(half_buffer[0], F32), pltpu.SemaphoreType.DMA],
        out_specs=(VMEM, HBM, VMEM),
        flops=10**9,
    )(earlier[1], received, own_second, other_second, total, own, other, x_twice, pairs, factor)
    (level_three,) = call(
        functools.partial(finish_kernel, scale, row_count),
        "finish",
        [third_shape],
        scratch=[pltpu.VMEM(half_buffer[0], F32), pltpu.SemaphoreType.DMA],
        in_specs=[VMEM, VMEM, HBM],
        out_specs=(HBM,),
        aliases={2: 0},
    )(returned, rest, partly)
    return points.T, level_one, level_two.reshape(1, width * width), level_three[None]


def solution(mesh):
    return jax.shard_map(
        per_device,
        mesh=mesh,
        in_specs=(P(WHOLE, None), P(), P(), P()),
        out_specs=(P(WHOLE, None), P("wide", None), P("wide", None), P("wide", "narrow", None)),
        check_vma=False,
    )
```

```python
import functools

import jax
import jax.numpy as jnp
from jax import lax
from jax.experimental import pallas as pl
from jax.experimental.pallas import tpu as pltpu
from jax.sharding import PartitionSpec as P

HALO = 16
ENDS = 16
LANES = 128
F32 = jnp.float32
BF16 = jnp.bfloat16
NT = (((1,), (1,)), ((), ()))
WHOLE = ("wide", "narrow")


def exchanged(array, axis, distance):
    size = lax.axis_size(axis)
    return lax.ppermute(array, axis, [(i, i ^ distance) for i in range(size)])


def edges_kernel(rec, outer, inner, sems):
    far = rec.shape[0] - HALO
    at = lax.rem(lax.axis_index("narrow"), 2) * far
    copies = [
        pltpu.make_async_copy(rec.at[pl.ds(pl.multiple_of(start, HALO), HALO), :], rows, sems.at[i])
        for i, (start, rows) in enumerate(((at, outer), (far - at, inner)))
    ]
    for copy in copies:
        copy.start()
    for copy in copies:
        copy.wait()


def again_kernel(outer, inner, outer_again, inner_again):
    outer_again[...] = outer[...]
    inner_again[...] = inner[...]


def edges_exchanged(recording):
    rows = ((HALO, recording.shape[1]), recording.dtype)
    source = pltpu.with_memory_space_constraint(recording, pltpu.HBM)
    outer, inner = call(
        edges_kernel, "edges", [rows, rows], scratch=[pltpu.SemaphoreType.DMA((2,))], in_specs=[HBM]
    )(source)
    again, inner = call(again_kernel, "again", [rows, rows])(outer, inner)
    wide_size, narrow_size = lax.axis_size("wide"), lax.axis_size("narrow")
    size = wide_size * narrow_size
    inside = {i: (i - 1 + 2 * (i % 2)) % narrow_size for i in range(narrow_size)}
    over = {i: (i - 1 + 2 * (i % 2)) % size for i in range(size)}
    if narrow_size > 2:
        end = size - 1
        over.update({0: 1, 1: 2, 2: 0, end: end - 1, end - 1: end - 2, end - 2: end})
    over = lax.ppermute(outer, WHOLE, list(over.items()))
    inside = lax.ppermute(again, "narrow", list(inside.items()))
    return over, inside, exchanged(inner, "narrow", 1)


def load_kernel(rec_hbm, weights_hbm, bias_hbm, proj_hbm, padded, weights, bias, proj, rec, sems):
    early = weights.shape[0]
    pairs = ((rec_hbm, rec), (weights_hbm.at[:early], weights), (bias_hbm, bias), (proj_hbm, proj))
    copies = [pltpu.make_async_copy(*pair, sems.at[i]) for i, pair in enumerate(pairs)]
    for copy in copies:
        copy.start()
    copies[0].wait()
    padded[: 8 + HALO, :] = jnp.zeros((8 + HALO, rec.shape[1]), F32)
    padded[8 + HALO : 8 + HALO + rec.shape[0], :] = rec[...].astype(F32)
    padded[8 + HALO + rec.shape[0] :, :] = jnp.zeros((8 + HALO, rec.shape[1]), F32)
    for copy in copies[1:]:
        copy.wait()


def conv_kernel(chunk, _, over, inside, inner, weights, weights_hbm, bias, proj, piece, padded, even, last_weights, path, sem):
    layers = 1 + weights.shape[0]
    rows = padded.shape[0] - 16
    length = rows - 2 * HALO
    far = HALO + length
    copy = pltpu.make_async_copy(weights_hbm.at[layers - 1], last_weights, sem)
    copy.start()
    narrow = lax.axis_index("narrow")
    place = lax.axis_index("wide") * lax.axis_size("narrow") + narrow
    is_first = place == 0
    is_last = place == lax.axis_size("wide") * lax.axis_size("narrow") - 1
    is_odd = lax.rem(narrow, 2) == 1
    width, full = path.shape
    path[:, full - LANES :] = jnp.zeros((width, LANES), F32)
    at_end = jnp.logical_or(is_first, is_last)
    at_edge = jnp.logical_or(narrow == 0, narrow == lax.axis_size("narrow") - 1)
    beyond = jnp.where(at_edge, over[...].astype(F32), inside[...].astype(F32))
    beyond = jnp.where(at_end, 0.0, beyond)
    within = inner[...].astype(F32)
    padded[8 : 8 + HALO, :] = jnp.where(is_odd, within, beyond)
    padded[8 + far : 8 + rows, :] = jnp.where(is_odd, beyond, within)
    source, target = padded, even
    for layer in range(layers):
        if layer == layers - 1:
            copy.wait()
        reach = 2**layer
        for start in range(0, rows, chunk):
            size = min(chunk, rows - start)
            windows = [
                source[8 + start + k * reach : 8 + start + k * reach + size, :] for k in (-1, 0, 1)
            ]
            conv = bias[layer : layer + 1, :]
            for tap, window in enumerate(windows):
                tap_weights = last_weights[tap] if layer == layers - 1 else weights[layer, tap]
                conv = conv + jnp.dot(window.astype(BF16), tap_weights, preferred_element_type=F32)
            half = 0.5 * conv
            hidden = (windows[1] + (half + half * jnp.tanh(half))).astype(BF16)
            if layer < layers - 1:
                target[8 + start : 8 + start + size, :] = hidden.astype(F32)
            else:
                part = lax.dot_general(hidden, proj[...], NT, preferred_element_type=F32)
                path[:, start : start + size] = part.astype(BF16).astype(F32).T
        if layer < layers - 1:
            target[8 : 8 + HALO, :] = jnp.where(is_first, 0.0, target[8 : 8 + HALO, :])
            target[8 + far : 8 + rows, :] = jnp.where(is_last, 0.0, target[8 + far : 8 + rows, :])
        source, target = target, source
    lane = lax.broadcasted_iota(jnp.int32, (width, LANES), 1)
    path[:, :LANES] = jnp.where(jnp.logical_and(is_first, lane < HALO), 0.0, path[:, :LANES])
    piece[...] = pltpu.roll(path[...], full - HALO + 1, 1).astype(BF16)


def coefficients(piece, diff, lead, rest):
    padded = piece.shape[1]
    length = padded - LANES
    points = piece[...].astype(F32)
    after = pltpu.roll(points, padded - 1, 1)[:, :length]
    before = pltpu.roll(points, 1, 1)[:, :length]
    here = points[:, :length]
    middle = 0.5 * (after + before)
    diff[...] = after - before
    lead[...] = 2.0 * here + middle
    rest[...] = middle - here
    return points, after


def half_sum(owner, half, piece, diff, lead, rest, lhs):
    width, padded = piece.shape
    length = padded - LANES
    row_count = 4 * lhs.shape[1] // width
    first_row = pl.multiple_of(owner * row_count, row_count)
    group = max(1, 16 // row_count)
    span = 2 * LANES
    sums = []
    for h in range(2):
        for lanes in [slice(at, at + span) for at in range(0, length, span)]:
            own_lead = lead[pl.ds(first_row, row_count), lanes]
            own_diff = diff[pl.ds(first_row, row_count), lanes]
            for at in range(0, width // 4, group):
                terms = []
                for g in range(group):
                    row = pl.ds(half * (width // 2) + 2 * (at + g) + h, 1)
                    terms.append(diff[row, lanes] * own_lead + rest[row, lanes] * own_diff)
                term = terms[0] if group == 1 else jnp.concatenate(terms, axis=0)
                lhs[h, at * row_count : (at + group) * row_count, lanes] = term.astype(BF16)
        sums.append(lax.dot_general(lhs[h], piece[:, :length], NT, preferred_element_type=F32))
    return jnp.concatenate(sums, axis=1)


def parity():
    return lax.rem(lax.axis_index("wide"), 2)


def target_sum(target, *refs):
    across, mask = target
    owner = jnp.bitwise_xor(lax.axis_index("narrow"), mask)
    return half_sum(owner, 1 - parity() if across else parity(), *refs)


def besides(mask, piece, points, after):
    width, padded = piece.shape
    length = padded - LANES
    crossed = lax.dot_general(after.astype(BF16), piece[:, :length], NT, preferred_element_type=F32)
    lane = lax.broadcasted_iota(jnp.int32, (width, LANES), 1)
    final = jnp.broadcast_to(points[:, length : length + 1], (width, LANES))
    previous = jnp.broadcast_to(points[:, length - 1 : length], (width, LANES))
    rows = jnp.where(lane == 0, final, previous).T
    row = jnp.concatenate([rows[0:1, :], rows[1:2, :]], axis=1)
    is_last = jnp.bitwise_xor(lax.axis_index("narrow"), mask) == lax.axis_size("narrow") - 1
    first = lax.broadcasted_iota(jnp.int32, (ENDS, LANES), 0) == 0
    return folded(crossed), jnp.where(jnp.logical_and(is_last, first), row, 0.0)


def own_kernel(targets, piece, second, ends, *refs):
    sums, (diff, lead, rest, lhs) = refs[: len(targets)], refs[len(targets) :]
    points, after = coefficients(piece, diff, lead, rest)
    second[...], ends[...] = besides(0, piece, points, after)
    for target, total in zip(targets, sums):
        total[...] = target_sum(target, piece, diff, lead, rest, lhs)


def mate_kernel(targets, piece, second, ends, *refs):
    count = len(targets)
    sums, (chip_second, chip_ends), messages, scratch = refs[:count], refs[count : count + 2], refs[count + 2 : -4], refs[-4:]
    diff, lead, rest, lhs = scratch
    points, after = coefficients(piece, diff, lead, rest)
    more_second, more_ends = besides(1, piece, points, after)
    both_second, both_ends = second[...] + more_second, ends[...] + more_ends
    chip_second[...] = both_second
    chip_ends[...] = both_ends
    for target, before, message in zip(targets, sums, messages):
        pack(message, before[...] + target_sum(target, piece, diff, lead, rest, lhs), both_second, both_ends)


def kept_kernel(piece, mate, total, path, diff, lead, rest, lhs):
    _, after = coefficients(piece, diff, lead, rest)
    path[...] = after.astype(BF16)
    first = target_sum((0, 0), piece, diff, lead, rest, lhs)
    coefficients(mate, diff, lead, rest)
    total[...] = first + target_sum((0, 0), mate, diff, lead, rest, lhs)


def folded(crossed):
    width = crossed.shape[0]
    turned = crossed.T - crossed
    row = lax.broadcasted_iota(jnp.int32, (width // 2, width), 0)
    lane = lax.broadcasted_iota(jnp.int32, (width // 2, width), 1)
    corner = jnp.concatenate([turned[width // 2 :, width // 2 :], turned[width // 2 :, : width // 2]], axis=1)
    upper = jnp.where(lane > row, turned[: width // 2, :], jnp.where(lane < row, corner, 0.0))
    return jnp.concatenate([upper, upper], axis=1)


def unfolded(upper):
    size = upper.shape[0]
    row = lax.broadcasted_iota(jnp.int32, (size, size), 0)
    lane = lax.broadcasted_iota(jnp.int32, (size, size), 1)
    near, far = upper[:, :size], upper[:, size : 2 * size]
    above = jnp.where(lane > row, near, 0.0)
    below = jnp.where(lane < row, near, 0.0)
    return jnp.concatenate(
        [
            jnp.concatenate([above - above.T, far], axis=1),
            jnp.concatenate([-far.T, below - below.T], axis=1),
        ],
        axis=0,
    )


def pack(sent, total, doubled, ends=None):
    count, rows = total.shape[0], doubled.shape[0]
    high = doubled.astype(BF16).astype(F32)
    lane = lax.broadcasted_iota(jnp.int32, doubled.shape, 1)
    sent[:count, :] = total.astype(BF16)
    sent[count : count + rows, :] = jnp.where(lane < LANES // 2, high, doubled - high).astype(BF16)
    if ends is not None:
        sent[count + rows :, :] = ends.astype(BF16)


def unpack(received, count, rows):
    coded = received[count : count + rows, :].astype(F32)
    return received[:count, :].astype(F32), coded + pltpu.roll(coded, LANES // 2, 1)


def reduce_kernel(targets, kept, chip_second, chip_ends, *refs):
    parts, refs = refs[: len(targets)], refs[len(targets) :]
    own, other, own_second, other_second, ends, sent = refs
    count, rows = kept.shape[0], chip_second.shape[0]
    sums = [[kept[...], chip_second[...]], None]
    last = chip_ends[...]
    for (across, _), part in zip(targets, parts):
        more = unpack(part, count, rows)
        sums[across] = [a + b for a, b in zip(sums[across], more)] if sums[across] else more
        if not across:
            last = last + part[count + rows :, :].astype(F32)
    own[...], own_second[...] = sums[0]
    other[...], other_second[...] = sums[1]
    total, doubled = sums[0][0] + sums[1][0], sums[0][1] + sums[1][1]
    ends[...] = last
    pack(sent, total, doubled)


def ends_kernel(scale, ends, level_one, x_twice, pairs, factor):
    width = pairs.shape[0]
    x_row, a_row = ends[0:1, :width], ends[0:1, width:]
    x_across = jnp.broadcast_to(x_row, (width, width))
    a_across = jnp.broadcast_to(a_row, (width, width))
    x_down, a_down = x_across.T, a_across.T
    xx = x_down * x_across
    edge = a_down * x_across - a_down * a_across - 2.0 * x_down * a_across
    level_one[...] = scale * x_row
    x_twice[...] = jnp.concatenate([x_row, x_row], axis=1)
    pairs[:, :width] = 0.5 * xx
    factor[:, :width] = 0.5 * xx - edge / 6.0 - xx / 3.0


def earlier_sum(flips, refs, start, size):
    me = lax.axis_index("wide")
    total = jnp.zeros((size, LANES), F32)
    for flip, ref in zip(flips, refs):
        come = ref[start : start + size, :].astype(F32)
        total = total + jnp.where(jnp.bitwise_xor(me, flip) < me, come, 0.0)
    return total


def return_kernel(flips, own, other, *refs):
    received, (earlier, sent) = refs[:-2], refs[-2:]
    total = earlier_sum(flips, received, 0, own.shape[0])
    earlier[...] = total
    sent[...] = (total + other[...] + jnp.where(parity() == 0, own[...], 0.0)).astype(BF16)


def products(result, half, factor, x_twice, total=None):
    row_count, width = factor.shape
    lane = lax.broadcasted_iota(jnp.int32, (row_count, LANES), 1)
    factor = jnp.where(half == 0, factor[:, : width // 2], factor[:, width // 2 :])
    for at in range(width // 4):
        low = jnp.broadcast_to(factor[:, 2 * at : 2 * at + 1], (row_count, LANES))
        high = jnp.broadcast_to(factor[:, 2 * at + 1 : 2 * at + 2], (row_count, LANES))
        value = jnp.where(lane < width, low, high) * x_twice
        if total is not None:
            value = value - total[at * row_count : (at + 1) * row_count, :]
        result[:, at * LANES : (at + 1) * LANES] = value


def levels_kernel(scale, row_count, flips, own_second, other_second, earlier, own, other, x_twice, pairs, factor, *refs):
    received, (level_two, partly, rest, held, own_half, sem) = refs[: len(flips)], refs[len(flips) :]
    width = pairs.shape[0]
    is_first = parity() == 0
    coded = earlier_sum(flips, received, own.shape[0], own_second.shape[0])
    upper = coded + pltpu.roll(coded, LANES // 2, 1)
    upper = upper + own_second[...] + jnp.where(is_first, 0.0, other_second[...])
    turned = 0.5 * unfolded(upper)
    held[:, :width] = scale**3 * (factor[:, :width] + turned)
    first_row = pl.multiple_of(lax.axis_index("narrow") * row_count, row_count)
    own_factor = held[pl.ds(first_row, row_count), :width]
    total = earlier[...] + own[...] + jnp.where(is_first, 0.0, other[...])
    products(own_half, parity(), own_factor, x_twice[...], total * (scale**3 / 6.0))
    size = own_half.shape[1]
    at = pl.multiple_of(parity() * size, size)
    copy = pltpu.make_async_copy(own_half, partly.at[:, pl.ds(at, size)], sem)
    copy.start()
    products(rest, 1 - parity(), own_factor, x_twice[...])
    held[:, :width] = scale**2 * (pairs[:, :width] + turned)
    level_two[:, :width] = held[pl.ds(0, width // 2, stride=2), :width]
    level_two[:, width:] = held[pl.ds(1, width // 2, stride=2), :width]
    copy.wait()


def finish_kernel(scale, row_count, received, rest, partly, level_three, other_half, sem):
    size = rest.shape[1]
    for at in range(size // LANES):
        lanes = slice(at * LANES, (at + 1) * LANES)
        come = received[at * row_count : (at + 1) * row_count, :].astype(F32)
        other_half[:, lanes] = rest[:, lanes] - come * (scale**3 / 6.0)
    at = pl.multiple_of((1 - parity()) * size, size)
    copy = pltpu.make_async_copy(other_half, level_three.at[:, pl.ds(at, size)], sem)
    copy.start()
    copy.wait()


VMEM = pl.BlockSpec(memory_space=pltpu.VMEM)
HBM = pl.BlockSpec(memory_space=pltpu.HBM)


def call(kernel, name, out_shape, scratch=(), in_specs=None, out_specs=None, aliases=None, flops=0, moved=0):
    shapes = [jax.ShapeDtypeStruct(dims, dtype) for dims, dtype in out_shape]

    def run(*operands):
        return pl.pallas_call(
            kernel,
            out_shape=tuple(shapes),
            in_specs=in_specs or [VMEM] * len(operands),
            out_specs=out_specs or (VMEM,) * len(shapes),
            input_output_aliases=aliases or {},
            scratch_shapes=list(scratch),
            compiler_params=pltpu.CompilerParams(vmem_limit_bytes=32 * 2**20),
            cost_estimate=pl.CostEstimate(flops=flops, bytes_accessed=moved, transcendentals=0),
            name=name,
        )(*operands)

    return run


def path_of(recording, conv_weight, conv_bias, projection):
    length, channels = recording.shape
    layers, taps = conv_weight.shape[:2]
    width = projection.shape[1]
    rows = length + 2 * HALO
    edges = edges_exchanged(recording)
    buffer = ((rows + 16, channels), F32)
    far = (recording, conv_weight, conv_bias, projection.T)
    far = [pltpu.with_memory_space_constraint(held, pltpu.HBM) for held in far]
    padded, *near = call(
        load_kernel,
        "load",
        [buffer, ((layers - 1,) + conv_weight.shape[1:], BF16), (conv_bias.shape, F32), ((width, channels), BF16)],
        scratch=[pltpu.VMEM(recording.shape, BF16), pltpu.SemaphoreType.DMA((4,))],
        in_specs=[HBM] * len(far),
        flops=10**9,
        moved=2 * sum(held.size for held in far),
    )(*far)
    piece, _ = call(
        functools.partial(conv_kernel, 3 * LANES),
        "conv",
        [((width, length + LANES), BF16), buffer],
        scratch=[
            pltpu.VMEM(buffer[0], F32),
            pltpu.VMEM(conv_weight.shape[1:], BF16),
            pltpu.VMEM((width, length + LANES), F32),
            pltpu.SemaphoreType.DMA,
        ],
        in_specs=[VMEM] * 5 + [HBM] + [VMEM] * 2,
        aliases={0: 1},
        flops=2 * layers * taps * length * channels**2,
        moved=2 * conv_weight.size,
    )(padded, *edges, near[0], far[1], near[1], near[2])
    return piece


def per_device(recording, conv_weight, conv_bias, projection):
    length = recording.shape[0]
    width = projection.shape[1]
    wide_size, narrow_size = lax.axis_size("wide"), lax.axis_size("narrow")
    scale = float(length * wide_size * narrow_size) ** -0.2
    row_count = width // narrow_size
    count = width // 4 * row_count
    piece = path_of(recording, conv_weight, conv_bias, projection)

    half, square, folds = ((count, LANES), F32), ((width, LANES), F32), ((width // 2, LANES), F32)
    last = ((ENDS, LANES), F32)
    message = ((count + width // 2, LANES), BF16)
    scratch = [pltpu.VMEM((width, length), F32)] * 3 + [pltpu.VMEM((2, count, length), BF16)]
    share = 10**9 // 2

    mate = exchanged(piece, "narrow", 1)
    targets = [(across, mask) for across in (1, 0) for mask in range(narrow_size - 2, -1, -2)][:-1]
    second, ends, *sums = call(
        functools.partial(own_kernel, targets),
        "own",
        [folds, last] + [half] * len(targets),
        scratch=scratch,
        flops=share * len(targets),
    )(piece)
    chip_second, chip_ends, *messages = call(
        functools.partial(mate_kernel, targets),
        "mate",
        [folds, last] + [((count + width // 2 + ENDS, LANES), BF16)] * len(targets),
        scratch=scratch,
        flops=share * len(targets),
    )(mate, second, ends, *sums)
    size = wide_size * narrow_size
    parts = []
    for (across, mask), sent in zip(targets, messages):
        flip = across * narrow_size + mask
        parts.append(lax.ppermute(sent, WHOLE, [(i, i ^ flip) for i in range(size)]))
    kept, points = call(
        kept_kernel, "kept", [half, ((width, length), BF16)], scratch=scratch, flops=2 * share
    )(piece, mate)
    own, other, own_second, other_second, ends, sent = call(
        functools.partial(reduce_kernel, targets),
        "reduce",
        [half, half, folds, folds, last, message],
    )(kept, chip_second, chip_ends, *parts)
    level_one, x_twice, pairs, factor = call(
        functools.partial(ends_kernel, scale),
        "ends",
        [((1, width), F32), ((1, LANES), F32), square, square],
        flops=share,
    )(ends)

    flips = [flip for flip in range(2, wide_size, 2) if flip != wide_size // 2] + [wide_size // 2]
    received = [exchanged(sent, "wide", flip) for flip in flips]
    total, sent = call(functools.partial(return_kernel, flips), "back", [half, ((count, LANES), BF16)])(
        own, other, *received
    )
    returned = exchanged(sent, "wide", 1)
    own_size = width * width // 2
    third_shape = ((row_count, 2 * own_size), F32)
    half_buffer = ((row_count, own_size), F32)
    level_two, partly, rest = call(
        functools.partial(levels_kernel, scale, row_count, flips),
        "levels",
        [folds, third_shape, half_buffer],
        scratch=[pltpu.VMEM((width, LANES), F32), pltpu.VMEM(half_buffer[0], F32), pltpu.SemaphoreType.DMA],
        out_specs=(VMEM, HBM, VMEM),
        flops=10**9,
    )(own_second, other_second, total, own, other, x_twice, pairs, factor, *received)
    (level_three,) = call(
        functools.partial(finish_kernel, scale, row_count),
        "finish",
        [third_shape],
        scratch=[pltpu.VMEM(half_buffer[0], F32), pltpu.SemaphoreType.DMA],
        in_specs=[VMEM, VMEM, HBM],
        out_specs=(HBM,),
        aliases={2: 0},
    )(returned, rest, partly)
    return points.T, level_one, level_two.reshape(1, width * width), level_three[None]


def solution(mesh):
    return jax.shard_map(
        per_device,
        mesh=mesh,
        in_specs=(P(WHOLE, None), P(), P(), P()),
        out_specs=(P(WHOLE, None), P("wide", None), P("wide", None), P("wide", "narrow", None)),
        check_vma=False,
    )
```

```python
import functools

import jax
import jax.numpy as jnp
from jax import lax
from jax.experimental import pallas as pl
from jax.experimental.pallas import tpu as pltpu
from jax.sharding import PartitionSpec as P

HALO = 16
ENDS = 16
LANES = 128
F32 = jnp.float32
BF16 = jnp.bfloat16
NT = (((1,), (1,)), ((), ()))
WHOLE = ("wide", "narrow")


def exchanged(array, axis, distance):
    size = lax.axis_size(axis)
    return lax.ppermute(array, axis, [(i, i ^ distance) for i in range(size)])


def edges_kernel(rec, outer, inner, sems):
    far = rec.shape[0] - HALO
    at = lax.rem(lax.axis_index("narrow"), 2) * far
    copies = [
        pltpu.make_async_copy(rec.at[pl.ds(pl.multiple_of(start, HALO), HALO), :], rows, sems.at[i])
        for i, (start, rows) in enumerate(((at, outer), (far - at, inner)))
    ]
    for copy in copies:
        copy.start()
    for copy in copies:
        copy.wait()


def again_kernel(outer, inner, outer_again, inner_again):
    outer_again[...] = outer[...]
    inner_again[...] = inner[...]


def edges_exchanged(recording):
    rows = ((HALO, recording.shape[1]), recording.dtype)
    source = pltpu.with_memory_space_constraint(recording, pltpu.HBM)
    outer, inner = call(
        edges_kernel, "edges", [rows, rows], scratch=[pltpu.SemaphoreType.DMA((2,))], in_specs=[HBM]
    )(source)
    again, inner = call(again_kernel, "again", [rows, rows])(outer, inner)
    wide_size, narrow_size = lax.axis_size("wide"), lax.axis_size("narrow")
    size = wide_size * narrow_size
    inside = {i: (i - 1 + 2 * (i % 2)) % narrow_size for i in range(narrow_size)}
    over = {i: (i - 1 + 2 * (i % 2)) % size for i in range(size)}
    if narrow_size > 2:
        end = size - 1
        over.update({0: 1, 1: 2, 2: 0, end: end - 1, end - 1: end - 2, end - 2: end})
    over = lax.ppermute(outer, WHOLE, list(over.items()))
    inside = lax.ppermute(again, "narrow", list(inside.items()))
    return over, inside, exchanged(inner, "narrow", 1)


def layer_rows(source, weights, bias, reach, start, size):
    windows = [source[8 + start + k * reach : 8 + start + k * reach + size, :] for k in (-1, 0, 1)]
    conv = bias
    for tap, window in enumerate(windows):
        conv = conv + jnp.dot(window.astype(BF16), weights[tap], preferred_element_type=F32)
    half = 0.5 * conv
    return (windows[1] + (half + half * jnp.tanh(half))).astype(BF16)


def load_kernel(middle, rec_hbm, weights_hbm, bias_hbm, proj_hbm, padded, hidden, weights, bias, proj, rec, sems):
    pairs = [(rec_hbm, rec), (bias_hbm, bias), (proj_hbm, proj)]
    pairs += [(weights_hbm.at[layer], weights.at[layer]) for layer in range(weights.shape[0])]
    copies = [pltpu.make_async_copy(*pair, sems.at[i]) for i, pair in enumerate(pairs)]
    for copy in copies[:4]:
        copy.start()
    copies[0].wait()
    for copy in copies[4:]:
        copy.start()
    padded[: 8 + HALO, :] = jnp.zeros((8 + HALO, rec.shape[1]), F32)
    padded[8 + HALO : 8 + HALO + rec.shape[0], :] = rec[...].astype(F32)
    padded[8 + HALO + rec.shape[0] :, :] = jnp.zeros((8 + HALO, rec.shape[1]), F32)
    for copy in copies[1:4]:
        copy.wait()
    for start, size in middle:
        rows = layer_rows(padded, weights.at[0], bias[0:1, :], 1, start, size)
        hidden[8 + start : 8 + start + size, :] = rows.astype(F32)
    for copy in copies[4:]:
        copy.wait()


def conv_kernel(
    chunks, _, __, over, inside, inner, weights, weights_hbm, bias, proj, piece, padded, even, last_weights, path, sem
):
    layers = 1 + weights.shape[0]
    rows = padded.shape[0] - 16
    length = rows - 2 * HALO
    far = HALO + length
    copy = pltpu.make_async_copy(weights_hbm.at[layers - 1], last_weights, sem)
    copy.start()
    narrow = lax.axis_index("narrow")
    place = lax.axis_index("wide") * lax.axis_size("narrow") + narrow
    is_first = place == 0
    is_last = place == lax.axis_size("wide") * lax.axis_size("narrow") - 1
    is_odd = lax.rem(narrow, 2) == 1
    width, full = path.shape
    path[:, full - LANES :] = jnp.zeros((width, LANES), F32)
    at_end = jnp.logical_or(is_first, is_last)
    at_edge = jnp.logical_or(narrow == 0, narrow == lax.axis_size("narrow") - 1)
    beyond = jnp.where(at_edge, over[...].astype(F32), inside[...].astype(F32))
    beyond = jnp.where(at_end, 0.0, beyond)
    within = inner[...].astype(F32)
    padded[8 : 8 + HALO, :] = jnp.where(is_odd, within, beyond)
    padded[8 + far : 8 + rows, :] = jnp.where(is_odd, beyond, within)
    source, target = padded, even
    for layer in range(layers):
        if layer == layers - 1:
            copy.wait()
        reach = 2**layer
        for start, size in chunks[layer]:
            layer_weights = last_weights if layer == layers - 1 else weights.at[layer]
            hidden = layer_rows(source, layer_weights, bias[layer : layer + 1, :], reach, start, size)
            if layer < layers - 1:
                target[8 + start : 8 + start + size, :] = hidden.astype(F32)
            else:
                part = lax.dot_general(hidden, proj[...], NT, preferred_element_type=F32)
                path[:, start : start + size] = part.astype(BF16).astype(F32).T
        if layer < layers - 1:
            target[8 : 8 + HALO, :] = jnp.where(is_first, 0.0, target[8 : 8 + HALO, :])
            target[8 + far : 8 + rows, :] = jnp.where(is_last, 0.0, target[8 + far : 8 + rows, :])
        source, target = target, source
    lane = lax.broadcasted_iota(jnp.int32, (width, LANES), 1)
    path[:, :LANES] = jnp.where(jnp.logical_and(is_first, lane < HALO), 0.0, path[:, :LANES])
    piece[...] = pltpu.roll(path[...], full - HALO + 1, 1).astype(BF16)


def coefficients(piece, diff, lead, rest):
    padded = piece.shape[1]
    length = padded - LANES
    points = piece[...].astype(F32)
    after = pltpu.roll(points, padded - 1, 1)[:, :length]
    before = pltpu.roll(points, 1, 1)[:, :length]
    here = points[:, :length]
    middle = 0.5 * (after + before)
    diff[...] = after - before
    lead[...] = 2.0 * here + middle
    rest[...] = middle - here
    return points, after


def half_sum(owner, half, piece, diff, lead, rest, lhs):
    width, padded = piece.shape
    length = padded - LANES
    row_count = 4 * lhs.shape[1] // width
    first_row = pl.multiple_of(owner * row_count, row_count)
    group = max(1, 16 // row_count)
    span = 2 * LANES
    sums = []
    for h in range(2):
        for lanes in [slice(at, at + span) for at in range(0, length, span)]:
            own_lead = lead[pl.ds(first_row, row_count), lanes]
            own_diff = diff[pl.ds(first_row, row_count), lanes]
            for at in range(0, width // 4, group):
                terms = []
                for g in range(group):
                    row = pl.ds(half * (width // 2) + 2 * (at + g) + h, 1)
                    terms.append(diff[row, lanes] * own_lead + rest[row, lanes] * own_diff)
                term = terms[0] if group == 1 else jnp.concatenate(terms, axis=0)
                lhs[h, at * row_count : (at + group) * row_count, lanes] = term.astype(BF16)
        sums.append(lax.dot_general(lhs[h], piece[:, :length], NT, preferred_element_type=F32))
    return jnp.concatenate(sums, axis=1)


def parity():
    return lax.rem(lax.axis_index("wide"), 2)


def target_sum(target, *refs):
    across, mask = target
    owner = jnp.bitwise_xor(lax.axis_index("narrow"), mask)
    return half_sum(owner, 1 - parity() if across else parity(), *refs)


def besides(mask, piece, points, after):
    width, padded = piece.shape
    length = padded - LANES
    crossed = lax.dot_general(after.astype(BF16), piece[:, :length], NT, preferred_element_type=F32)
    lane = lax.broadcasted_iota(jnp.int32, (width, LANES), 1)
    final = jnp.broadcast_to(points[:, length : length + 1], (width, LANES))
    previous = jnp.broadcast_to(points[:, length - 1 : length], (width, LANES))
    rows = jnp.where(lane == 0, final, previous).T
    row = jnp.concatenate([rows[0:1, :], rows[1:2, :]], axis=1)
    is_last = jnp.bitwise_xor(lax.axis_index("narrow"), mask) == lax.axis_size("narrow") - 1
    first = lax.broadcasted_iota(jnp.int32, (ENDS, LANES), 0) == 0
    return folded(crossed), jnp.where(jnp.logical_and(is_last, first), row, 0.0)


def own_kernel(targets, piece, second, ends, *refs):
    sums, (diff, lead, rest, lhs) = refs[: len(targets)], refs[len(targets) :]
    points, after = coefficients(piece, diff, lead, rest)
    second[...], ends[...] = besides(0, piece, points, after)
    for target, total in zip(targets, sums):
        total[...] = target_sum(target, piece, diff, lead, rest, lhs)


def mate_kernel(targets, piece, second, ends, *refs):
    count = len(targets)
    sums, (chip_second, chip_ends), messages, scratch = refs[:count], refs[count : count + 2], refs[count + 2 : -4], refs[-4:]
    diff, lead, rest, lhs = scratch
    points, after = coefficients(piece, diff, lead, rest)
    more_second, more_ends = besides(1, piece, points, after)
    both_second, both_ends = second[...] + more_second, ends[...] + more_ends
    chip_second[...] = both_second
    chip_ends[...] = both_ends
    for target, before, message in zip(targets, sums, messages):
        pack(message, before[...] + target_sum(target, piece, diff, lead, rest, lhs), both_second, both_ends)


def kept_kernel(piece, mate, total, path, diff, lead, rest, lhs):
    _, after = coefficients(piece, diff, lead, rest)
    path[...] = after.astype(BF16)
    first = target_sum((0, 0), piece, diff, lead, rest, lhs)
    coefficients(mate, diff, lead, rest)
    total[...] = first + target_sum((0, 0), mate, diff, lead, rest, lhs)


def folded(crossed):
    width = crossed.shape[0]
    turned = crossed.T - crossed
    row = lax.broadcasted_iota(jnp.int32, (width // 2, width), 0)
    lane = lax.broadcasted_iota(jnp.int32, (width // 2, width), 1)
    corner = jnp.concatenate([turned[width // 2 :, width // 2 :], turned[width // 2 :, : width // 2]], axis=1)
    upper = jnp.where(lane > row, turned[: width // 2, :], jnp.where(lane < row, corner, 0.0))
    return jnp.concatenate([upper, upper], axis=1)


def unfolded(upper):
    size = upper.shape[0]
    row = lax.broadcasted_iota(jnp.int32, (size, size), 0)
    lane = lax.broadcasted_iota(jnp.int32, (size, size), 1)
    near, far = upper[:, :size], upper[:, size : 2 * size]
    above = jnp.where(lane > row, near, 0.0)
    below = jnp.where(lane < row, near, 0.0)
    return jnp.concatenate(
        [
            jnp.concatenate([above - above.T, far], axis=1),
            jnp.concatenate([-far.T, below - below.T], axis=1),
        ],
        axis=0,
    )


def pack(sent, total, doubled, ends=None):
    count, rows = total.shape[0], doubled.shape[0]
    high = doubled.astype(BF16).astype(F32)
    lane = lax.broadcasted_iota(jnp.int32, doubled.shape, 1)
    sent[:count, :] = total.astype(BF16)
    sent[count : count + rows, :] = jnp.where(lane < LANES // 2, high, doubled - high).astype(BF16)
    if ends is not None:
        sent[count + rows :, :] = ends.astype(BF16)


def unpack(received, count, rows):
    coded = received[count : count + rows, :].astype(F32)
    return received[:count, :].astype(F32), coded + pltpu.roll(coded, LANES // 2, 1)


def reduce_kernel(targets, kept, chip_second, chip_ends, *refs):
    parts, refs = refs[: len(targets)], refs[len(targets) :]
    own, other, own_second, other_second, ends, sent = refs
    count, rows = kept.shape[0], chip_second.shape[0]
    sums = [[kept[...], chip_second[...]], None]
    last = chip_ends[...]
    for (across, _), part in zip(targets, parts):
        more = unpack(part, count, rows)
        sums[across] = [a + b for a, b in zip(sums[across], more)] if sums[across] else more
        if not across:
            last = last + part[count + rows :, :].astype(F32)
    own[...], own_second[...] = sums[0]
    other[...], other_second[...] = sums[1]
    total, doubled = sums[0][0] + sums[1][0], sums[0][1] + sums[1][1]
    ends[...] = last
    pack(sent, total, doubled)


def ends_kernel(scale, ends, level_one, x_twice, pairs, factor):
    width = pairs.shape[0]
    x_row, a_row = ends[0:1, :width], ends[0:1, width:]
    x_across = jnp.broadcast_to(x_row, (width, width))
    a_across = jnp.broadcast_to(a_row, (width, width))
    x_down, a_down = x_across.T, a_across.T
    xx = x_down * x_across
    edge = a_down * x_across - a_down * a_across - 2.0 * x_down * a_across
    level_one[...] = scale * x_row
    x_twice[...] = jnp.concatenate([x_row, x_row], axis=1)
    pairs[:, :width] = 0.5 * xx
    factor[:, :width] = 0.5 * xx - edge / 6.0 - xx / 3.0


def earlier_sum(flips, refs, start, size):
    me = lax.axis_index("wide")
    total = jnp.zeros((size, LANES), F32)
    for flip, ref in zip(flips, refs):
        come = ref[start : start + size, :].astype(F32)
        total = total + jnp.where(jnp.bitwise_xor(me, flip) < me, come, 0.0)
    return total


def return_kernel(flips, own, other, *refs):
    received, (earlier, sent) = refs[:-2], refs[-2:]
    total = earlier_sum(flips, received, 0, own.shape[0])
    earlier[...] = total
    sent[...] = (total + other[...] + jnp.where(parity() == 0, own[...], 0.0)).astype(BF16)


def products(result, half, factor, x_twice, total=None):
    row_count, width = factor.shape
    lane = lax.broadcasted_iota(jnp.int32, (row_count, LANES), 1)
    factor = jnp.where(half == 0, factor[:, : width // 2], factor[:, width // 2 :])
    for at in range(width // 4):
        low = jnp.broadcast_to(factor[:, 2 * at : 2 * at + 1], (row_count, LANES))
        high = jnp.broadcast_to(factor[:, 2 * at + 1 : 2 * at + 2], (row_count, LANES))
        value = jnp.where(lane < width, low, high) * x_twice
        if total is not None:
            value = value - total[at * row_count : (at + 1) * row_count, :]
        result[:, at * LANES : (at + 1) * LANES] = value


def levels_kernel(scale, row_count, flips, own_second, other_second, earlier, own, other, x_twice, pairs, factor, *refs):
    received, (level_two, partly, rest, held, own_half, sem) = refs[: len(flips)], refs[len(flips) :]
    width = pairs.shape[0]
    is_first = parity() == 0
    coded = earlier_sum(flips, received, own.shape[0], own_second.shape[0])
    upper = coded + pltpu.roll(coded, LANES // 2, 1)
    upper = upper + own_second[...] + jnp.where(is_first, 0.0, other_second[...])
    turned = 0.5 * unfolded(upper)
    held[:, :width] = scale**3 * (factor[:, :width] + turned)
    first_row = pl.multiple_of(lax.axis_index("narrow") * row_count, row_count)
    own_factor = held[pl.ds(first_row, row_count), :width]
    total = earlier[...] + own[...] + jnp.where(is_first, 0.0, other[...])
    products(own_half, parity(), own_factor, x_twice[...], total * (scale**3 / 6.0))
    size = own_half.shape[1]
    at = pl.multiple_of(parity() * size, size)
    copy = pltpu.make_async_copy(own_half, partly.at[:, pl.ds(at, size)], sem)
    copy.start()
    products(rest, 1 - parity(), own_factor, x_twice[...])
    held[:, :width] = scale**2 * (pairs[:, :width] + turned)
    level_two[:, :width] = held[pl.ds(0, width // 2, stride=2), :width]
    level_two[:, width:] = held[pl.ds(1, width // 2, stride=2), :width]
    copy.wait()


def finish_kernel(scale, row_count, received, rest, partly, level_three, other_half, sem):
    size = rest.shape[1]
    for at in range(size // LANES):
        lanes = slice(at * LANES, (at + 1) * LANES)
        come = received[at * row_count : (at + 1) * row_count, :].astype(F32)
        other_half[:, lanes] = rest[:, lanes] - come * (scale**3 / 6.0)
    at = pl.multiple_of((1 - parity()) * size, size)
    copy = pltpu.make_async_copy(other_half, level_three.at[:, pl.ds(at, size)], sem)
    copy.start()
    copy.wait()


VMEM = pl.BlockSpec(memory_space=pltpu.VMEM)
HBM = pl.BlockSpec(memory_space=pltpu.HBM)


def call(kernel, name, out_shape, scratch=(), in_specs=None, out_specs=None, aliases=None, flops=0, moved=0):
    shapes = [jax.ShapeDtypeStruct(dims, dtype) for dims, dtype in out_shape]

    def run(*operands):
        return pl.pallas_call(
            kernel,
            out_shape=tuple(shapes),
            in_specs=in_specs or [VMEM] * len(operands),
            out_specs=out_specs or (VMEM,) * len(shapes),
            input_output_aliases=aliases or {},
            scratch_shapes=list(scratch),
            compiler_params=pltpu.CompilerParams(vmem_limit_bytes=32 * 2**20),
            cost_estimate=pl.CostEstimate(flops=flops, bytes_accessed=moved, transcendentals=0),
            name=name,
        )(*operands)

    return run


def path_of(recording, conv_weight, conv_bias, projection):
    length, channels = recording.shape
    layers, taps = conv_weight.shape[:2]
    width = projection.shape[1]
    rows = length + 2 * HALO
    edges = edges_exchanged(recording)
    buffer = ((rows + 16, channels), F32)
    far = (recording, conv_weight, conv_bias, projection.T)
    far = [pltpu.with_memory_space_constraint(held, pltpu.HBM) for held in far]
    edge = rows // 4 // HALO * HALO
    middle = [(edge, rows - 2 * edge - 2 * HALO)]
    after = sum(middle[0])
    chunk = 3 * LANES
    chunks = [[(start, min(chunk, rows - start)) for start in range(0, rows, chunk)]] * layers
    chunks[0] = [(0, edge), (after, rows - after)]
    padded, hidden, *near = call(
        functools.partial(load_kernel, middle),
        "load",
        [buffer, buffer, ((layers - 1,) + conv_weight.shape[1:], BF16), (conv_bias.shape, F32), ((width, channels), BF16)],
        scratch=[pltpu.VMEM(recording.shape, BF16), pltpu.SemaphoreType.DMA((2 + layers,))],
        in_specs=[HBM] * len(far),
        flops=10**9,
        moved=2 * sum(held.size for held in far),
    )(*far)
    piece, *_ = call(
        functools.partial(conv_kernel, chunks),
        "conv",
        [((width, length + LANES), BF16), buffer, buffer],
        scratch=[
            pltpu.VMEM(conv_weight.shape[1:], BF16),
            pltpu.VMEM((width, length + LANES), F32),
            pltpu.SemaphoreType.DMA,
        ],
        in_specs=[VMEM] * 6 + [HBM] + [VMEM] * 2,
        aliases={0: 1, 1: 2},
        flops=2 * layers * taps * length * channels**2,
        moved=2 * conv_weight.size,
    )(padded, hidden, *edges, near[0], far[1], near[1], near[2])
    return piece


def per_device(recording, conv_weight, conv_bias, projection):
    length = recording.shape[0]
    width = projection.shape[1]
    wide_size, narrow_size = lax.axis_size("wide"), lax.axis_size("narrow")
    scale = float(length * wide_size * narrow_size) ** -0.2
    row_count = width // narrow_size
    count = width // 4 * row_count
    piece = path_of(recording, conv_weight, conv_bias, projection)

    half, square, folds = ((count, LANES), F32), ((width, LANES), F32), ((width // 2, LANES), F32)
    last = ((ENDS, LANES), F32)
    message = ((count + width // 2, LANES), BF16)
    scratch = [pltpu.VMEM((width, length), F32)] * 3 + [pltpu.VMEM((2, count, length), BF16)]
    share = 10**9 // 2

    mate = exchanged(piece, "narrow", 1)
    targets = [(across, mask) for across in (1, 0) for mask in range(narrow_size - 2, -1, -2)][:-1]
    second, ends, *sums = call(
        functools.partial(own_kernel, targets),
        "own",
        [folds, last] + [half] * len(targets),
        scratch=scratch,
        flops=share * len(targets),
    )(piece)
    chip_second, chip_ends, *messages = call(
        functools.partial(mate_kernel, targets),
        "mate",
        [folds, last] + [((count + width // 2 + ENDS, LANES), BF16)] * len(targets),
        scratch=scratch,
        flops=share * len(targets),
    )(mate, second, ends, *sums)
    size = wide_size * narrow_size
    parts = []
    for (across, mask), sent in zip(targets, messages):
        flip = across * narrow_size + mask
        parts.append(lax.ppermute(sent, WHOLE, [(i, i ^ flip) for i in range(size)]))
    kept, points = call(
        kept_kernel, "kept", [half, ((width, length), BF16)], scratch=scratch, flops=2 * share
    )(piece, mate)
    own, other, own_second, other_second, ends, sent = call(
        functools.partial(reduce_kernel, targets),
        "reduce",
        [half, half, folds, folds, last, message],
    )(kept, chip_second, chip_ends, *parts)
    level_one, x_twice, pairs, factor = call(
        functools.partial(ends_kernel, scale),
        "ends",
        [((1, width), F32), ((1, LANES), F32), square, square],
        flops=share,
    )(ends)

    flips = [flip for flip in range(2, wide_size, 2) if flip != wide_size // 2] + [wide_size // 2]
    received = [exchanged(sent, "wide", flip) for flip in flips]
    total, sent = call(functools.partial(return_kernel, flips), "back", [half, ((count, LANES), BF16)])(
        own, other, *received
    )
    returned = exchanged(sent, "wide", 1)
    own_size = width * width // 2
    third_shape = ((row_count, 2 * own_size), F32)
    half_buffer = ((row_count, own_size), F32)
    level_two, partly, rest = call(
        functools.partial(levels_kernel, scale, row_count, flips),
        "levels",
        [folds, third_shape, half_buffer],
        scratch=[pltpu.VMEM((width, LANES), F32), pltpu.VMEM(half_buffer[0], F32), pltpu.SemaphoreType.DMA],
        out_specs=(VMEM, HBM, VMEM),
        flops=10**9,
    )(own_second, other_second, total, own, other, x_twice, pairs, factor, *received)
    (level_three,) = call(
        functools.partial(finish_kernel, scale, row_count),
        "finish",
        [third_shape],
        scratch=[pltpu.VMEM(half_buffer[0], F32), pltpu.SemaphoreType.DMA],
        in_specs=[VMEM, VMEM, HBM],
        out_specs=(HBM,),
        aliases={2: 0},
    )(returned, rest, partly)
    return points.T, level_one, level_two.reshape(1, width * width), level_three[None]


def solution(mesh):
    return jax.shard_map(
        per_device,
        mesh=mesh,
        in_specs=(P(WHOLE, None), P(), P(), P()),
        out_specs=(P(WHOLE, None), P("wide", None), P("wide", None), P("wide", "narrow", None)),
        check_vma=False,
    )
```

```python
import functools

import jax
import jax.numpy as jnp
from jax import lax
from jax.experimental import pallas as pl
from jax.experimental.pallas import tpu as pltpu
from jax.sharding import PartitionSpec as P

HALO = 16
ENDS = 16
LANES = 128
F32 = jnp.float32
BF16 = jnp.bfloat16
NT = (((1,), (1,)), ((), ()))
WHOLE = ("wide", "narrow")


def exchanged(array, axis, distance):
    size = lax.axis_size(axis)
    return lax.ppermute(array, axis, [(i, i ^ distance) for i in range(size)])


def edges_kernel(rec, outer, inner, sems):
    far = rec.shape[0] - HALO
    at = lax.rem(lax.axis_index("narrow"), 2) * far
    copies = [
        pltpu.make_async_copy(rec.at[pl.ds(pl.multiple_of(start, HALO), HALO), :], rows, sems.at[i])
        for i, (start, rows) in enumerate(((at, outer), (far - at, inner)))
    ]
    for copy in copies:
        copy.start()
    for copy in copies:
        copy.wait()


def again_kernel(outer, inner, outer_again, inner_again):
    outer_again[...] = outer[...]
    inner_again[...] = inner[...]


def edges_exchanged(recording):
    rows = ((HALO, recording.shape[1]), recording.dtype)
    source = pltpu.with_memory_space_constraint(recording, pltpu.HBM)
    outer, inner = call(
        edges_kernel, "edges", [rows, rows], scratch=[pltpu.SemaphoreType.DMA((2,))], in_specs=[HBM]
    )(source)
    again, inner = call(again_kernel, "again", [rows, rows])(outer, inner)
    wide_size, narrow_size = lax.axis_size("wide"), lax.axis_size("narrow")
    size = wide_size * narrow_size
    inside = {i: (i - 1 + 2 * (i % 2)) % narrow_size for i in range(narrow_size)}
    over = {i: (i - 1 + 2 * (i % 2)) % size for i in range(size)}
    if narrow_size > 2:
        end = size - 1
        over.update({0: 1, 1: 2, 2: 0, end: end - 1, end - 1: end - 2, end - 2: end})
    over = lax.ppermute(outer, WHOLE, list(over.items()))
    inside = lax.ppermute(again, "narrow", list(inside.items()))
    return over, inside, exchanged(inner, "narrow", 1)


def layer_rows(source, weights, bias, reach, start, size):
    windows = [source[8 + start + k * reach : 8 + start + k * reach + size, :] for k in (-1, 0, 1)]
    conv = bias
    for tap, window in enumerate(windows):
        conv = conv + jnp.dot(window.astype(BF16), weights[tap], preferred_element_type=F32)
    half = 0.5 * conv
    return (windows[1] + (half + half * jnp.tanh(half))).astype(BF16)


def load_kernel(middle, rec_hbm, weights_hbm, bias_hbm, proj_hbm, padded, hidden, weights, bias, proj, rec, sems):
    length, channels = rec.shape
    low = middle[0][0] - 2 * HALO
    high = sum(middle[-1])
    parts = [slice(low, high), slice(0, low), slice(high, length)]
    pairs = [(rec_hbm.at[parts[0]], rec.at[parts[0]]), (weights_hbm.at[0], weights.at[0]), (bias_hbm, bias)]
    pairs += [(rec_hbm.at[part], rec.at[part]) for part in parts[1:]]
    pairs += [(weights_hbm.at[layer], weights.at[layer]) for layer in range(1, weights.shape[0])]
    pairs += [(proj_hbm, proj)]
    copies = [pltpu.make_async_copy(*pair, sems.at[i]) for i, pair in enumerate(pairs)]

    def widen(part):
        padded[8 + HALO + part.start : 8 + HALO + part.stop, :] = rec[part, :].astype(F32)

    for copy in copies[:3]:
        copy.start()
    copies[0].wait()
    for copy in copies[3:]:
        copy.start()
    widen(parts[0])
    padded[: 8 + HALO, :] = jnp.zeros((8 + HALO, channels), F32)
    padded[8 + HALO + length :, :] = jnp.zeros((8 + HALO, channels), F32)
    for copy in copies[1:3]:
        copy.wait()
    for start, size in middle:
        rows = layer_rows(padded, weights.at[0], bias[0:1, :], 1, start, size)
        hidden[8 + start : 8 + start + size, :] = rows.astype(F32)
    for copy in copies[3:]:
        copy.wait()
    for part in parts[1:]:
        widen(part)


def conv_kernel(
    chunks, _, __, over, inside, inner, weights, weights_hbm, bias, proj, piece, padded, even, last_weights, path, sem
):
    layers = 1 + weights.shape[0]
    rows = padded.shape[0] - 16
    length = rows - 2 * HALO
    far = HALO + length
    copy = pltpu.make_async_copy(weights_hbm.at[layers - 1], last_weights, sem)
    copy.start()
    narrow = lax.axis_index("narrow")
    place = lax.axis_index("wide") * lax.axis_size("narrow") + narrow
    is_first = place == 0
    is_last = place == lax.axis_size("wide") * lax.axis_size("narrow") - 1
    is_odd = lax.rem(narrow, 2) == 1
    width, full = path.shape
    path[:, full - LANES :] = jnp.zeros((width, LANES), F32)
    at_end = jnp.logical_or(is_first, is_last)
    at_edge = jnp.logical_or(narrow == 0, narrow == lax.axis_size("narrow") - 1)
    beyond = jnp.where(at_edge, over[...].astype(F32), inside[...].astype(F32))
    beyond = jnp.where(at_end, 0.0, beyond)
    within = inner[...].astype(F32)
    padded[8 : 8 + HALO, :] = jnp.where(is_odd, within, beyond)
    padded[8 + far : 8 + rows, :] = jnp.where(is_odd, beyond, within)
    source, target = padded, even
    for layer in range(layers):
        if layer == layers - 1:
            copy.wait()
        reach = 2**layer
        for start, size in chunks[layer]:
            layer_weights = last_weights if layer == layers - 1 else weights.at[layer]
            hidden = layer_rows(source, layer_weights, bias[layer : layer + 1, :], reach, start, size)
            if layer < layers - 1:
                target[8 + start : 8 + start + size, :] = hidden.astype(F32)
            else:
                part = lax.dot_general(hidden, proj[...], NT, preferred_element_type=F32)
                path[:, start : start + size] = part.astype(BF16).astype(F32).T
        if layer < layers - 1:
            target[8 : 8 + HALO, :] = jnp.where(is_first, 0.0, target[8 : 8 + HALO, :])
            target[8 + far : 8 + rows, :] = jnp.where(is_last, 0.0, target[8 + far : 8 + rows, :])
        source, target = target, source
    lane = lax.broadcasted_iota(jnp.int32, (width, LANES), 1)
    path[:, :LANES] = jnp.where(jnp.logical_and(is_first, lane < HALO), 0.0, path[:, :LANES])
    piece[...] = pltpu.roll(path[...], full - HALO + 1, 1).astype(BF16)


def coefficients(piece, diff, lead, rest):
    padded = piece.shape[1]
    length = padded - LANES
    points = piece[...].astype(F32)
    after = pltpu.roll(points, padded - 1, 1)[:, :length]
    before = pltpu.roll(points, 1, 1)[:, :length]
    here = points[:, :length]
    middle = 0.5 * (after + before)
    diff[...] = after - before
    lead[...] = 2.0 * here + middle
    rest[...] = middle - here
    return points, after


def half_sum(owner, half, piece, diff, lead, rest, lhs):
    width, padded = piece.shape
    length = padded - LANES
    row_count = 4 * lhs.shape[1] // width
    first_row = pl.multiple_of(owner * row_count, row_count)
    group = max(1, 16 // row_count)
    span = 2 * LANES
    sums = []
    for h in range(2):
        for lanes in [slice(at, at + span) for at in range(0, length, span)]:
            own_lead = lead[pl.ds(first_row, row_count), lanes]
            own_diff = diff[pl.ds(first_row, row_count), lanes]
            for at in range(0, width // 4, group):
                terms = []
                for g in range(group):
                    row = pl.ds(half * (width // 2) + 2 * (at + g) + h, 1)
                    terms.append(diff[row, lanes] * own_lead + rest[row, lanes] * own_diff)
                term = terms[0] if group == 1 else jnp.concatenate(terms, axis=0)
                lhs[h, at * row_count : (at + group) * row_count, lanes] = term.astype(BF16)
        sums.append(lax.dot_general(lhs[h], piece[:, :length], NT, preferred_element_type=F32))
    return jnp.concatenate(sums, axis=1)


def parity():
    return lax.rem(lax.axis_index("wide"), 2)


def target_sum(target, *refs):
    across, mask = target
    owner = jnp.bitwise_xor(lax.axis_index("narrow"), mask)
    return half_sum(owner, 1 - parity() if across else parity(), *refs)


def besides(mask, piece, points, after):
    width, padded = piece.shape
    length = padded - LANES
    crossed = lax.dot_general(after.astype(BF16), piece[:, :length], NT, preferred_element_type=F32)
    lane = lax.broadcasted_iota(jnp.int32, (width, LANES), 1)
    final = jnp.broadcast_to(points[:, length : length + 1], (width, LANES))
    previous = jnp.broadcast_to(points[:, length - 1 : length], (width, LANES))
    rows = jnp.where(lane == 0, final, previous).T
    row = jnp.concatenate([rows[0:1, :], rows[1:2, :]], axis=1)
    is_last = jnp.bitwise_xor(lax.axis_index("narrow"), mask) == lax.axis_size("narrow") - 1
    first = lax.broadcasted_iota(jnp.int32, (ENDS, LANES), 0) == 0
    return folded(crossed), jnp.where(jnp.logical_and(is_last, first), row, 0.0)


def own_kernel(targets, piece, second, ends, *refs):
    sums, (diff, lead, rest, lhs) = refs[: len(targets)], refs[len(targets) :]
    points, after = coefficients(piece, diff, lead, rest)
    second[...], ends[...] = besides(0, piece, points, after)
    for target, total in zip(targets, sums):
        total[...] = target_sum(target, piece, diff, lead, rest, lhs)


def mate_kernel(targets, piece, second, ends, *refs):
    count = len(targets)
    sums, (chip_second, chip_ends), messages, scratch = refs[:count], refs[count : count + 2], refs[count + 2 : -4], refs[-4:]
    diff, lead, rest, lhs = scratch
    points, after = coefficients(piece, diff, lead, rest)
    more_second, more_ends = besides(1, piece, points, after)
    both_second, both_ends = second[...] + more_second, ends[...] + more_ends
    chip_second[...] = both_second
    chip_ends[...] = both_ends
    for target, before, message in zip(targets, sums, messages):
        pack(message, before[...] + target_sum(target, piece, diff, lead, rest, lhs), both_second, both_ends)


def kept_kernel(piece, mate, total, path, diff, lead, rest, lhs):
    _, after = coefficients(piece, diff, lead, rest)
    path[...] = after.astype(BF16)
    first = target_sum((0, 0), piece, diff, lead, rest, lhs)
    coefficients(mate, diff, lead, rest)
    total[...] = first + target_sum((0, 0), mate, diff, lead, rest, lhs)


def folded(crossed):
    width = crossed.shape[0]
    turned = crossed.T - crossed
    row = lax.broadcasted_iota(jnp.int32, (width // 2, width), 0)
    lane = lax.broadcasted_iota(jnp.int32, (width // 2, width), 1)
    corner = jnp.concatenate([turned[width // 2 :, width // 2 :], turned[width // 2 :, : width // 2]], axis=1)
    upper = jnp.where(lane > row, turned[: width // 2, :], jnp.where(lane < row, corner, 0.0))
    return jnp.concatenate([upper, upper], axis=1)


def unfolded(upper):
    size = upper.shape[0]
    row = lax.broadcasted_iota(jnp.int32, (size, size), 0)
    lane = lax.broadcasted_iota(jnp.int32, (size, size), 1)
    near, far = upper[:, :size], upper[:, size : 2 * size]
    above = jnp.where(lane > row, near, 0.0)
    below = jnp.where(lane < row, near, 0.0)
    return jnp.concatenate(
        [
            jnp.concatenate([above - above.T, far], axis=1),
            jnp.concatenate([-far.T, below - below.T], axis=1),
        ],
        axis=0,
    )


def pack(sent, total, doubled, ends=None):
    count, rows = total.shape[0], doubled.shape[0]
    high = doubled.astype(BF16).astype(F32)
    lane = lax.broadcasted_iota(jnp.int32, doubled.shape, 1)
    sent[:count, :] = total.astype(BF16)
    sent[count : count + rows, :] = jnp.where(lane < LANES // 2, high, doubled - high).astype(BF16)
    if ends is not None:
        sent[count + rows :, :] = ends.astype(BF16)


def unpack(received, count, rows):
    coded = received[count : count + rows, :].astype(F32)
    return received[:count, :].astype(F32), coded + pltpu.roll(coded, LANES // 2, 1)


def reduce_kernel(targets, kept, chip_second, chip_ends, *refs):
    parts, refs = refs[: len(targets)], refs[len(targets) :]
    own, other, own_second, other_second, ends, sent = refs
    count, rows = kept.shape[0], chip_second.shape[0]
    sums = [[kept[...], chip_second[...]], None]
    last = chip_ends[...]
    for (across, _), part in zip(targets, parts):
        more = unpack(part, count, rows)
        sums[across] = [a + b for a, b in zip(sums[across], more)] if sums[across] else more
        if not across:
            last = last + part[count + rows :, :].astype(F32)
    own[...], own_second[...] = sums[0]
    other[...], other_second[...] = sums[1]
    total, doubled = sums[0][0] + sums[1][0], sums[0][1] + sums[1][1]
    ends[...] = last
    pack(sent, total, doubled)


def ends_kernel(scale, ends, level_one, x_twice, pairs, factor):
    width = pairs.shape[0]
    x_row, a_row = ends[0:1, :width], ends[0:1, width:]
    x_across = jnp.broadcast_to(x_row, (width, width))
    a_across = jnp.broadcast_to(a_row, (width, width))
    x_down, a_down = x_across.T, a_across.T
    xx = x_down * x_across
    edge = a_down * x_across - a_down * a_across - 2.0 * x_down * a_across
    level_one[...] = scale * x_row
    x_twice[...] = jnp.concatenate([x_row, x_row], axis=1)
    pairs[:, :width] = 0.5 * xx
    factor[:, :width] = 0.5 * xx - edge / 6.0 - xx / 3.0


def earlier_sum(flips, refs, start, size):
    me = lax.axis_index("wide")
    total = jnp.zeros((size, LANES), F32)
    for flip, ref in zip(flips, refs):
        come = ref[start : start + size, :].astype(F32)
        total = total + jnp.where(jnp.bitwise_xor(me, flip) < me, come, 0.0)
    return total


def return_kernel(flips, own, other, *refs):
    received, (earlier, sent) = refs[:-2], refs[-2:]
    total = earlier_sum(flips, received, 0, own.shape[0])
    earlier[...] = total
    sent[...] = (total + other[...] + jnp.where(parity() == 0, own[...], 0.0)).astype(BF16)


def products(result, half, factor, x_twice, total=None):
    row_count, width = factor.shape
    lane = lax.broadcasted_iota(jnp.int32, (row_count, LANES), 1)
    factor = jnp.where(half == 0, factor[:, : width // 2], factor[:, width // 2 :])
    for at in range(width // 4):
        low = jnp.broadcast_to(factor[:, 2 * at : 2 * at + 1], (row_count, LANES))
        high = jnp.broadcast_to(factor[:, 2 * at + 1 : 2 * at + 2], (row_count, LANES))
        value = jnp.where(lane < width, low, high) * x_twice
        if total is not None:
            value = value - total[at * row_count : (at + 1) * row_count, :]
        result[:, at * LANES : (at + 1) * LANES] = value


def levels_kernel(scale, row_count, flips, own_second, other_second, earlier, own, other, x_twice, pairs, factor, *refs):
    received, (level_two, partly, rest, held, own_half, sem) = refs[: len(flips)], refs[len(flips) :]
    width = pairs.shape[0]
    is_first = parity() == 0
    coded = earlier_sum(flips, received, own.shape[0], own_second.shape[0])
    upper = coded + pltpu.roll(coded, LANES // 2, 1)
    upper = upper + own_second[...] + jnp.where(is_first, 0.0, other_second[...])
    turned = 0.5 * unfolded(upper)
    held[:, :width] = scale**3 * (factor[:, :width] + turned)
    first_row = pl.multiple_of(lax.axis_index("narrow") * row_count, row_count)
    own_factor = held[pl.ds(first_row, row_count), :width]
    total = earlier[...] + own[...] + jnp.where(is_first, 0.0, other[...])
    products(own_half, parity(), own_factor, x_twice[...], total * (scale**3 / 6.0))
    size = own_half.shape[1]
    at = pl.multiple_of(parity() * size, size)
    copy = pltpu.make_async_copy(own_half, partly.at[:, pl.ds(at, size)], sem)
    copy.start()
    products(rest, 1 - parity(), own_factor, x_twice[...])
    held[:, :width] = scale**2 * (pairs[:, :width] + turned)
    level_two[:, :width] = held[pl.ds(0, width // 2, stride=2), :width]
    level_two[:, width:] = held[pl.ds(1, width // 2, stride=2), :width]
    copy.wait()


def finish_kernel(scale, row_count, received, rest, partly, level_three, other_half, sem):
    size = rest.shape[1]
    for at in range(size // LANES):
        lanes = slice(at * LANES, (at + 1) * LANES)
        come = received[at * row_count : (at + 1) * row_count, :].astype(F32)
        other_half[:, lanes] = rest[:, lanes] - come * (scale**3 / 6.0)
    at = pl.multiple_of((1 - parity()) * size, size)
    copy = pltpu.make_async_copy(other_half, level_three.at[:, pl.ds(at, size)], sem)
    copy.start()
    copy.wait()


VMEM = pl.BlockSpec(memory_space=pltpu.VMEM)
HBM = pl.BlockSpec(memory_space=pltpu.HBM)


def call(kernel, name, out_shape, scratch=(), in_specs=None, out_specs=None, aliases=None, flops=0, moved=0):
    shapes = [jax.ShapeDtypeStruct(dims, dtype) for dims, dtype in out_shape]

    def run(*operands):
        return pl.pallas_call(
            kernel,
            out_shape=tuple(shapes),
            in_specs=in_specs or [VMEM] * len(operands),
            out_specs=out_specs or (VMEM,) * len(shapes),
            input_output_aliases=aliases or {},
            scratch_shapes=list(scratch),
            compiler_params=pltpu.CompilerParams(vmem_limit_bytes=32 * 2**20),
            cost_estimate=pl.CostEstimate(flops=flops, bytes_accessed=moved, transcendentals=0),
            name=name,
        )(*operands)

    return run


def path_of(recording, conv_weight, conv_bias, projection):
    length, channels = recording.shape
    layers, taps = conv_weight.shape[:2]
    width = projection.shape[1]
    rows = length + 2 * HALO
    edges = edges_exchanged(recording)
    buffer = ((rows + 16, channels), F32)
    far = (recording, conv_weight, conv_bias, projection.T)
    far = [pltpu.with_memory_space_constraint(held, pltpu.HBM) for held in far]
    edge = rows // 4 // HALO * HALO
    middle = [(edge, rows - 2 * edge - 2 * HALO)]
    after = sum(middle[0])
    chunk = 3 * LANES
    chunks = [[(start, min(chunk, rows - start)) for start in range(0, rows, chunk)]] * layers
    chunks[0] = [(0, edge), (after, rows - after)]
    padded, hidden, *near = call(
        functools.partial(load_kernel, middle),
        "load",
        [buffer, buffer, ((layers - 1,) + conv_weight.shape[1:], BF16), (conv_bias.shape, F32), ((width, channels), BF16)],
        scratch=[pltpu.VMEM(recording.shape, BF16), pltpu.SemaphoreType.DMA((5 + layers,))],
        in_specs=[HBM] * len(far),
        flops=10**9,
        moved=2 * sum(held.size for held in far),
    )(*far)
    piece, *_ = call(
        functools.partial(conv_kernel, chunks),
        "conv",
        [((width, length + LANES), BF16), buffer, buffer],
        scratch=[
            pltpu.VMEM(conv_weight.shape[1:], BF16),
            pltpu.VMEM((width, length + LANES), F32),
            pltpu.SemaphoreType.DMA,
        ],
        in_specs=[VMEM] * 6 + [HBM] + [VMEM] * 2,
        aliases={0: 1, 1: 2},
        flops=2 * layers * taps * length * channels**2,
        moved=2 * conv_weight.size,
    )(padded, hidden, *edges, near[0], far[1], near[1], near[2])
    return piece


def per_device(recording, conv_weight, conv_bias, projection):
    length = recording.shape[0]
    width = projection.shape[1]
    wide_size, narrow_size = lax.axis_size("wide"), lax.axis_size("narrow")
    scale = float(length * wide_size * narrow_size) ** -0.2
    row_count = width // narrow_size
    count = width // 4 * row_count
    piece = path_of(recording, conv_weight, conv_bias, projection)

    half, square, folds = ((count, LANES), F32), ((width, LANES), F32), ((width // 2, LANES), F32)
    last = ((ENDS, LANES), F32)
    message = ((count + width // 2, LANES), BF16)
    scratch = [pltpu.VMEM((width, length), F32)] * 3 + [pltpu.VMEM((2, count, length), BF16)]
    share = 10**9 // 2

    mate = exchanged(piece, "narrow", 1)
    targets = [(across, mask) for across in (1, 0) for mask in range(narrow_size - 2, -1, -2)][:-1]
    second, ends, *sums = call(
        functools.partial(own_kernel, targets),
        "own",
        [folds, last] + [half] * len(targets),
        scratch=scratch,
        flops=share * len(targets),
    )(piece)
    chip_second, chip_ends, *messages = call(
        functools.partial(mate_kernel, targets),
        "mate",
        [folds, last] + [((count + width // 2 + ENDS, LANES), BF16)] * len(targets),
        scratch=scratch,
        flops=share * len(targets),
    )(mate, second, ends, *sums)
    size = wide_size * narrow_size
    parts = []
    for (across, mask), sent in zip(targets, messages):
        flip = across * narrow_size + mask
        parts.append(lax.ppermute(sent, WHOLE, [(i, i ^ flip) for i in range(size)]))
    kept, points = call(
        kept_kernel, "kept", [half, ((width, length), BF16)], scratch=scratch, flops=2 * share
    )(piece, mate)
    own, other, own_second, other_second, ends, sent = call(
        functools.partial(reduce_kernel, targets),
        "reduce",
        [half, half, folds, folds, last, message],
    )(kept, chip_second, chip_ends, *parts)
    level_one, x_twice, pairs, factor = call(
        functools.partial(ends_kernel, scale),
        "ends",
        [((1, width), F32), ((1, LANES), F32), square, square],
        flops=share,
    )(ends)

    flips = [flip for flip in range(2, wide_size, 2) if flip != wide_size // 2] + [wide_size // 2]
    received = [exchanged(sent, "wide", flip) for flip in flips]
    total, sent = call(functools.partial(return_kernel, flips), "back", [half, ((count, LANES), BF16)])(
        own, other, *received
    )
    returned = exchanged(sent, "wide", 1)
    own_size = width * width // 2
    third_shape = ((row_count, 2 * own_size), F32)
    half_buffer = ((row_count, own_size), F32)
    level_two, partly, rest = call(
        functools.partial(levels_kernel, scale, row_count, flips),
        "levels",
        [folds, third_shape, half_buffer],
        scratch=[pltpu.VMEM((width, LANES), F32), pltpu.VMEM(half_buffer[0], F32), pltpu.SemaphoreType.DMA],
        out_specs=(VMEM, HBM, VMEM),
        flops=10**9,
    )(own_second, other_second, total, own, other, x_twice, pairs, factor, *received)
    (level_three,) = call(
        functools.partial(finish_kernel, scale, row_count),
        "finish",
        [third_shape],
        scratch=[pltpu.VMEM(half_buffer[0], F32), pltpu.SemaphoreType.DMA],
        in_specs=[VMEM, VMEM, HBM],
        out_specs=(HBM,),
        aliases={2: 0},
    )(returned, rest, partly)
    return points.T, level_one, level_two.reshape(1, width * width), level_three[None]


def solution(mesh):
    return jax.shard_map(
        per_device,
        mesh=mesh,
        in_specs=(P(WHOLE, None), P(), P(), P()),
        out_specs=(P(WHOLE, None), P("wide", None), P("wide", None), P("wide", "narrow", None)),
        check_vma=False,
    )
```

```python
import functools

import jax
import jax.numpy as jnp
from jax import lax
from jax.experimental import pallas as pl
from jax.experimental.pallas import tpu as pltpu
from jax.sharding import PartitionSpec as P

HALO = 16
ENDS = 16
LANES = 128
F32 = jnp.float32
BF16 = jnp.bfloat16
NT = (((1,), (1,)), ((), ()))
WHOLE = ("wide", "narrow")


def exchanged(array, axis, distance):
    size = lax.axis_size(axis)
    return lax.ppermute(array, axis, [(i, i ^ distance) for i in range(size)])


def edges_kernel(rec, outer, inner, sems):
    far = rec.shape[0] - HALO
    at = lax.rem(lax.axis_index("narrow"), 2) * far
    copies = [
        pltpu.make_async_copy(rec.at[pl.ds(pl.multiple_of(start, HALO), HALO), :], rows, sems.at[i])
        for i, (start, rows) in enumerate(((at, outer), (far - at, inner)))
    ]
    for copy in copies:
        copy.start()
    for copy in copies:
        copy.wait()


def again_kernel(outer, inner, outer_again, inner_again):
    outer_again[...] = outer[...]
    inner_again[...] = inner[...]


def edges_exchanged(recording):
    rows = ((HALO, recording.shape[1]), recording.dtype)
    source = pltpu.with_memory_space_constraint(recording, pltpu.HBM)
    outer, inner = call(
        edges_kernel, "edges", [rows, rows], scratch=[pltpu.SemaphoreType.DMA((2,))], in_specs=[HBM]
    )(source)
    again, inner = call(again_kernel, "again", [rows, rows])(outer, inner)
    wide_size, narrow_size = lax.axis_size("wide"), lax.axis_size("narrow")
    size = wide_size * narrow_size
    inside = {i: (i - 1 + 2 * (i % 2)) % narrow_size for i in range(narrow_size)}
    over = {i: (i - 1 + 2 * (i % 2)) % size for i in range(size)}
    if narrow_size > 2:
        end = size - 1
        over.update({0: 1, 1: 2, 2: 0, end: end - 1, end - 1: end - 2, end - 2: end})
    over = lax.ppermute(outer, WHOLE, list(over.items()))
    inside = lax.ppermute(again, "narrow", list(inside.items()))
    return over, inside, exchanged(inner, "narrow", 1)


def layer_rows(source, weights, bias, reach, start, size, arriving=None):
    windows = [source[8 + start + k * reach : 8 + start + k * reach + size, :] for k in (-1, 0, 1)]
    conv = bias
    for tap, window in enumerate(windows):
        if arriving:
            arriving[tap].wait()
        conv = conv + jnp.dot(window.astype(BF16), weights[tap], preferred_element_type=F32)
    half = 0.5 * conv
    return (windows[1] + (half + half * jnp.tanh(half))).astype(BF16)


def load_kernel(middle, rec_hbm, weights_hbm, bias_hbm, proj_hbm, padded, hidden, weights, bias, proj, rec, sems):
    length, channels = rec.shape
    low = middle[0][0] - 2 * HALO
    high = sum(middle[-1])
    parts = [slice(low, high), slice(0, low), slice(high, length)]
    taps = weights.shape[1]
    pairs = [(rec_hbm.at[parts[0]], rec.at[parts[0]]), (bias_hbm, bias)]
    pairs += [(weights_hbm.at[0, tap], weights.at[0, tap]) for tap in range(taps)]
    early = len(pairs)
    pairs += [(rec_hbm.at[part], rec.at[part]) for part in parts[1:]]
    pairs += [(weights_hbm.at[layer], weights.at[layer]) for layer in range(1, weights.shape[0])]
    pairs += [(proj_hbm, proj)]
    copies = [pltpu.make_async_copy(*pair, sems.at[i]) for i, pair in enumerate(pairs)]

    def widen(part):
        padded[8 + HALO + part.start : 8 + HALO + part.stop, :] = rec[part, :].astype(F32)

    for copy in copies[:early]:
        copy.start()
    copies[0].wait()
    for copy in copies[early:]:
        copy.start()
    widen(parts[0])
    padded[: 8 + HALO, :] = jnp.zeros((8 + HALO, channels), F32)
    padded[8 + HALO + length :, :] = jnp.zeros((8 + HALO, channels), F32)
    copies[1].wait()
    for at, (start, size) in enumerate(middle):
        arriving = None if at else copies[2:early]
        rows = layer_rows(padded, weights.at[0], bias[0:1, :], 1, start, size, arriving)
        hidden[8 + start : 8 + start + size, :] = rows.astype(F32)
    for copy, part in zip(copies[early:], parts[1:]):
        copy.wait()
        widen(part)
    for copy in copies[early + 2 :]:
        copy.wait()


def conv_kernel(
    chunks, _, __, over, inside, inner, weights, weights_hbm, bias, proj, piece, padded, even, last_weights, path, sem
):
    layers = 1 + weights.shape[0]
    rows = padded.shape[0] - 16
    length = rows - 2 * HALO
    far = HALO + length
    copy = pltpu.make_async_copy(weights_hbm.at[layers - 1], last_weights, sem)
    copy.start()
    narrow = lax.axis_index("narrow")
    place = lax.axis_index("wide") * lax.axis_size("narrow") + narrow
    is_first = place == 0
    is_last = place == lax.axis_size("wide") * lax.axis_size("narrow") - 1
    is_odd = lax.rem(narrow, 2) == 1
    width, full = path.shape
    path[:, full - LANES :] = jnp.zeros((width, LANES), F32)
    at_end = jnp.logical_or(is_first, is_last)
    at_edge = jnp.logical_or(narrow == 0, narrow == lax.axis_size("narrow") - 1)
    beyond = jnp.where(at_edge, over[...].astype(F32), inside[...].astype(F32))
    beyond = jnp.where(at_end, 0.0, beyond)
    within = inner[...].astype(F32)
    padded[8 : 8 + HALO, :] = jnp.where(is_odd, within, beyond)
    padded[8 + far : 8 + rows, :] = jnp.where(is_odd, beyond, within)
    source, target = padded, even
    for layer in range(layers):
        if layer == layers - 1:
            copy.wait()
        reach = 2**layer
        for start, size in chunks[layer]:
            layer_weights = last_weights if layer == layers - 1 else weights.at[layer]
            hidden = layer_rows(source, layer_weights, bias[layer : layer + 1, :], reach, start, size)
            if layer < layers - 1:
                target[8 + start : 8 + start + size, :] = hidden.astype(F32)
            else:
                part = lax.dot_general(hidden, proj[...], NT, preferred_element_type=F32)
                path[:, start : start + size] = part.astype(BF16).astype(F32).T
        if layer < layers - 1:
            target[8 : 8 + HALO, :] = jnp.where(is_first, 0.0, target[8 : 8 + HALO, :])
            target[8 + far : 8 + rows, :] = jnp.where(is_last, 0.0, target[8 + far : 8 + rows, :])
        source, target = target, source
    lane = lax.broadcasted_iota(jnp.int32, (width, LANES), 1)
    path[:, :LANES] = jnp.where(jnp.logical_and(is_first, lane < HALO), 0.0, path[:, :LANES])
    piece[...] = pltpu.roll(path[...], full - HALO + 1, 1).astype(BF16)


def coefficients(piece, diff, lead, rest):
    padded = piece.shape[1]
    length = padded - LANES
    points = piece[...].astype(F32)
    after = pltpu.roll(points, padded - 1, 1)[:, :length]
    before = pltpu.roll(points, 1, 1)[:, :length]
    here = points[:, :length]
    middle = 0.5 * (after + before)
    diff[...] = after - before
    lead[...] = 2.0 * here + middle
    rest[...] = middle - here
    return points, after


def half_sum(owner, half, piece, diff, lead, rest, lhs):
    width, padded = piece.shape
    length = padded - LANES
    row_count = 4 * lhs.shape[1] // width
    first_row = pl.multiple_of(owner * row_count, row_count)
    group = max(1, 16 // row_count)
    span = 4 * LANES
    sums = [None, None]
    for lanes in [slice(at, at + span) for at in range(0, length, span)]:
        own_lead = lead[pl.ds(first_row, row_count), lanes]
        own_diff = diff[pl.ds(first_row, row_count), lanes]
        for h in range(2):
            for at in range(0, width // 4, group):
                terms = []
                for g in range(group):
                    row = pl.ds(half * (width // 2) + 2 * (at + g) + h, 1)
                    terms.append(diff[row, lanes] * own_lead + rest[row, lanes] * own_diff)
                term = terms[0] if group == 1 else jnp.concatenate(terms, axis=0)
                lhs[h, at * row_count : (at + group) * row_count, lanes] = term.astype(BF16)
            part = lax.dot_general(lhs[h, :, lanes], piece[:, lanes], NT, preferred_element_type=F32)
            sums[h] = part if sums[h] is None else sums[h] + part
    return jnp.concatenate(sums, axis=1)


def parity():
    return lax.rem(lax.axis_index("wide"), 2)


def target_sum(target, *refs):
    across, mask = target
    owner = jnp.bitwise_xor(lax.axis_index("narrow"), mask)
    return half_sum(owner, 1 - parity() if across else parity(), *refs)


def besides(mask, piece, points, after):
    width, padded = piece.shape
    length = padded - LANES
    crossed = lax.dot_general(after.astype(BF16), piece[:, :length], NT, preferred_element_type=F32)
    lane = lax.broadcasted_iota(jnp.int32, (width, LANES), 1)
    final = jnp.broadcast_to(points[:, length : length + 1], (width, LANES))
    previous = jnp.broadcast_to(points[:, length - 1 : length], (width, LANES))
    rows = jnp.where(lane == 0, final, previous).T
    row = jnp.concatenate([rows[0:1, :], rows[1:2, :]], axis=1)
    is_last = jnp.bitwise_xor(lax.axis_index("narrow"), mask) == lax.axis_size("narrow") - 1
    first = lax.broadcasted_iota(jnp.int32, (ENDS, LANES), 0) == 0
    return folded(crossed), jnp.where(jnp.logical_and(is_last, first), row, 0.0)


def own_kernel(targets, piece, second, ends, *refs):
    sums, (diff, lead, rest, lhs) = refs[: len(targets)], refs[len(targets) :]
    points, after = coefficients(piece, diff, lead, rest)
    second[...], ends[...] = besides(0, piece, points, after)
    for target, total in zip(targets, sums):
        total[...] = target_sum(target, piece, diff, lead, rest, lhs)


def mate_kernel(targets, piece, second, ends, *refs):
    count = len(targets)
    sums, (chip_second, chip_ends), messages, scratch = refs[:count], refs[count : count + 2], refs[count + 2 : -4], refs[-4:]
    diff, lead, rest, lhs = scratch
    points, after = coefficients(piece, diff, lead, rest)
    more_second, more_ends = besides(1, piece, points, after)
    both_second, both_ends = second[...] + more_second, ends[...] + more_ends
    chip_second[...] = both_second
    chip_ends[...] = both_ends
    for target, before, message in zip(targets, sums, messages):
        total = before[...] + target_sum(target, piece, diff, lead, rest, lhs)
        pack(message, total, both_second, None if target[0] else both_ends)


def kept_kernel(piece, mate, total, path, diff, lead, rest, lhs):
    _, after = coefficients(piece, diff, lead, rest)
    path[...] = after.astype(BF16)
    first = target_sum((0, 0), piece, diff, lead, rest, lhs)
    coefficients(mate, diff, lead, rest)
    total[...] = first + target_sum((0, 0), mate, diff, lead, rest, lhs)


def folded(crossed):
    width = crossed.shape[0]
    turned = crossed.T - crossed
    row = lax.broadcasted_iota(jnp.int32, (width // 2, width), 0)
    lane = lax.broadcasted_iota(jnp.int32, (width // 2, width), 1)
    corner = jnp.concatenate([turned[width // 2 :, width // 2 :], turned[width // 2 :, : width // 2]], axis=1)
    upper = jnp.where(lane > row, turned[: width // 2, :], jnp.where(lane < row, corner, 0.0))
    return jnp.concatenate([upper, upper], axis=1)


def unfolded(upper):
    size = upper.shape[0]
    row = lax.broadcasted_iota(jnp.int32, (size, size), 0)
    lane = lax.broadcasted_iota(jnp.int32, (size, size), 1)
    near, far = upper[:, :size], upper[:, size : 2 * size]
    above = jnp.where(lane > row, near, 0.0)
    below = jnp.where(lane < row, near, 0.0)
    return jnp.concatenate(
        [
            jnp.concatenate([above - above.T, far], axis=1),
            jnp.concatenate([-far.T, below - below.T], axis=1),
        ],
        axis=0,
    )


def pack(sent, total, doubled, ends=None):
    count, rows = total.shape[0], doubled.shape[0]
    high = doubled.astype(BF16).astype(F32)
    lane = lax.broadcasted_iota(jnp.int32, doubled.shape, 1)
    sent[:count, :] = total.astype(BF16)
    sent[count : count + rows, :] = jnp.where(lane < LANES // 2, high, doubled - high).astype(BF16)
    if ends is not None:
        sent[count + rows :, :] = ends.astype(BF16)


def unpack(received, count, rows):
    coded = received[count : count + rows, :].astype(F32)
    return received[:count, :].astype(F32), coded + pltpu.roll(coded, LANES // 2, 1)


def reduce_kernel(targets, kept, chip_second, chip_ends, *refs):
    parts, refs = refs[: len(targets)], refs[len(targets) :]
    own, other, own_second, other_second, ends, sent = refs
    count, rows = kept.shape[0], chip_second.shape[0]
    sums = [[kept[...], chip_second[...]], None]
    last = chip_ends[...]
    for (across, _), part in zip(targets, parts):
        more = unpack(part, count, rows)
        sums[across] = [a + b for a, b in zip(sums[across], more)] if sums[across] else more
        if not across:
            last = last + part[count + rows :, :].astype(F32)
    own[...], own_second[...] = sums[0]
    other[...], other_second[...] = sums[1]
    total, doubled = sums[0][0] + sums[1][0], sums[0][1] + sums[1][1]
    ends[...] = last
    pack(sent, total, doubled)


def ends_kernel(scale, ends, level_one, x_twice, pairs, factor):
    width = pairs.shape[0]
    x_row, a_row = ends[0:1, :width], ends[0:1, width:]
    x_across = jnp.broadcast_to(x_row, (width, width))
    a_across = jnp.broadcast_to(a_row, (width, width))
    x_down, a_down = x_across.T, a_across.T
    xx = x_down * x_across
    edge = a_down * x_across - a_down * a_across - 2.0 * x_down * a_across
    level_one[...] = scale * x_row
    x_twice[...] = jnp.concatenate([x_row, x_row], axis=1)
    pairs[:, :width] = 0.5 * xx
    factor[:, :width] = 0.5 * xx - edge / 6.0 - xx / 3.0


def earlier_sum(flips, refs, start, size):
    me = lax.axis_index("wide")
    total = jnp.zeros((size, LANES), F32)
    for flip, ref in zip(flips, refs):
        come = ref[start : start + size, :].astype(F32)
        total = total + jnp.where(jnp.bitwise_xor(me, flip) < me, come, 0.0)
    return total


def return_kernel(flips, own, other, *refs):
    received, (earlier, sent) = refs[:-2], refs[-2:]
    total = earlier_sum(flips, received, 0, own.shape[0])
    earlier[...] = total
    sent[...] = (total + other[...] + jnp.where(parity() == 0, own[...], 0.0)).astype(BF16)


def products(result, half, factor, x_twice, total=None):
    row_count, width = factor.shape
    lane = lax.broadcasted_iota(jnp.int32, (row_count, LANES), 1)
    factor = jnp.where(half == 0, factor[:, : width // 2], factor[:, width // 2 :])
    for at in range(width // 4):
        low = jnp.broadcast_to(factor[:, 2 * at : 2 * at + 1], (row_count, LANES))
        high = jnp.broadcast_to(factor[:, 2 * at + 1 : 2 * at + 2], (row_count, LANES))
        value = jnp.where(lane < width, low, high) * x_twice
        if total is not None:
            value = value - total[at * row_count : (at + 1) * row_count, :]
        result[:, at * LANES : (at + 1) * LANES] = value


def levels_kernel(scale, row_count, flips, own_second, other_second, earlier, own, other, x_twice, pairs, factor, *refs):
    received, (level_two, partly, rest, held, own_half, sem) = refs[: len(flips)], refs[len(flips) :]
    width = pairs.shape[0]
    is_first = parity() == 0
    coded = earlier_sum(flips, received, own.shape[0], own_second.shape[0])
    upper = coded + pltpu.roll(coded, LANES // 2, 1)
    upper = upper + own_second[...] + jnp.where(is_first, 0.0, other_second[...])
    turned = 0.5 * unfolded(upper)
    held[:, :width] = scale**3 * (factor[:, :width] + turned)
    first_row = pl.multiple_of(lax.axis_index("narrow") * row_count, row_count)
    own_factor = held[pl.ds(first_row, row_count), :width]
    total = earlier[...] + own[...] + jnp.where(is_first, 0.0, other[...])
    products(own_half, parity(), own_factor, x_twice[...], total * (scale**3 / 6.0))
    size = own_half.shape[1]
    at = pl.multiple_of(parity() * size, size)
    copy = pltpu.make_async_copy(own_half, partly.at[:, pl.ds(at, size)], sem)
    copy.start()
    products(rest, 1 - parity(), own_factor, x_twice[...])
    held[:, :width] = scale**2 * (pairs[:, :width] + turned)
    level_two[:, :width] = held[pl.ds(0, width // 2, stride=2), :width]
    level_two[:, width:] = held[pl.ds(1, width // 2, stride=2), :width]
    copy.wait()


def finish_kernel(scale, row_count, received, rest, partly, level_three, other_half, sem):
    size = rest.shape[1]
    for at in range(size // LANES):
        lanes = slice(at * LANES, (at + 1) * LANES)
        come = received[at * row_count : (at + 1) * row_count, :].astype(F32)
        other_half[:, lanes] = rest[:, lanes] - come * (scale**3 / 6.0)
    at = pl.multiple_of((1 - parity()) * size, size)
    copy = pltpu.make_async_copy(other_half, level_three.at[:, pl.ds(at, size)], sem)
    copy.start()
    copy.wait()


VMEM = pl.BlockSpec(memory_space=pltpu.VMEM)
HBM = pl.BlockSpec(memory_space=pltpu.HBM)


def call(kernel, name, out_shape, scratch=(), in_specs=None, out_specs=None, aliases=None, flops=0, moved=0):
    shapes = [jax.ShapeDtypeStruct(dims, dtype) for dims, dtype in out_shape]

    def run(*operands):
        return pl.pallas_call(
            kernel,
            out_shape=tuple(shapes),
            in_specs=in_specs or [VMEM] * len(operands),
            out_specs=out_specs or (VMEM,) * len(shapes),
            input_output_aliases=aliases or {},
            scratch_shapes=list(scratch),
            compiler_params=pltpu.CompilerParams(vmem_limit_bytes=32 * 2**20),
            cost_estimate=pl.CostEstimate(flops=flops, bytes_accessed=moved, transcendentals=0),
            name=name,
        )(*operands)

    return run


def path_of(recording, conv_weight, conv_bias, projection):
    length, channels = recording.shape
    layers, taps = conv_weight.shape[:2]
    width = projection.shape[1]
    rows = length + 2 * HALO
    edges = edges_exchanged(recording)
    buffer = ((rows + 16, channels), F32)
    far = (recording, conv_weight, conv_bias, projection.T)
    far = [pltpu.with_memory_space_constraint(held, pltpu.HBM) for held in far]
    edge = rows // 4 // HALO * HALO
    middle = [(edge, rows - 2 * edge - 2 * HALO)]
    after = sum(middle[0])
    chunk = 3 * LANES
    chunks = [[(start, min(chunk, rows - start)) for start in range(0, rows, chunk)]] * layers
    chunks[0] = [(0, edge), (after, rows - after)]
    padded, hidden, *near = call(
        functools.partial(load_kernel, middle),
        "load",
        [buffer, buffer, ((layers - 1,) + conv_weight.shape[1:], BF16), (conv_bias.shape, F32), ((width, channels), BF16)],
        scratch=[pltpu.VMEM(recording.shape, BF16), pltpu.SemaphoreType.DMA((4 + taps + layers,))],
        in_specs=[HBM] * len(far),
        flops=10**9,
        moved=2 * sum(held.size for held in far),
    )(*far)
    piece, *_ = call(
        functools.partial(conv_kernel, chunks),
        "conv",
        [((width, length + LANES), BF16), buffer, buffer],
        scratch=[
            pltpu.VMEM(conv_weight.shape[1:], BF16),
            pltpu.VMEM((width, length + LANES), F32),
            pltpu.SemaphoreType.DMA,
        ],
        in_specs=[VMEM] * 6 + [HBM] + [VMEM] * 2,
        aliases={0: 1, 1: 2},
        flops=2 * layers * taps * length * channels**2,
        moved=2 * conv_weight.size,
    )(padded, hidden, *edges, near[0], far[1], near[1], near[2])
    return piece


def per_device(recording, conv_weight, conv_bias, projection):
    length = recording.shape[0]
    width = projection.shape[1]
    wide_size, narrow_size = lax.axis_size("wide"), lax.axis_size("narrow")
    scale = float(length * wide_size * narrow_size) ** -0.2
    row_count = width // narrow_size
    count = width // 4 * row_count
    piece = path_of(recording, conv_weight, conv_bias, projection)

    half, square, folds = ((count, LANES), F32), ((width, LANES), F32), ((width // 2, LANES), F32)
    last = ((ENDS, LANES), F32)
    message = ((count + width // 2, LANES), BF16)
    scratch = [pltpu.VMEM((width, length), F32)] * 3 + [pltpu.VMEM((2, count, length), BF16)]
    share = 10**9 // 2

    mate = exchanged(piece, "narrow", 1)
    targets = [(across, mask) for across in (1, 0) for mask in range(narrow_size - 2, -1, -2)][:-1]
    second, ends, *sums = call(
        functools.partial(own_kernel, targets),
        "own",
        [folds, last] + [half] * len(targets),
        scratch=scratch,
        flops=share * len(targets),
    )(piece)
    chip_second, chip_ends, *messages = call(
        functools.partial(mate_kernel, targets),
        "mate",
        [folds, last] + [((count + width // 2 + (0 if across else ENDS), LANES), BF16) for across, _ in targets],
        scratch=scratch,
        flops=share * len(targets),
    )(mate, second, ends, *sums)
    size = wide_size * narrow_size
    parts = []
    for (across, mask), sent in zip(targets, messages):
        flip = across * narrow_size + mask
        parts.append(lax.ppermute(sent, WHOLE, [(i, i ^ flip) for i in range(size)]))
    kept, points = call(
        kept_kernel, "kept", [half, ((width, length), BF16)], scratch=scratch, flops=2 * share
    )(piece, mate)
    own, other, own_second, other_second, ends, sent = call(
        functools.partial(reduce_kernel, targets),
        "reduce",
        [half, half, folds, folds, last, message],
    )(kept, chip_second, chip_ends, *parts)
    level_one, x_twice, pairs, factor = call(
        functools.partial(ends_kernel, scale),
        "ends",
        [((1, width), F32), ((1, LANES), F32), square, square],
        flops=share,
    )(ends)

    flips = [flip for flip in range(2, wide_size, 2) if flip != wide_size // 2] + [wide_size // 2]
    received = [exchanged(sent, "wide", flip) for flip in flips]
    total, sent = call(functools.partial(return_kernel, flips), "back", [half, ((count, LANES), BF16)])(
        own, other, *received
    )
    returned = exchanged(sent, "wide", 1)
    own_size = width * width // 2
    third_shape = ((row_count, 2 * own_size), F32)
    half_buffer = ((row_count, own_size), F32)
    level_two, partly, rest = call(
        functools.partial(levels_kernel, scale, row_count, flips),
        "levels",
        [folds, third_shape, half_buffer],
        scratch=[pltpu.VMEM((width, LANES), F32), pltpu.VMEM(half_buffer[0], F32), pltpu.SemaphoreType.DMA],
        out_specs=(VMEM, HBM, VMEM),
        flops=10**9,
    )(own_second, other_second, total, own, other, x_twice, pairs, factor, *received)
    (level_three,) = call(
        functools.partial(finish_kernel, scale, row_count),
        "finish",
        [third_shape],
        scratch=[pltpu.VMEM(half_buffer[0], F32), pltpu.SemaphoreType.DMA],
        in_specs=[VMEM, VMEM, HBM],
        out_specs=(HBM,),
        aliases={2: 0},
    )(returned, rest, partly)
    return points.T, level_one, level_two.reshape(1, width * width), level_three[None]


def solution(mesh):
    return jax.shard_map(
        per_device,
        mesh=mesh,
        in_specs=(P(WHOLE, None), P(), P(), P()),
        out_specs=(P(WHOLE, None), P("wide", None), P("wide", None), P("wide", "narrow", None)),
        check_vma=False,
    )
```

```python
import functools

import jax
import jax.numpy as jnp
from jax import lax
from jax.experimental import pallas as pl
from jax.experimental.pallas import tpu as pltpu
from jax.sharding import PartitionSpec as P

HALO = 16
ENDS = 16
LANES = 128
F32 = jnp.float32
BF16 = jnp.bfloat16
NT = (((1,), (1,)), ((), ()))
WHOLE = ("wide", "narrow")


def exchanged(array, axis, distance):
    size = lax.axis_size(axis)
    return lax.ppermute(array, axis, [(i, i ^ distance) for i in range(size)])


def edges_kernel(rec, outer, inner, sems):
    far = rec.shape[0] - HALO
    at = lax.rem(lax.axis_index("narrow"), 2) * far
    copies = [
        pltpu.make_async_copy(rec.at[pl.ds(pl.multiple_of(start, HALO), HALO), :], rows, sems.at[i])
        for i, (start, rows) in enumerate(((at, outer), (far - at, inner)))
    ]
    for copy in copies:
        copy.start()
    for copy in copies:
        copy.wait()


def again_kernel(outer, inner, outer_again, inner_again):
    outer_again[...] = outer[...]
    inner_again[...] = inner[...]


def edges_exchanged(recording):
    rows = ((HALO, recording.shape[1]), recording.dtype)
    source = pltpu.with_memory_space_constraint(recording, pltpu.HBM)
    outer, inner = call(
        edges_kernel, "edges", [rows, rows], scratch=[pltpu.SemaphoreType.DMA((2,))], in_specs=[HBM]
    )(source)
    again, inner = call(again_kernel, "again", [rows, rows])(outer, inner)
    wide_size, narrow_size = lax.axis_size("wide"), lax.axis_size("narrow")
    size = wide_size * narrow_size
    inside = {i: (i - 1 + 2 * (i % 2)) % narrow_size for i in range(narrow_size)}
    over = {i: (i - 1 + 2 * (i % 2)) % size for i in range(size)}
    if narrow_size > 2:
        end = size - 1
        over.update({0: 1, 1: 2, 2: 0, end: end - 1, end - 1: end - 2, end - 2: end})
    over = lax.ppermute(outer, WHOLE, list(over.items()))
    inside = lax.ppermute(again, "narrow", list(inside.items()))
    return over, inside, exchanged(inner, "narrow", 1)


def layer_rows(source, weights, bias, reach, start, size, arriving=None):
    windows = [source[8 + start + k * reach : 8 + start + k * reach + size, :] for k in (-1, 0, 1)]
    conv = bias
    for tap, window in enumerate(windows):
        if arriving and tap:
            arriving[tap - 1].wait()
        conv = conv + jnp.dot(window.astype(BF16), weights[tap], preferred_element_type=F32)
    half = 0.5 * conv
    return (windows[1] + (half + half * jnp.tanh(half))).astype(BF16)


def load_kernel(middle, rec_hbm, weights_hbm, bias_hbm, proj_hbm, padded, hidden, weights, bias, proj, rec, sems):
    length, channels = rec.shape
    low = middle[0][0] - 2 * HALO
    high = sum(middle[-1])
    parts = [slice(low, high), slice(0, low), slice(high, length)]
    taps = weights.shape[1]
    pairs = [(rec_hbm.at[parts[0]], rec.at[parts[0]]), (bias_hbm, bias)]
    pairs += [(weights_hbm.at[0, tap], weights.at[0, tap]) for tap in range(taps)]
    early = len(pairs)
    pairs += [(rec_hbm.at[part], rec.at[part]) for part in parts[1:]]
    pairs += [(weights_hbm.at[layer], weights.at[layer]) for layer in range(1, weights.shape[0])]
    pairs += [(proj_hbm, proj)]
    copies = [pltpu.make_async_copy(*pair, sems.at[i]) for i, pair in enumerate(pairs)]

    def widen(part):
        padded[8 + HALO + part.start : 8 + HALO + part.stop, :] = rec[part, :].astype(F32)

    for copy in copies[:early]:
        copy.start()
    copies[0].wait()
    for copy in copies[early : early + 2]:
        copy.start()
    widen(parts[0])
    padded[: 8 + HALO, :] = jnp.zeros((8 + HALO, channels), F32)
    padded[8 + HALO + length :, :] = jnp.zeros((8 + HALO, channels), F32)
    copies[1].wait()
    copies[2].wait()
    for copy in copies[early + 2 :]:
        copy.start()
    for at, (start, size) in enumerate(middle):
        arriving = None if at else copies[3:early]
        rows = layer_rows(padded, weights.at[0], bias[0:1, :], 1, start, size, arriving)
        hidden[8 + start : 8 + start + size, :] = rows.astype(F32)
    for copy, part in zip(copies[early:], parts[1:]):
        copy.wait()
        widen(part)
    for copy in copies[early + 2 :]:
        copy.wait()


def conv_kernel(
    chunks, _, __, over, inside, inner, weights, weights_hbm, bias, proj, piece, padded, even, last_weights, path, sem
):
    layers = 1 + weights.shape[0]
    rows = padded.shape[0] - 16
    length = rows - 2 * HALO
    far = HALO + length
    copy = pltpu.make_async_copy(weights_hbm.at[layers - 1], last_weights, sem)
    copy.start()
    narrow = lax.axis_index("narrow")
    place = lax.axis_index("wide") * lax.axis_size("narrow") + narrow
    is_first = place == 0
    is_last = place == lax.axis_size("wide") * lax.axis_size("narrow") - 1
    is_odd = lax.rem(narrow, 2) == 1
    width, full = path.shape
    path[:, full - LANES :] = jnp.zeros((width, LANES), F32)
    at_end = jnp.logical_or(is_first, is_last)
    at_edge = jnp.logical_or(narrow == 0, narrow == lax.axis_size("narrow") - 1)
    beyond = jnp.where(at_edge, over[...].astype(F32), inside[...].astype(F32))
    beyond = jnp.where(at_end, 0.0, beyond)
    within = inner[...].astype(F32)
    padded[8 : 8 + HALO, :] = jnp.where(is_odd, within, beyond)
    padded[8 + far : 8 + rows, :] = jnp.where(is_odd, beyond, within)
    source, target = padded, even
    for layer in range(layers):
        if layer == layers - 1:
            copy.wait()
        reach = 2**layer
        for start, size in chunks[layer]:
            layer_weights = last_weights if layer == layers - 1 else weights.at[layer]
            hidden = layer_rows(source, layer_weights, bias[layer : layer + 1, :], reach, start, size)
            if layer < layers - 1:
                target[8 + start : 8 + start + size, :] = hidden.astype(F32)
            else:
                part = lax.dot_general(hidden, proj[...], NT, preferred_element_type=F32)
                path[:, start : start + size] = part.astype(BF16).astype(F32).T
        if layer < layers - 1:
            target[8 : 8 + HALO, :] = jnp.where(is_first, 0.0, target[8 : 8 + HALO, :])
            target[8 + far : 8 + rows, :] = jnp.where(is_last, 0.0, target[8 + far : 8 + rows, :])
        source, target = target, source
    lane = lax.broadcasted_iota(jnp.int32, (width, LANES), 1)
    path[:, :LANES] = jnp.where(jnp.logical_and(is_first, lane < HALO), 0.0, path[:, :LANES])
    piece[...] = pltpu.roll(path[...], full - HALO + 1, 1).astype(BF16)


def coefficients(piece, diff, lead, rest):
    padded = piece.shape[1]
    length = padded - LANES
    points = piece[...].astype(F32)
    after = pltpu.roll(points, padded - 1, 1)[:, :length]
    before = pltpu.roll(points, 1, 1)[:, :length]
    here = points[:, :length]
    middle = 0.5 * (after + before)
    diff[...] = after - before
    lead[...] = 2.0 * here + middle
    rest[...] = middle - here
    return points, after


def half_sum(owner, half, piece, diff, lead, rest, lhs):
    width, padded = piece.shape
    length = padded - LANES
    row_count = 4 * lhs.shape[1] // width
    first_row = pl.multiple_of(owner * row_count, row_count)
    group = max(1, 16 // row_count)
    span = 4 * LANES
    sums = [None, None]
    for lanes in [slice(at, at + span) for at in range(0, length, span)]:
        own_lead = lead[pl.ds(first_row, row_count), lanes]
        own_diff = diff[pl.ds(first_row, row_count), lanes]
        for h in range(2):
            for at in range(0, width // 4, group):
                terms = []
                for g in range(group):
                    row = pl.ds(half * (width // 2) + 2 * (at + g) + h, 1)
                    terms.append(diff[row, lanes] * own_lead + rest[row, lanes] * own_diff)
                term = terms[0] if group == 1 else jnp.concatenate(terms, axis=0)
                lhs[h, at * row_count : (at + group) * row_count, lanes] = term.astype(BF16)
            part = lax.dot_general(lhs[h, :, lanes], piece[:, lanes], NT, preferred_element_type=F32)
            sums[h] = part if sums[h] is None else sums[h] + part
    return jnp.concatenate(sums, axis=1)


def parity():
    return lax.rem(lax.axis_index("wide"), 2)


def target_sum(target, *refs):
    across, mask = target
    owner = jnp.bitwise_xor(lax.axis_index("narrow"), mask)
    return half_sum(owner, 1 - parity() if across else parity(), *refs)


def besides(mask, piece, points, after):
    width, padded = piece.shape
    length = padded - LANES
    crossed = lax.dot_general(after.astype(BF16), piece[:, :length], NT, preferred_element_type=F32)
    lane = lax.broadcasted_iota(jnp.int32, (width, LANES), 1)
    final = jnp.broadcast_to(points[:, length : length + 1], (width, LANES))
    previous = jnp.broadcast_to(points[:, length - 1 : length], (width, LANES))
    rows = jnp.where(lane == 0, final, previous).T
    row = jnp.concatenate([rows[0:1, :], rows[1:2, :]], axis=1)
    is_last = jnp.bitwise_xor(lax.axis_index("narrow"), mask) == lax.axis_size("narrow") - 1
    first = lax.broadcasted_iota(jnp.int32, (ENDS, LANES), 0) == 0
    return folded(crossed), jnp.where(jnp.logical_and(is_last, first), row, 0.0)


def own_kernel(targets, piece, second, ends, *refs):
    sums, (diff, lead, rest, lhs) = refs[: len(targets)], refs[len(targets) :]
    points, after = coefficients(piece, diff, lead, rest)
    second[...], ends[...] = besides(0, piece, points, after)
    for target, total in zip(targets, sums):
        total[...] = target_sum(target, piece, diff, lead, rest, lhs)


def mate_kernel(targets, piece, second, ends, *refs):
    count = len(targets)
    sums, (chip_second, chip_ends), messages, scratch = refs[:count], refs[count : count + 2], refs[count + 2 : -4], refs[-4:]
    diff, lead, rest, lhs = scratch
    points, after = coefficients(piece, diff, lead, rest)
    more_second, more_ends = besides(1, piece, points, after)
    both_second, both_ends = second[...] + more_second, ends[...] + more_ends
    chip_second[...] = both_second
    chip_ends[...] = both_ends
    for target, before, message in zip(targets, sums, messages):
        total = before[...] + target_sum(target, piece, diff, lead, rest, lhs)
        pack(message, total, both_second, None if target[0] else both_ends)


def kept_kernel(piece, mate, total, path, diff, lead, rest, lhs):
    _, after = coefficients(piece, diff, lead, rest)
    path[...] = after.astype(BF16)
    first = target_sum((0, 0), piece, diff, lead, rest, lhs)
    coefficients(mate, diff, lead, rest)
    total[...] = first + target_sum((0, 0), mate, diff, lead, rest, lhs)


def folded(crossed):
    width = crossed.shape[0]
    turned = crossed.T - crossed
    row = lax.broadcasted_iota(jnp.int32, (width // 2, width), 0)
    lane = lax.broadcasted_iota(jnp.int32, (width // 2, width), 1)
    corner = jnp.concatenate([turned[width // 2 :, width // 2 :], turned[width // 2 :, : width // 2]], axis=1)
    upper = jnp.where(lane > row, turned[: width // 2, :], jnp.where(lane < row, corner, 0.0))
    return jnp.concatenate([upper, upper], axis=1)


def unfolded(upper):
    size = upper.shape[0]
    row = lax.broadcasted_iota(jnp.int32, (size, size), 0)
    lane = lax.broadcasted_iota(jnp.int32, (size, size), 1)
    near, far = upper[:, :size], upper[:, size : 2 * size]
    above = jnp.where(lane > row, near, 0.0)
    below = jnp.where(lane < row, near, 0.0)
    return jnp.concatenate(
        [
            jnp.concatenate([above - above.T, far], axis=1),
            jnp.concatenate([-far.T, below - below.T], axis=1),
        ],
        axis=0,
    )


def pack(sent, total, doubled, ends=None):
    count, rows = total.shape[0], doubled.shape[0]
    high = doubled.astype(BF16).astype(F32)
    lane = lax.broadcasted_iota(jnp.int32, doubled.shape, 1)
    sent[:count, :] = total.astype(BF16)
    sent[count : count + rows, :] = jnp.where(lane < LANES // 2, high, doubled - high).astype(BF16)
    if ends is not None:
        sent[count + rows :, :] = ends.astype(BF16)


def unpack(received, count, rows):
    coded = received[count : count + rows, :].astype(F32)
    return received[:count, :].astype(F32), coded + pltpu.roll(coded, LANES // 2, 1)


def reduce_kernel(targets, kept, chip_second, chip_ends, *refs):
    parts, refs = refs[: len(targets)], refs[len(targets) :]
    own, other, own_second, other_second, ends, sent = refs
    count, rows = kept.shape[0], chip_second.shape[0]
    sums = [[kept[...], chip_second[...]], None]
    last = chip_ends[...]
    for (across, _), part in zip(targets, parts):
        more = unpack(part, count, rows)
        sums[across] = [a + b for a, b in zip(sums[across], more)] if sums[across] else more
        if not across:
            last = last + part[count + rows :, :].astype(F32)
    own[...], own_second[...] = sums[0]
    other[...], other_second[...] = sums[1]
    total, doubled = sums[0][0] + sums[1][0], sums[0][1] + sums[1][1]
    ends[...] = last
    pack(sent, total, doubled)


def ends_kernel(scale, ends, level_one, x_twice, pairs, factor):
    width = pairs.shape[0]
    x_row, a_row = ends[0:1, :width], ends[0:1, width:]
    x_across = jnp.broadcast_to(x_row, (width, width))
    a_across = jnp.broadcast_to(a_row, (width, width))
    x_down, a_down = x_across.T, a_across.T
    xx = x_down * x_across
    edge = a_down * x_across - a_down * a_across - 2.0 * x_down * a_across
    level_one[...] = scale * x_row
    x_twice[...] = jnp.concatenate([x_row, x_row], axis=1)
    pairs[:, :width] = 0.5 * xx
    factor[:, :width] = 0.5 * xx - edge / 6.0 - xx / 3.0


def earlier_sum(flips, refs, start, size):
    me = lax.axis_index("wide")
    total = jnp.zeros((size, LANES), F32)
    for flip, ref in zip(flips, refs):
        come = ref[start : start + size, :].astype(F32)
        total = total + jnp.where(jnp.bitwise_xor(me, flip) < me, come, 0.0)
    return total


def return_kernel(flips, own, other, *refs):
    received, (earlier, sent) = refs[:-2], refs[-2:]
    total = earlier_sum(flips, received, 0, own.shape[0])
    earlier[...] = total
    sent[...] = (total + other[...] + jnp.where(parity() == 0, own[...], 0.0)).astype(BF16)


def products(result, half, factor, x_twice, total=None):
    row_count, width = factor.shape
    lane = lax.broadcasted_iota(jnp.int32, (row_count, LANES), 1)
    factor = jnp.where(half == 0, factor[:, : width // 2], factor[:, width // 2 :])
    for at in range(width // 4):
        low = jnp.broadcast_to(factor[:, 2 * at : 2 * at + 1], (row_count, LANES))
        high = jnp.broadcast_to(factor[:, 2 * at + 1 : 2 * at + 2], (row_count, LANES))
        value = jnp.where(lane < width, low, high) * x_twice
        if total is not None:
            value = value - total[at * row_count : (at + 1) * row_count, :]
        result[:, at * LANES : (at + 1) * LANES] = value


def levels_kernel(scale, row_count, flips, own_second, other_second, earlier, own, other, x_twice, pairs, factor, *refs):
    received, (level_two, partly, rest, held, own_half, sem) = refs[: len(flips)], refs[len(flips) :]
    width = pairs.shape[0]
    is_first = parity() == 0
    coded = earlier_sum(flips, received, own.shape[0], own_second.shape[0])
    upper = coded + pltpu.roll(coded, LANES // 2, 1)
    upper = upper + own_second[...] + jnp.where(is_first, 0.0, other_second[...])
    turned = 0.5 * unfolded(upper)
    held[:, :width] = scale**3 * (factor[:, :width] + turned)
    first_row = pl.multiple_of(lax.axis_index("narrow") * row_count, row_count)
    own_factor = held[pl.ds(first_row, row_count), :width]
    total = earlier[...] + own[...] + jnp.where(is_first, 0.0, other[...])
    products(own_half, parity(), own_factor, x_twice[...], total * (scale**3 / 6.0))
    size = own_half.shape[1]
    at = pl.multiple_of(parity() * size, size)
    copy = pltpu.make_async_copy(own_half, partly.at[:, pl.ds(at, size)], sem)
    copy.start()
    products(rest, 1 - parity(), own_factor, x_twice[...])
    held[:, :width] = scale**2 * (pairs[:, :width] + turned)
    level_two[:, :width] = held[pl.ds(0, width // 2, stride=2), :width]
    level_two[:, width:] = held[pl.ds(1, width // 2, stride=2), :width]
    copy.wait()


def finish_kernel(scale, row_count, received, rest, partly, level_three, other_half, sem):
    size = rest.shape[1]
    for at in range(size // LANES):
        lanes = slice(at * LANES, (at + 1) * LANES)
        come = received[at * row_count : (at + 1) * row_count, :].astype(F32)
        other_half[:, lanes] = rest[:, lanes] - come * (scale**3 / 6.0)
    at = pl.multiple_of((1 - parity()) * size, size)
    copy = pltpu.make_async_copy(other_half, level_three.at[:, pl.ds(at, size)], sem)
    copy.start()
    copy.wait()


VMEM = pl.BlockSpec(memory_space=pltpu.VMEM)
HBM = pl.BlockSpec(memory_space=pltpu.HBM)


def call(kernel, name, out_shape, scratch=(), in_specs=None, out_specs=None, aliases=None, flops=0, moved=0):
    shapes = [jax.ShapeDtypeStruct(dims, dtype) for dims, dtype in out_shape]

    def run(*operands):
        return pl.pallas_call(
            kernel,
            out_shape=tuple(shapes),
            in_specs=in_specs or [VMEM] * len(operands),
            out_specs=out_specs or (VMEM,) * len(shapes),
            input_output_aliases=aliases or {},
            scratch_shapes=list(scratch),
            compiler_params=pltpu.CompilerParams(vmem_limit_bytes=32 * 2**20),
            cost_estimate=pl.CostEstimate(flops=flops, bytes_accessed=moved, transcendentals=0),
            name=name,
        )(*operands)

    return run


def path_of(recording, conv_weight, conv_bias, projection):
    length, channels = recording.shape
    layers, taps = conv_weight.shape[:2]
    width = projection.shape[1]
    rows = length + 2 * HALO
    edges = edges_exchanged(recording)
    buffer = ((rows + 16, channels), F32)
    far = (recording, conv_weight, conv_bias, projection.T)
    far = [pltpu.with_memory_space_constraint(held, pltpu.HBM) for held in far]
    edge = rows // 4 // HALO * HALO
    middle = [(edge, rows - 2 * edge - 2 * HALO)]
    after = sum(middle[0])
    chunk = 3 * LANES
    chunks = [[(start, min(chunk, rows - start)) for start in range(0, rows, chunk)]] * layers
    chunks[0] = [(0, edge), (after, rows - after)]
    padded, hidden, *near = call(
        functools.partial(load_kernel, middle),
        "load",
        [buffer, buffer, ((layers - 1,) + conv_weight.shape[1:], BF16), (conv_bias.shape, F32), ((width, channels), BF16)],
        scratch=[pltpu.VMEM(recording.shape, BF16), pltpu.SemaphoreType.DMA((4 + taps + layers,))],
        in_specs=[HBM] * len(far),
        flops=10**9,
        moved=2 * sum(held.size for held in far),
    )(*far)
    piece, *_ = call(
        functools.partial(conv_kernel, chunks),
        "conv",
        [((width, length + LANES), BF16), buffer, buffer],
        scratch=[
            pltpu.VMEM(conv_weight.shape[1:], BF16),
            pltpu.VMEM((width, length + LANES), F32),
            pltpu.SemaphoreType.DMA,
        ],
        in_specs=[VMEM] * 6 + [HBM] + [VMEM] * 2,
        aliases={0: 1, 1: 2},
        flops=2 * layers * taps * length * channels**2,
        moved=2 * conv_weight.size,
    )(padded, hidden, *edges, near[0], far[1], near[1], near[2])
    return piece


def per_device(recording, conv_weight, conv_bias, projection):
    length = recording.shape[0]
    width = projection.shape[1]
    wide_size, narrow_size = lax.axis_size("wide"), lax.axis_size("narrow")
    scale = float(length * wide_size * narrow_size) ** -0.2
    row_count = width // narrow_size
    count = width // 4 * row_count
    piece = path_of(recording, conv_weight, conv_bias, projection)

    half, square, folds = ((count, LANES), F32), ((width, LANES), F32), ((width // 2, LANES), F32)
    last = ((ENDS, LANES), F32)
    message = ((count + width // 2, LANES), BF16)
    scratch = [pltpu.VMEM((width, length), F32)] * 3 + [pltpu.VMEM((2, count, length), BF16)]
    share = 10**9 // 2

    mate = exchanged(piece, "narrow", 1)
    targets = [(across, mask) for across in (1, 0) for mask in range(narrow_size - 2, -1, -2)][:-1]
    second, ends, *sums = call(
        functools.partial(own_kernel, targets),
        "own",
        [folds, last] + [half] * len(targets),
        scratch=scratch,
        flops=share * len(targets),
    )(piece)
    chip_second, chip_ends, *messages = call(
        functools.partial(mate_kernel, targets),
        "mate",
        [folds, last] + [((count + width // 2 + (0 if across else ENDS), LANES), BF16) for across, _ in targets],
        scratch=scratch,
        flops=share * len(targets),
    )(mate, second, ends, *sums)
    size = wide_size * narrow_size
    parts = []
    for (across, mask), sent in zip(targets, messages):
        flip = across * narrow_size + mask
        parts.append(lax.ppermute(sent, WHOLE, [(i, i ^ flip) for i in range(size)]))
    kept, points = call(
        kept_kernel, "kept", [half, ((width, length), BF16)], scratch=scratch, flops=2 * share
    )(piece, mate)
    own, other, own_second, other_second, ends, sent = call(
        functools.partial(reduce_kernel, targets),
        "reduce",
        [half, half, folds, folds, last, message],
    )(kept, chip_second, chip_ends, *parts)
    level_one, x_twice, pairs, factor = call(
        functools.partial(ends_kernel, scale),
        "ends",
        [((1, width), F32), ((1, LANES), F32), square, square],
        flops=share,
    )(ends)

    flips = [flip for flip in range(2, wide_size, 2) if flip != wide_size // 2] + [wide_size // 2]
    received = [exchanged(sent, "wide", flip) for flip in flips]
    total, sent = call(functools.partial(return_kernel, flips), "back", [half, ((count, LANES), BF16)])(
        own, other, *received
    )
    returned = exchanged(sent, "wide", 1)
    own_size = width * width // 2
    third_shape = ((row_count, 2 * own_size), F32)
    half_buffer = ((row_count, own_size), F32)
    level_two, partly, rest = call(
        functools.partial(levels_kernel, scale, row_count, flips),
        "levels",
        [folds, third_shape, half_buffer],
        scratch=[pltpu.VMEM((width, LANES), F32), pltpu.VMEM(half_buffer[0], F32), pltpu.SemaphoreType.DMA],
        out_specs=(VMEM, HBM, VMEM),
        flops=10**9,
    )(own_second, other_second, total, own, other, x_twice, pairs, factor, *received)
    (level_three,) = call(
        functools.partial(finish_kernel, scale, row_count),
        "finish",
        [third_shape],
        scratch=[pltpu.VMEM(half_buffer[0], F32), pltpu.SemaphoreType.DMA],
        in_specs=[VMEM, VMEM, HBM],
        out_specs=(HBM,),
        aliases={2: 0},
    )(returned, rest, partly)
    return points.T, level_one, level_two.reshape(1, width * width), level_three[None]


def solution(mesh):
    return jax.shard_map(
        per_device,
        mesh=mesh,
        in_specs=(P(WHOLE, None), P(), P(), P()),
        out_specs=(P(WHOLE, None), P("wide", None), P("wide", None), P("wide", "narrow", None)),
        check_vma=False,
    )
```
